256 devices in a mesh: dp: 16 (over x_lo, y, core), tensor: 16 (over x_hi, z).
Axes of the slice: x: 4 (x_hi: 2, x_lo: 2; x = x_hi * 2 + x_lo), y: 4, z: 8, core: 2. Of those that a mesh axis runs over, the one named last changes fastest.
Arguments:
- tokens: bfloat16 [8192, 2048], P('dp', 'tensor'), may hold values from -6 to 6
- series_ids: int32 [8192], replicated, may hold values from 0 to 7, never falling along the last dimension, each value on 1 to 5120 neighbouring positions
- offsets: int32 [8192], P('dp'), may hold values from 0 to 65535
- norm_gain: float32 [2048], replicated, may hold values from 0.5 to 1.5
- mlp_gain: float32 [2048], replicated, may hold values from 0.5 to 1.5
- w_query: bfloat16 [2048, 2048], P(None, 'tensor')
- w_key: bfloat16 [2048, 2048], P(None, 'tensor')
- w_value: bfloat16 [2048, 2048], P(None, 'tensor'), may hold values from -0.125 to 0.125
- w_out: bfloat16 [2048, 2048], P('tensor'), may hold values from -0.125 to 0.125
- w_gate: bfloat16 [2048, 8192], P(None, 'tensor'), may hold values from -0.125 to 0.125
- w_up: bfloat16 [2048, 8192], P(None, 'tensor'), may hold values from -0.125 to 0.125
- w_down: bfloat16 [8192, 2048], P('tensor'), may hold values from -0.0625 to 0.0625
- projector: bfloat16 [2048, 512], replicated, may hold values from -0.125 to 0.125
- student_in: bfloat16 [8192, 512], P('dp'), may hold values from -6 to 6
- s_gate: bfloat16 [512, 2048], P(None, 'tensor'), may hold values from -0.25 to 0.25
- s_up: bfloat16 [512, 2048], P(None, 'tensor'), may hold values from -0.25 to 0.25
- s_down: bfloat16 [2048, 512], P('tensor'), may hold values from -0.125 to 0.125
Outputs:
- teacher_out: bfloat16 [8192, 2048], P('dp', 'tensor')
- grad_gate: float32 [512, 2048], P(None, 'tensor')
- grad_up: float32 [512, 2048], P(None, 'tensor')
- grad_down: float32 [2048, 512], P('tensor')
- error: float32 [], replicated
The draws below stay inside these ranges and needn't reach their ends.
Inputs may be any that keep to these rules, and one draw needn't show every extreme that they name: `series_ids`: ids never fall along the window; each series covers 1 to 5120 consecutive rows, one series exactly that many.
All inputs are finite; a program needn't handle non-finite values.
Results may differ from the reference program's by a relative error of at most 0.025.
Values may be sent and summed in bfloat16 or wider, within the bound.
A program may use at most 128 MiB of HBM per device.

```python
import math
import jax
import jax.numpy as jnp
import numpy as np
from jax import lax

D = 2048
HEADS = 16
HD = 128
FF = 8192
SD = 512
SFF = 2048
SERIES = 8
TOKENS = 8192


def shared_base(key):
    return jax.random.normal(key, (D, D), jnp.float32)


def draw_w_query(key, part):
    base = shared_base(key)
    return (base * D ** (-0.5)).astype(jnp.bfloat16)


def draw_w_key(key, part):
    key = jax.random.fold_in(key, 12)
    fresh = jax.random.normal(key, (D, D), jnp.float32)
    return (fresh * D ** (-0.5)).astype(jnp.bfloat16)


def with_ends(entries, own_key, smallest, top_value):
    longest = entries.shape.index(max(entries.shape))
    spots = []
    for shift in (0, 1):
        where = [jax.random.randint(jax.random.fold_in(own_key, axis), (), 0, length) for axis, length in enumerate(entries.shape)]
        where[longest] = (where[longest] + shift) % entries.shape[longest]
        spots.append(tuple(where))
    return entries.at[spots[0]].set(smallest).at[spots[1]].set(top_value)


def block_levels(rng, extent, split, low, high):
    level = 1.0
    for axis_at, blocks in split:
        heights = jax.random.uniform(jax.random.fold_in(jax.random.fold_in(rng, 6), axis_at), (blocks,), jnp.float32, low / len(split), high / len(split))
        level = level * jnp.repeat(jnp.exp(heights), extent[axis_at] // blocks).reshape((-1,) + (1,) * (len(extent) - 1 - axis_at))
    return level


def length_profile(number_of, total, most, slope):
    loads = [(1 << 20) // math.isqrt(rank ** slope) + 1 for rank in range(2, number_of + 1)]
    spare, holding = total - most - (number_of - 1), [1] * (number_of - 1)
    while spare > 0:
        movable = [i for i in range(number_of - 1) if holding[i] < most]
        pool, budget = sum([loads[i] for i in movable]), spare
        for i in movable:
            more = min(most - holding[i], max(1, budget * loads[i] // pool), spare)
            holding[i] = holding[i] + more
            spare = spare - more
    return np.array([most] + holding)


def uneven_parts(stream_key, number_of, total, most, slope):
    if number_of == 2:
        one = jax.random.randint(stream_key, (), max(1, total - most), min(most, total - 1) + 1)
        return jnp.stack([one, total - one])
    tallies = jnp.asarray(length_profile(number_of, total, most, slope), jnp.int32)
    pairs = (number_of - 1) // 2
    giver, sink = tallies[1:1 + 2 * pairs:2], tallies[2:2 + 2 * pairs:2]
    slack = jnp.minimum(giver - 1, most - sink)
    moved = jax.random.randint(jax.random.fold_in(stream_key, 1), (pairs,), 0, 1 << 20) % (slack + 1)
    tallies = tallies.at[1:1 + 2 * pairs:2].set(giver - moved).at[2:2 + 2 * pairs:2].set(sink + moved)
    return tallies[jax.random.permutation(jax.random.fold_in(stream_key, 2), number_of)]


def scatter_about(own_key, dims, spread, limit, cuts=(), kind=jnp.bfloat16):
    values = spread * jax.random.normal(own_key, dims, jnp.float32)
    if cuts:
        values = values * block_levels(own_key, dims, cuts, -0.22, 0.18)
    return jnp.clip(values, -limit, limit).astype(kind)


def setup_inputs(seed: int = 0) -> dict:
    arg_keys = jax.random.split(jax.random.key(seed), 18)
    tokens = scatter_about(arg_keys[0], (TOKENS, D), 1.0, 6.0, ((0, 16), (1, 16)))
    series_ids = jnp.searchsorted(jnp.cumsum(uneven_parts(arg_keys[1], SERIES, TOKENS, 5 * TOKENS // 8, 1)), jnp.arange(TOKENS), side="right").astype(jnp.int32)
    offsets = with_ends(jax.random.randint(arg_keys[2], (TOKENS,), 0, 65536), jax.random.fold_in(arg_keys[2], 1), 0, 65535).astype(jnp.int32)
    norm_gain = jnp.clip(1.0 + 0.1 * jax.random.normal(arg_keys[3], (D,), jnp.float32), 0.5, 1.5)
    mlp_gain = jnp.clip(1.0 + 0.1 * jax.random.normal(arg_keys[4], (D,), jnp.float32), 0.5, 1.5)
    w_query = draw_w_query(jax.random.fold_in(arg_keys[17], 71), 0)
    w_key = draw_w_key(jax.random.fold_in(arg_keys[17], 71), 0)
    w_value = scatter_about(arg_keys[7], (D, D), D ** -0.5, 0.125, ((1, 16),))
    w_out = scatter_about(arg_keys[8], (D, D), D ** -0.5, 0.125, ((0, 16),))
    w_gate = scatter_about(arg_keys[9], (D, FF), D ** -0.5, 0.125, ((1, 16),))
    w_up = scatter_about(arg_keys[10], (D, FF), D ** -0.5, 0.125, ((1, 16),))
    w_down = scatter_about(arg_keys[11], (FF, D), FF ** -0.5, 0.0625, ((0, 16),))
    projector = scatter_about(arg_keys[12], (D, SD), D ** -0.5, 0.125)
    student_in = scatter_about(arg_keys[13], (TOKENS, SD), 1.0, 6.0, ((0, 16),))
    s_gate = scatter_about(arg_keys[14], (SD, SFF), SD ** -0.5, 0.25, ((1, 16),))
    s_up = scatter_about(arg_keys[15], (SD, SFF), SD ** -0.5, 0.25, ((1, 16),))
    s_down = scatter_about(arg_keys[16], (SFF, SD), SFF ** -0.5, 0.125, ((0, 16),))
    return {"tokens": tokens, "series_ids": series_ids, "offsets": offsets, "norm_gain": norm_gain, "mlp_gain": mlp_gain, "w_query": w_query, "w_key": w_key, "w_value": w_value, "w_out": w_out, "w_gate": w_gate, "w_up": w_up, "w_down": w_down, "projector": projector, "student_in": student_in, "s_gate": s_gate, "s_up": s_up, "s_down": s_down}


def rms_scale(values):
    return values * lax.rsqrt(lax.optimization_barrier(jnp.mean(values * values, axis=-1, keepdims=True)) + 1e-05)

def frequencies(head_dim):
    indices = jnp.arange(head_dim // 2).astype(jnp.float32)
    return jnp.exp(-jnp.log(500000.0) * 2.0 * indices / head_dim)

def rotary(inputs, angles):
    half_dim = inputs.shape[-1] // 2
    cosine = jnp.cos(angles)
    sine = jnp.sin(angles)
    first_half = inputs[..., :half_dim]
    second_half = inputs[..., half_dim:]
    return jnp.concatenate([first_half * cosine - second_half * sine, first_half * sine + second_half * cosine], axis=-1)

def reference(tokens, series_ids, offsets, norm_gain, mlp_gain, w_query, w_key, w_value, w_out, w_gate, w_up, w_down, projector, student_in, s_gate, s_up, s_down):
    tokens_full = tokens.astype(jnp.float32)
    normed = (rms_scale(tokens_full) * norm_gain).astype(jnp.bfloat16)
    angles = offsets.astype(jnp.float32)[:, None, None] * frequencies(HD)[None, None, :]
    queries = rotary(jnp.dot(normed, w_query, preferred_element_type=jnp.float32).reshape(TOKENS, HEADS, HD), angles).astype(jnp.bfloat16)
    keys_rot = rotary(jnp.dot(normed, w_key, preferred_element_type=jnp.float32).reshape(TOKENS, HEADS, HD), angles).astype(jnp.bfloat16)
    values_all = jnp.dot(normed, w_value, preferred_element_type=jnp.float32).astype(jnp.bfloat16).reshape(TOKENS, HEADS, HD)
    position = jnp.arange(TOKENS, dtype=jnp.int32)
    allowed = (position[None, :] <= position[:, None]) & (series_ids[None, :] == series_ids[:, None])
    factor = HD ** (-0.5)

    def one_head(head_index):
        query_head = lax.dynamic_index_in_dim(queries, head_index, 1, keepdims=False)
        key_head = lax.dynamic_index_in_dim(keys_rot, head_index, 1, keepdims=False)
        value_head = lax.dynamic_index_in_dim(values_all, head_index, 1, keepdims=False)
        scores = jnp.dot(query_head, key_head.T, preferred_element_type=jnp.float32) * factor
        scores = jnp.where(allowed, scores, -1e+30)
        peak = lax.optimization_barrier(jnp.max(scores, axis=1, keepdims=True))
        weights = jnp.where(allowed, jnp.exp(scores - peak), 0.0)
        denom = lax.optimization_barrier(jnp.sum(weights, axis=1, keepdims=True))
        result = jnp.dot(weights.astype(jnp.bfloat16), value_head, preferred_element_type=jnp.float32) / denom
        return result.astype(jnp.bfloat16)
    heads_out = lax.map(one_head, jnp.arange(HEADS, dtype=jnp.int32))
    attended = jnp.transpose(heads_out, (1, 0, 2)).reshape(TOKENS, D)
    mixed = (tokens_full + jnp.dot(attended, w_out, preferred_element_type=jnp.float32)).astype(jnp.bfloat16)
    normed_two = (rms_scale(mixed.astype(jnp.float32)) * mlp_gain).astype(jnp.bfloat16)
    gate_out = jnp.dot(normed_two, w_gate, preferred_element_type=jnp.float32)
    up_out = jnp.dot(normed_two, w_up, preferred_element_type=jnp.float32)
    hidden = (jax.nn.silu(gate_out) * up_out).astype(jnp.bfloat16)
    teacher_out = (mixed.astype(jnp.float32) + jnp.dot(hidden, w_down, preferred_element_type=jnp.float32)).astype(jnp.bfloat16)
    target = jnp.dot(teacher_out, projector, preferred_element_type=jnp.float32)
    student_full = student_in.astype(jnp.float32)
    student_normed = rms_scale(student_full).astype(jnp.bfloat16)
    s_gate_out = jnp.dot(student_normed, s_gate, preferred_element_type=jnp.float32)
    s_up_out = jnp.dot(student_normed, s_up, preferred_element_type=jnp.float32)
    sigmoid_gate = jax.nn.sigmoid(s_gate_out)
    s_hidden = (s_gate_out * sigmoid_gate * s_up_out).astype(jnp.bfloat16)
    predicted = student_full + jnp.dot(s_hidden, s_down, preferred_element_type=jnp.float32)
    difference = predicted - target
    error = jnp.mean(difference * difference)
    scaled = (difference * TOKENS ** (-0.5)).astype(jnp.bfloat16)
    grad_down = jnp.dot(s_hidden.T, scaled, preferred_element_type=jnp.float32)
    grad_hidden = jnp.dot(scaled, s_down.T, preferred_element_type=jnp.float32)
    grad_up_in = (grad_hidden * s_gate_out * sigmoid_gate).astype(jnp.bfloat16)
    grad_gate_in = (grad_hidden * s_up_out * sigmoid_gate * (1.0 + s_gate_out * (1.0 - sigmoid_gate))).astype(jnp.bfloat16)
    grad_gate = jnp.dot(student_normed.T, grad_gate_in, preferred_element_type=jnp.float32)
    grad_up = jnp.dot(student_normed.T, grad_up_in, preferred_element_type=jnp.float32)
    return (teacher_out, grad_gate, grad_up, grad_down, error)
```

```python
import functools

import jax
import jax.numpy as jnp
from jax import lax
from jax.experimental import pallas as pl
from jax.experimental.pallas import tpu as pltpu
from jax.sharding import PartitionSpec as P

HD = 128
NZ = 8
NY = 4
MESH = pl.DeviceIdType.MESH
VM = pl.BlockSpec(memory_space=pltpu.VMEM)
SM = pl.BlockSpec(memory_space=pltpu.SMEM)
LIMIT = 56 * 1024 * 1024
F32 = jnp.float32
BF16 = jnp.bfloat16


def params(collective_id):
    return pltpu.CompilerParams(
        collective_id=collective_id, has_side_effects=True, vmem_limit_bytes=LIMIT
    )


def remote(src, dst, send_sem, recv_sem, device):
    return pltpu.make_async_remote_copy(
        src_ref=src,
        dst_ref=dst,
        send_sem=send_sem,
        recv_sem=recv_sem,
        device_id=device,
        device_id_type=MESH,
    )


def greet(devices):
    barrier = pltpu.get_barrier_semaphore()
    for device in devices:
        pl.semaphore_signal(barrier, inc=1, device_id=device, device_id_type=MESH)
    pl.semaphore_wait(barrier, len(devices))


def places():
    dp, tensor = lax.axis_index("dp"), lax.axis_index("tensor")
    x_hi, z = tensor // NZ, lax.rem(tensor, NZ)
    return dp, tensor, x_hi, z


def turn(z, by, size):
    return lax.rem(z + by + size, size)


def carries(way, far, half):
    return far < 4 or half == way


class Ring:
    def __init__(self, ref, at, z, device, send_sem, recv_sem):
        self.ref, self.at, self.z = ref, at, z
        self.next = (device(turn(z, 1, NZ)), device(turn(z, -1, NZ)))
        self.send_sem, self.recv_sem = send_sem, recv_sem
        self.sent = []

    def copy(self, way, far, half, hops):
        sign = 1 if way == 0 else -1
        block = self.ref.at[self.at(turn(self.z, -sign * hops, NZ), half)]
        return remote(
            block,
            block,
            self.send_sem.at[way, far - 1, half],
            self.recv_sem.at[way, far - 1, half],
            self.next[way],
        )

    def send(self, way, far, half):
        copy = self.copy(way, far, half, far - 1)
        copy.start()
        self.sent.append(copy)

    def arrived(self, way, far, half):
        self.copy(way, far, half, far).wait_recv()

    def finish(self):
        for copy in self.sent:
            copy.wait_send()


def gather_body(order, x_ref, out_ref, send_sem, recv_sem, x_send, x_recv):
    dp, tensor, x_hi, z = places()
    partner = (dp, (1 - x_hi) * NZ + z)

    def device(zz):
        return (dp, x_hi * NZ + zz)

    def at(zz, half):
        xx = x_hi if half == 0 else 1 - x_hi
        return xx * NZ + zz if order == "tensor" else zz * 2 + xx

    ring = Ring(out_ref, at, z, device, send_sem, recv_sem)
    out_ref[at(z, 0)] = x_ref[...]
    greet([partner, ring.next[0], ring.next[1]])
    own = out_ref.at[at(z, 0)]
    other = out_ref.at[at(z, 1)]
    cross = remote(own, own, x_send, x_recv, partner)
    cross.start()
    for half in range(2):
        if half == 1:
            remote(other, other, x_send, x_recv, partner).wait_recv()
        for way in range(2):
            ring.send(way, 1, half)
    for far in range(2, 5):
        for half in range(2):
            for way in range(2):
                if carries(way, far, half):
                    ring.arrived(way, far - 1, half)
                    ring.send(way, far, half)
    for way in range(2):
        ring.arrived(way, 3, 1 - way)
        ring.arrived(way, 4, way)
    cross.wait_send()
    ring.finish()


def tensor_gather(block, order, collective_id):
    return pl.pallas_call(
        functools.partial(gather_body, order),
        out_shape=jax.ShapeDtypeStruct((2 * NZ,) + block.shape, block.dtype),
        in_specs=[VM],
        out_specs=VM,
        scratch_shapes=[
            pltpu.SemaphoreType.DMA((2, 4, 2)),
            pltpu.SemaphoreType.DMA((2, 4, 2)),
            pltpu.SemaphoreType.DMA,
            pltpu.SemaphoreType.DMA,
        ],
        compiler_params=params(collective_id),
        name="tensor_gather",
    )(block)


def scatter_body(
    part_ref, out_ref, sbuf, rbuf, xsend_buf, xrecv_buf, send_sem, recv_sem, x_send, x_recv
):
    dp, tensor, x_hi, z = places()
    partner = (dp, (1 - x_hi) * NZ + z)
    nexts = ((dp, x_hi * NZ + turn(z, 1, NZ)), (dp, x_hi * NZ + turn(z, -1, NZ)))

    def at(zz, half):
        return zz * 2 + (x_hi if half == 0 else 1 - x_hi)

    greet([partner, nexts[0], nexts[1]])
    sent = []

    def copy(way, far, half, src):
        return remote(
            src,
            rbuf.at[way, far - 1, half],
            send_sem.at[way, far - 1, half],
            recv_sem.at[way, far - 1, half],
            nexts[way],
        )

    def arrived(way, far, half):
        copy(way, far, half, rbuf.at[way, far - 1, half]).wait_recv()

    for far in range(4, 0, -1):
        for half in (1, 0):
            for way in range(2):
                if not carries(way, far, half):
                    continue
                place = at(turn(z, far if way == 0 else -far, NZ), half)
                if far == 4 or (far == 3 and half != way):
                    src = part_ref.at[place]
                else:
                    arrived(way, far + 1, half)
                    sbuf[way, far - 1, half] = (
                        part_ref[place].astype(F32) + rbuf[way, far, half].astype(F32)
                    ).astype(BF16)
                    src = sbuf.at[way, far - 1, half]
                one = copy(way, far, half, src)
                one.start()
                sent.append(one)

    def total(half):
        for way in range(2):
            arrived(way, 1, half)
        return (
            part_ref[at(z, half)].astype(F32)
            + rbuf[0, 0, half].astype(F32)
            + rbuf[1, 0, half].astype(F32)
        )

    xsend_buf[...] = total(1).astype(BF16)
    cross = remote(xsend_buf, xrecv_buf, x_send, x_recv, partner)
    cross.start()
    mine = total(0)
    cross.wait_recv()
    out_ref[...] = mine + xrecv_buf[...].astype(F32)
    cross.wait_send()
    for one in sent:
        one.wait_send()


def tensor_scatter(part, collective_id):
    block = part.shape[1:]
    return pl.pallas_call(
        scatter_body,
        out_shape=jax.ShapeDtypeStruct(block, F32),
        in_specs=[VM],
        out_specs=VM,
        scratch_shapes=[
            pltpu.VMEM((2, 4, 2) + block, BF16),
            pltpu.VMEM((2, 4, 2) + block, BF16),
            pltpu.VMEM(block, BF16),
            pltpu.VMEM(block, BF16),
            pltpu.SemaphoreType.DMA((2, 4, 2)),
            pltpu.SemaphoreType.DMA((2, 4, 2)),
            pltpu.SemaphoreType.DMA,
            pltpu.SemaphoreType.DMA,
        ],
        compiler_params=params(collective_id),
        name="tensor_scatter",
    )(part)


def dp_gather_body(x_ref, out_ref, y_send, y_recv, x_send, x_recv, c_send, c_recv):
    dp, tensor, _, _ = places()
    x_lo, y, core = dp // (2 * NY), lax.rem(dp // 2, NY), lax.rem(dp, 2)

    def index(xx, yy, cc):
        return xx * 2 * NY + yy * 2 + cc

    def at(yy, half, cc):
        return index(x_lo if half == 0 else 1 - x_lo, yy, cc)

    partner = (index(1 - x_lo, y, core), tensor)
    sibling = (index(x_lo, y, 1 - core), tensor)
    nexts = (
        (index(x_lo, turn(y, 1, NY), core), tensor),
        (index(x_lo, turn(y, -1, NY), core), tensor),
    )
    out_ref[at(y, 0, core)] = x_ref[...]
    greet([partner, sibling, nexts[0], nexts[1]])
    sent = []

    def start(copy):
        copy.start()
        sent.append(copy)

    def share(yy, half, slot):
        block = out_ref.at[at(yy, half, core)]
        start(remote(block, block, c_send.at[slot], c_recv.at[slot], sibling))

    def copy(way, far, half, hops):
        block = out_ref.at[at(turn(y, -hops if way == 0 else hops, NY), half, core)]
        return remote(
            block,
            block,
            y_send.at[way, far - 1, half],
            y_recv.at[way, far - 1, half],
            nexts[way],
        )

    own = out_ref.at[at(y, 0, core)]
    other = out_ref.at[at(y, 1, core)]
    start(remote(own, own, x_send, x_recv, partner))
    for way in range(2):
        start(copy(way, 1, 0, 0))
    share(y, 0, 0)
    remote(other, other, x_send, x_recv, partner).wait_recv()
    for way in range(2):
        start(copy(way, 1, 1, 0))
    share(y, 1, 1)
    slot = 2
    origins = []
    for half in range(2):
        for way in range(2):
            copy(way, 1, half, 1).wait_recv()
            if half == way:
                start(copy(way, 2, half, 1))
            origin = turn(y, -1 if way == 0 else 1, NY)
            share(origin, half, slot)
            slot += 1
    for way in range(2):
        copy(way, 2, way, 2).wait_recv()
        share(turn(y, 2, NY), way, slot)
        slot += 1
    arrivals = [(0, 0), (0, 1), (-1, 0), (1, 0), (-1, 1), (1, 1), (2, 0), (2, 1)]
    for slot, (by, half) in enumerate(arrivals):
        block = out_ref.at[at(turn(y, by, NY), half, 1 - core)]
        remote(block, block, c_send.at[slot], c_recv.at[slot], sibling).wait_recv()
    for one in sent:
        one.wait_send()


def dp_gather(block, collective_id):
    return pl.pallas_call(
        dp_gather_body,
        out_shape=jax.ShapeDtypeStruct((4 * NY,) + block.shape, block.dtype),
        in_specs=[VM],
        out_specs=VM,
        scratch_shapes=[
            pltpu.SemaphoreType.DMA((2, 2, 2)),
            pltpu.SemaphoreType.DMA((2, 2, 2)),
            pltpu.SemaphoreType.DMA,
            pltpu.SemaphoreType.DMA,
            pltpu.SemaphoreType.DMA((8,)),
            pltpu.SemaphoreType.DMA((8,)),
        ],
        compiler_params=params(collective_id),
        name="dp_gather",
    )(block)


def dp_sum_body(
    part_ref,
    square_ref,
    out_ref,
    total_ref,
    inbox,
    squares,
    result,
    send1,
    recv1,
    send2,
    recv2,
    send3,
    recv3,
):
    dp, tensor, _, _ = places()
    size = 4 * NY
    peers = [turn(dp, by, size) for by in range(1, size)]
    greet([(peer, tensor) for peer in peers])
    sent = []

    def start(copy):
        copy.start()
        sent.append(copy)

    for by, peer in enumerate(peers):
        start(
            remote(part_ref.at[peer], inbox.at[by], send1.at[by], recv1.at[by], (peer, tensor))
        )
        start(remote(square_ref, squares.at[by], send2.at[by], recv2.at[by], (peer, tensor)))
    total = part_ref[dp].astype(F32)
    for by, peer in enumerate(peers):
        remote(
            part_ref.at[peer], inbox.at[by], send1.at[by], recv1.at[by], (peer, tensor)
        ).wait_recv()
        total = total + inbox[by].astype(F32)
    result[dp] = total.astype(BF16)
    mine = result.at[dp]
    for by, peer in enumerate(peers):
        start(remote(mine, mine, send3.at[by], recv3.at[by], (peer, tensor)))
    square = square_ref[...]
    for by, peer in enumerate(peers):
        remote(square_ref, squares.at[by], send2.at[by], recv2.at[by], (peer, tensor)).wait_recv()
        square = square + squares[by]
    total_ref[...] = square
    for by, peer in enumerate(peers):
        origin = turn(dp, -(by + 1), size)
        block = result.at[origin]
        remote(block, block, send3.at[by], recv3.at[by], (peer, tensor)).wait_recv()
    out_ref[...] = result[...].astype(F32)
    for one in sent:
        one.wait_send()


def dp_sum(part, square, collective_id):
    size = 4 * NY
    return pl.pallas_call(
        dp_sum_body,
        out_shape=(
            jax.ShapeDtypeStruct(part.shape, F32),
            jax.ShapeDtypeStruct(square.shape, F32),
        ),
        in_specs=[VM, VM],
        out_specs=(VM, VM),
        scratch_shapes=[
            pltpu.VMEM((size - 1,) + part.shape[1:], BF16),
            pltpu.VMEM((size - 1,) + square.shape, F32),
            pltpu.VMEM(part.shape, BF16),
        ]
        + [pltpu.SemaphoreType.DMA((size - 1,))] * 6,
        compiler_params=params(collective_id),
        name="dp_sum",
    )(part, square)


def spread_body(
    scaled_ref,
    teacher_ref,
    out_ref,
    columns_ref,
    send_sem,
    recv_sem,
    x_send,
    x_recv,
    t_send,
    t_recv,
):
    dp, tensor, x_hi, z = places()
    partner = (dp, (1 - x_hi) * NZ + z)
    size = 2 * NZ
    row = z * 2 + x_hi

    def device(zz):
        return (dp, x_hi * NZ + zz)

    def at(zz, half):
        return zz * 2 + (x_hi if half == 0 else 1 - x_hi)

    ring = Ring(out_ref, at, z, device, send_sem, recv_sem)
    out_ref[row] = scaled_ref[...]
    peers = [turn(tensor, by, size) for by in range(1, size)]
    greet([(dp, peer) for peer in peers])
    own = out_ref.at[at(z, 0)]
    other = out_ref.at[at(z, 1)]
    cross = remote(own, own, x_send, x_recv, partner)
    cross.start()
    for half in range(2):
        if half == 1:
            remote(other, other, x_send, x_recv, partner).wait_recv()
        for way in range(2):
            ring.send(way, 1, half)
    sent = []
    for by, peer in enumerate(peers):
        one = remote(
            teacher_ref.at[peer],
            columns_ref.at[row],
            t_send.at[by],
            t_recv.at[by],
            (dp, peer),
        )
        one.start()
        sent.append(one)
    columns_ref[row] = teacher_ref[tensor]
    for far in range(2, 5):
        for half in range(2):
            for way in range(2):
                if carries(way, far, half):
                    ring.arrived(way, far - 1, half)
                    ring.send(way, far, half)
    for way in range(2):
        ring.arrived(way, 3, 1 - way)
        ring.arrived(way, 4, way)
    for by, peer in enumerate(peers):
        origin = turn(tensor, -(by + 1), size)
        theirs = columns_ref.at[lax.rem(origin, NZ) * 2 + origin // NZ]
        remote(theirs, theirs, t_send.at[by], t_recv.at[by], (dp, peer)).wait_recv()
    cross.wait_send()
    for one in sent:
        one.wait_send()
    ring.finish()


def spread(scaled, teacher, collective_id):
    size = 2 * NZ
    return pl.pallas_call(
        spread_body,
        out_shape=(
            jax.ShapeDtypeStruct((size,) + scaled.shape, scaled.dtype),
            jax.ShapeDtypeStruct((size,) + teacher.shape[1:], teacher.dtype),
        ),
        in_specs=[VM, VM],
        out_specs=(VM, VM),
        scratch_shapes=[
            pltpu.SemaphoreType.DMA((2, 4, 2)),
            pltpu.SemaphoreType.DMA((2, 4, 2)),
            pltpu.SemaphoreType.DMA,
            pltpu.SemaphoreType.DMA,
            pltpu.SemaphoreType.DMA((size - 1,)),
            pltpu.SemaphoreType.DMA((size - 1,)),
        ],
        compiler_params=params(collective_id),
        name="spread",
    )(scaled, teacher)


def attention_body(tile, bounds, query_ref, pair_ref, start_ref, out_ref):
    rows = query_ref.shape[0]
    span = pair_ref.shape[2]
    mine = bounds[0]
    factor = HD ** (-0.5) * 1.4426950408889634
    for index in range(rows // tile):
        at = pl.ds(index * tile, tile)
        query = query_ref[at, :]
        start = start_ref[at, :]
        position = mine * rows + index * tile + lax.broadcasted_iota(jnp.int32, (tile, 1), 0)

        def step(masked, j, carry):
            peak, denom, accum = carry
            scores = lax.dot_general(
                query, pair_ref[j, 0], (((1,), (1,)), ((), ())), preferred_element_type=F32
            )
            if masked:
                column = j * span + lax.broadcasted_iota(jnp.int32, (tile, span), 1)
                allowed = (column >= start) & (column <= position)
                scores = jnp.where(allowed, scores, -1e30)
            new_peak = jnp.maximum(peak, jnp.max(scores, axis=1, keepdims=True))
            weights = jnp.exp2((scores - new_peak) * factor)
            if masked:
                weights = jnp.where(allowed, weights, 0.0)
            scale = jnp.exp2((peak - new_peak) * factor)
            denom = denom * scale + jnp.sum(weights, axis=1, keepdims=True)
            accum = accum * scale + jnp.dot(
                weights.astype(BF16), pair_ref[j, 1], preferred_element_type=F32
            )
            return new_peak, denom, accum

        carry = (
            jnp.full((tile, 1), -1e30, F32),
            jnp.zeros((tile, 1), F32),
            jnp.zeros((tile, HD), F32),
        )
        low, inner = bounds[1 + 2 * index], bounds[2 + 2 * index]
        carry = lax.fori_loop(low, inner, functools.partial(step, True), carry)
        carry = lax.fori_loop(inner, mine, functools.partial(step, False), carry)
        peak, denom, accum = step(True, mine, carry)
        out_ref[at, :] = (accum / denom).astype(BF16)


def attention(query, pairs, starts, first_row):
    rows, span, tile = query.shape[0], pairs.shape[2], 256
    mine = first_row // rows
    bounds = [mine]
    for index in range(rows // tile):
        bounds.append(starts[index * tile] // span)
        last = starts[(index + 1) * tile - 1]
        bounds.append(jnp.minimum((last + span - 1) // span, mine))
    return pl.pallas_call(
        functools.partial(attention_body, tile),
        out_shape=jax.ShapeDtypeStruct(query.shape, BF16),
        in_specs=[SM, VM, VM, VM],
        out_specs=VM,
        compiler_params=pltpu.CompilerParams(vmem_limit_bytes=LIMIT),
        name="attention",
    )(jnp.stack(bounds).astype(jnp.int32), query, pairs, starts[:, None])


def rms_scale(values):
    return values * lax.rsqrt(jnp.mean(values * values, axis=-1, keepdims=True) + 1e-05)


def frequencies(head_dim):
    indices = jnp.arange(head_dim // 2).astype(F32)
    return jnp.exp(-jnp.log(500000.0) * 2.0 * indices / head_dim)


def local(
    tokens,
    series_ids,
    offsets,
    norm_gain,
    mlp_gain,
    w_query,
    w_key,
    w_value,
    w_out,
    w_gate,
    w_up,
    w_down,
    projector,
    student_in,
    s_gate,
    s_up,
    s_down,
):
    rows = tokens.shape[0]
    size = 2 * NZ
    own = rows // size
    dp, tensor, x_hi, z = places()
    first_row = dp * rows
    my_rows = (z * 2 + x_hi) * own

    angles = offsets.astype(F32)[:, None] * frequencies(HD)[None, :]
    cosine, sine = jnp.cos(angles), jnp.sin(angles)

    def rotary(values):
        a, b = values[:, : HD // 2], values[:, HD // 2 :]
        return jnp.concatenate([a * cosine - b * sine, a * sine + b * cosine], axis=1).astype(BF16)

    student_full = student_in.astype(F32)
    student_normed = rms_scale(student_full).astype(BF16)
    s_gate_out = jnp.dot(student_normed, s_gate, preferred_element_type=F32)
    s_up_out = jnp.dot(student_normed, s_up, preferred_element_type=F32)
    sigmoid_gate = jax.nn.sigmoid(s_gate_out)
    s_hidden = (s_gate_out * sigmoid_gate * s_up_out).astype(BF16)
    student_part = jnp.dot(s_hidden, s_down, preferred_element_type=F32).astype(BF16)
    student_sum = tensor_scatter(student_part.reshape(size, own, -1), 1)

    blocks = tensor_gather(tokens, "tensor", 2)
    tokens_full = jnp.transpose(blocks, (1, 0, 2)).reshape(rows, -1)
    normed = (rms_scale(tokens_full.astype(F32)) * norm_gain).astype(BF16)
    query = rotary(jnp.dot(normed, w_query, preferred_element_type=F32))
    key = rotary(jnp.dot(normed, w_key, preferred_element_type=F32))
    value = jnp.dot(normed, w_value, preferred_element_type=F32).astype(BF16)
    pairs = dp_gather(jnp.stack([key, value]), 3)

    series = jnp.arange(8, dtype=jnp.int32)
    series_start = jnp.sum((series_ids[None, :] < series[:, None]).astype(jnp.int32), axis=1)
    query_series = lax.dynamic_slice_in_dim(series_ids, first_row, rows, 0)
    starts = jnp.sum(
        jnp.where(query_series[:, None] == series[None, :], series_start[None, :], 0), axis=1
    )
    attended = attention(query, pairs, starts, first_row)

    partial_out = jnp.dot(attended, w_out, preferred_element_type=F32).astype(BF16)
    own_sum = tensor_scatter(partial_out.reshape(size, own, -1), 4)
    my_tokens = lax.dynamic_slice_in_dim(tokens_full, my_rows, own, 0).astype(F32)
    mixed = (my_tokens + own_sum).astype(BF16)
    normed_two = (rms_scale(mixed.astype(F32)) * mlp_gain).astype(BF16)
    normed_two = tensor_gather(normed_two, "rows", 5).reshape(rows, -1)

    gate_out = jnp.dot(normed_two, w_gate, preferred_element_type=F32)
    up_out = jnp.dot(normed_two, w_up, preferred_element_type=F32)
    hidden = (jax.nn.silu(gate_out) * up_out).astype(BF16)
    mlp_part = jnp.dot(hidden, w_down, preferred_element_type=F32).astype(BF16)
    mlp_sum = tensor_scatter(mlp_part.reshape(size, own, -1), 6)
    teacher = (mixed.astype(F32) + mlp_sum).astype(BF16)

    target = jnp.dot(teacher, projector, preferred_element_type=F32)
    my_student = lax.dynamic_slice_in_dim(student_in, my_rows, own, 0).astype(F32)
    difference = my_student + student_sum - target
    total_rows = rows * lax.axis_size("dp")
    scaled = (difference * total_rows ** (-0.5)).astype(BF16)
    teacher_columns = jnp.transpose(teacher.reshape(own, size, -1), (1, 0, 2))
    scaled, teacher_out = spread(scaled, teacher_columns, 7)
    scaled = scaled.reshape(rows, -1)
    teacher_out = teacher_out.reshape(rows, -1)

    grad_hidden = jnp.einsum("rc,kc->rk", scaled, s_down, preferred_element_type=F32)
    grad_up_in = (grad_hidden * s_gate_out * sigmoid_gate).astype(BF16)
    grad_gate_in = (
        grad_hidden * s_up_out * sigmoid_gate * (1.0 + s_gate_out * (1.0 - sigmoid_gate))
    ).astype(BF16)
    grads = [
        jnp.einsum("rc,rk->ck", left, right, preferred_element_type=F32).astype(BF16)
        for left, right in (
            (student_normed, grad_gate_in),
            (student_normed, grad_up_in),
            (scaled, s_hidden),
        )
    ]
    units = grads[0].shape[1]
    parts = jnp.stack([one.reshape(size, -1, units) for one in grads], axis=1)
    parts = parts.reshape(size, -1, units)
    squares = jnp.square(scaled.astype(F32))
    squares = jnp.sum(squares.reshape(-1, 8, 128), axis=0)
    sums, square_total = dp_sum(parts, squares, 8)
    sums = sums.reshape(size, 3, -1, units)
    grad_gate, grad_up, grad_down = (sums[:, i].reshape(-1, units) for i in range(3))
    error = jnp.sum(square_total) / student_in.shape[1]
    return (teacher_out, grad_gate, grad_up, grad_down.T, error)


def solution(mesh):
    in_specs = (
        P("dp", "tensor"),
        P(),
        P("dp"),
        P(),
        P(),
        P(None, "tensor"),
        P(None, "tensor"),
        P(None, "tensor"),
        P("tensor", None),
        P(None, "tensor"),
        P(None, "tensor"),
        P("tensor", None),
        P(),
        P("dp", None),
        P(None, "tensor"),
        P(None, "tensor"),
        P("tensor", None),
    )
    out_specs = (P("dp", "tensor"), P(None, "tensor"), P(None, "tensor"), P("tensor", None), P())
    return jax.shard_map(local, mesh=mesh, in_specs=in_specs, out_specs=out_specs, check_vma=False)
```

```python
import functools

import jax
import jax.numpy as jnp
from jax import lax
from jax.experimental import pallas as pl
from jax.experimental.pallas import tpu as pltpu
from jax.sharding import PartitionSpec as P

HD = 128
NZ = 8
NY = 4
MESH = pl.DeviceIdType.MESH
VM = pl.BlockSpec(memory_space=pltpu.VMEM)
SM = pl.BlockSpec(memory_space=pltpu.SMEM)
LIMIT = 56 * 1024 * 1024
F32 = jnp.float32
BF16 = jnp.bfloat16


def params(collective_id):
    return pltpu.CompilerParams(
        collective_id=collective_id, has_side_effects=True, vmem_limit_bytes=LIMIT
    )


def remote(src, dst, send_sem, recv_sem, device):
    return pltpu.make_async_remote_copy(
        src_ref=src,
        dst_ref=dst,
        send_sem=send_sem,
        recv_sem=recv_sem,
        device_id=device,
        device_id_type=MESH,
    )


def greet(devices):
    barrier = pltpu.get_barrier_semaphore()
    for device in devices:
        pl.semaphore_signal(barrier, inc=1, device_id=device, device_id_type=MESH)
    pl.semaphore_wait(barrier, len(devices))


def places():
    dp, tensor = lax.axis_index("dp"), lax.axis_index("tensor")
    x_hi, z = tensor // NZ, lax.rem(tensor, NZ)
    return dp, tensor, x_hi, z


def turn(z, by, size):
    return lax.rem(z + by + size, size)


def dma(*shape):
    return pltpu.SemaphoreType.DMA(shape)


def call(body, name, collective_id, inputs, outputs, scratch, specs=None):
    return pl.pallas_call(
        body,
        out_shape=tuple(jax.ShapeDtypeStruct(shape, kind) for shape, kind in outputs),
        in_specs=specs or [VM] * len(inputs),
        out_specs=tuple([VM] * len(outputs)),
        scratch_shapes=scratch,
        compiler_params=params(collective_id),
        name=name,
    )(*inputs)


class Sent:
    def __init__(self):
        self.copies = []

    def start(self, copy):
        copy.start()
        self.copies.append(copy)

    def finish(self):
        for copy in self.copies:
            copy.wait_send()


def on_ring(way, far, sub):
    return far < 4 or (way == 1) == (sub == 1)


def towards(way, by):
    return by if way == 0 else -by


RING_SEMS = [dma(2, 4, 3), dma(2, 4, 3), dma(9), dma(9)]


def mix_gather(ref, at, half, sems, hook=lambda step: None):
    ring_send, ring_recv, x_send, x_recv = sems
    dp, tensor, x_hi, z = places()
    partner = (dp, (1 - x_hi) * NZ + z)
    nexts = tuple((dp, x_hi * NZ + turn(z, by, NZ)) for by in (1, -1))
    sent = Sent()

    def view(zz, sub):
        plane = x_hi if sub < 2 else 1 - x_hi
        return ref.at[at(zz, plane), pl.ds((sub % 2) * half, half)]

    def ring(way, far, sub, hops):
        block = view(turn(z, -towards(way, hops), NZ), sub)
        sems = ring_send.at[way, far - 1, sub], ring_recv.at[way, far - 1, sub]
        return remote(block, block, *sems, nexts[way])

    def cross(zz, sub, slot):
        block = view(zz, sub)
        return remote(block, block, x_send.at[slot], x_recv.at[slot], partner)

    def slot(way, far):
        return 1 + far + 3 * way if way == 0 else 4 + far

    sent.start(cross(z, 0, 0))
    for sub in range(2):
        for way in range(2):
            sent.start(ring(way, 1, sub, 0))
    sent.start(cross(z, 1, 1))
    hook(0)
    cross(z, 2, 0).wait_recv()
    for way in range(2):
        sent.start(ring(way, 1, 2, 0))
    for far in range(2, 5):
        hook(far - 1)
        for sub in range(3):
            for way in range(2):
                ring(way, far - 1, sub, far - 1).wait_recv()
                if on_ring(way, far, sub):
                    sent.start(ring(way, far, sub, far - 1))
                if sub == 1:
                    origin = turn(z, -towards(way, far - 1), NZ)
                    sent.start(cross(origin, 1, slot(way, far - 1)))
    ring(1, 4, 1, 4).wait_recv()
    sent.start(cross(turn(z, 4, NZ), 1, slot(1, 4)))
    for sub in (0, 2):
        ring(0, 4, sub, 4).wait_recv()
    cross(z, 3, 1).wait_recv()
    for way in range(2):
        for far in range(1, 4 + way):
            cross(turn(z, -towards(way, far), NZ), 3, slot(way, far)).wait_recv()
    sent.finish()


def scatter_scratch(half, width):
    return [
        pltpu.VMEM((2, 4, 3, half, width), BF16),
        pltpu.VMEM((2, 4, 3, half, width), BF16),
        pltpu.VMEM((8, half, width), BF16),
        pltpu.VMEM((half, width), BF16),
        pltpu.VMEM((half, width), BF16),
        dma(2, 4, 3),
        dma(2, 4, 3),
        dma(9),
        dma(9),
    ]


def mix_scatter(part, make, scratch):
    sbuf, rbuf, xbuf, xlast, xgot, ring_send, ring_recv, x_send, x_recv = scratch
    half = sbuf.shape[3]
    dp, tensor, x_hi, z = places()
    partner = (dp, (1 - x_hi) * NZ + z)
    nexts = tuple((dp, x_hi * NZ + turn(z, by, NZ)) for by in (1, -1))
    sent = Sent()

    def view(zz, sub):
        plane = x_hi if sub < 2 else 1 - x_hi
        return part.at[zz * 2 + plane, pl.ds((sub % 2) * half, half)]

    def slot(way, far):
        return 7 if far == 4 else 1 + 3 * way + far - 1

    def cross(zz, at):
        return remote(view(zz, 3), xbuf.at[at], x_send.at[at], x_recv.at[at], partner)

    def ring(way, far, sub, source):
        sems = ring_send.at[way, far - 1, sub], ring_recv.at[way, far - 1, sub]
        return remote(source, rbuf.at[way, far - 1, sub], *sems, nexts[way])

    def arrived(way, far, sub):
        ring(way, far, sub, rbuf.at[way, far - 1, sub]).wait_recv()
        return rbuf[way, far - 1, sub].astype(F32)

    def crossed(at):
        cross(z, at).wait_recv()
        return xbuf[at].astype(F32)

    def send(way, far, sub):
        source = view(turn(z, towards(way, far), NZ), sub)
        extra = []
        if far < 4 and on_ring(way, far + 1, sub):
            extra.append(arrived(way, far + 1, sub))
        if sub == 1:
            extra.append(crossed(slot(way, far)))
        if extra:
            total = source[...].astype(F32)
            for one in extra:
                total = total + one
            sbuf[way, far - 1, sub] = total.astype(BF16)
            source = sbuf.at[way, far - 1, sub]
        sent.start(ring(way, far, sub, source))

    far4 = turn(z, 4, NZ)
    make([far4])
    sent.start(cross(far4, 7))
    for sub in (0, 2):
        send(0, 4, sub)
    for far in (3, 2, 1):
        places_now = [turn(z, by, NZ) for by in (far, -far)]
        make(places_now)
        for way in range(2):
            sent.start(cross(places_now[way], slot(way, far)))
        if far == 3:
            for sub in (0, 2):
                send(1, 3, sub)
            send(1, 4, 1)
        for sub in (2, 0, 1):
            for way in range(2):
                if not (far == 3 and way == 1 and sub != 1):
                    send(way, far, sub)
    make([z])
    sent.start(cross(z, 0))

    def total(sub):
        return view(z, sub)[...].astype(F32) + arrived(0, 1, sub) + arrived(1, 1, sub)

    xlast[...] = total(2).astype(BF16)
    last = remote(xlast, xgot, x_send.at[8], x_recv.at[8], partner)
    sent.start(last)
    second = total(1) + crossed(0)
    first = total(0)
    last.wait_recv()
    first = first + xgot[...].astype(F32)
    return first, second, sent


def rms(values):
    return values * lax.rsqrt(jnp.mean(values * values, axis=-1, keepdims=True) + 1e-05)


def project_body(
    tokens_ref,
    gain_ref,
    cos_ref,
    sin_ref,
    wq_ref,
    wk_ref,
    wv_ref,
    student_ref,
    s_gate_ref,
    s_up_ref,
    s_down_ref,
    query_ref,
    pair_ref,
    my_tokens_ref,
    part_ref,
    normed_t_ref,
    hidden_t_ref,
    gate_ref,
    up_ref,
    blocks,
    normed,
    weights,
    *sems,
):
    dp, tensor, x_hi, z = places()
    rows = tokens_ref.shape[0]
    own = rows // (2 * NZ)
    blocks[tensor] = tokens_ref[...]
    greet(
        [
            (dp, (1 - x_hi) * NZ + z),
            (dp, x_hi * NZ + turn(z, 1, NZ)),
            (dp, x_hi * NZ + turn(z, -1, NZ)),
        ]
    )

    def student(step):
        at = pl.ds(step * 128, 128)
        values = rms(student_ref[at, :].astype(F32))
        normed_t_ref[:, at] = values.T.astype(BF16)
        values = values.astype(BF16)
        gate = jnp.dot(values, s_gate_ref[...], preferred_element_type=F32)
        up = jnp.dot(values, s_up_ref[...], preferred_element_type=F32)
        gate_ref[at, :] = gate
        up_ref[at, :] = up
        hidden = gate * jax.nn.sigmoid(gate) * up
        hidden_t_ref[:, at] = hidden.T.astype(BF16)
        out = jnp.dot(hidden.astype(BF16), s_down_ref[...], preferred_element_type=F32)
        for index in range(128 // own):
            block = out[index * own : (index + 1) * own].astype(BF16)
            part_ref[index % 2, step * (64 // own) + index // 2] = block

    def hook(step):
        if step == 0:
            weights[:, :HD] = wq_ref[...]
            weights[:, HD : 2 * HD] = wk_ref[...]
            weights[:, 2 * HD :] = wv_ref[...]
        student(step)

    mix_gather(blocks, lambda zz, plane: plane * NZ + zz, rows // 2, sems, hook)
    my_rows = pl.multiple_of((z * 2 + x_hi) * own, own)
    for index in range(2 * NZ):
        my_tokens_ref[:, index * HD : (index + 1) * HD] = blocks[index, pl.ds(my_rows, own)]
    tile = 128

    @pl.loop(0, rows // tile)
    def _(step):
        at = pl.ds(pl.multiple_of(step * tile, tile), tile)
        square = jnp.zeros((tile, HD), F32)
        for index in range(2 * NZ):
            value = blocks[index, at].astype(F32)
            square = square + value * value
        mean = jnp.sum(square, axis=1, keepdims=True) / (2 * NZ * HD)
        scale = lax.rsqrt(mean + 1e-05)
        for index in range(2 * NZ):
            lanes = slice(index * HD, (index + 1) * HD)
            value = blocks[index, at].astype(F32) * scale * gain_ref[:, lanes]
            normed[at, lanes] = value.astype(BF16)

    tile = 256

    @pl.loop(0, rows // tile)
    def _(step):
        at = pl.ds(pl.multiple_of(step * tile, tile), tile)
        out = jnp.dot(normed[at, :], weights[...], preferred_element_type=F32)
        cosine, sine = cos_ref[at, :], sin_ref[at, :]

        def rotary(values):
            return (values * cosine + pltpu.roll(values, HD // 2, 1) * sine).astype(BF16)

        query_ref[at, :] = rotary(out[:, :HD])
        pair_ref[0, at, :] = rotary(out[:, HD : 2 * HD])
        pair_ref[1, at, :] = out[:, 2 * HD :].astype(BF16)


def exchange_body(
    pair_ref,
    w_out_ref,
    part_ref,
    out_ref,
    wide_ref,
    sum_ref,
    x_got,
    z_out,
    z_in,
    k_x_send,
    k_x_recv,
    k_y_send,
    k_y_recv,
    k_c_send,
    k_c_recv,
    w_send,
    w_recv,
    wc_send,
    wc_recv,
    s_x_send,
    s_x_recv,
    s_z_send,
    s_z_recv,
):
    dp, tensor, x_hi, z = places()
    x_lo, y, core = dp // (2 * NY), lax.rem(dp // 2, NY), lax.rem(dp, 2)

    def index(xx, yy, cc):
        return xx * 2 * NY + yy * 2 + cc

    def at(yy, half, cc):
        return index(x_lo if half == 0 else 1 - x_lo, yy, cc)

    k_partner = (index(1 - x_lo, y, core), tensor)
    sibling = (index(x_lo, y, 1 - core), tensor)
    y_nexts = tuple((index(x_lo, turn(y, by, NY), core), tensor) for by in (1, -1))
    z_peers = [(dp, x_hi * NZ + turn(z, by, NZ)) for by in range(1, NZ)]
    z_nexts = (z_peers[0], z_peers[-1])
    s_partner = (dp, (1 - x_hi) * NZ + z)
    out_ref[at(y, 0, core)] = pair_ref[...]
    wide_ref[z] = w_out_ref[...]
    greet([k_partner, sibling, s_partner, *y_nexts, *z_peers])
    sent = Sent()
    deep = w_out_ref.shape[0] // 4

    def share(by, half, slot):
        block = out_ref.at[at(turn(y, by, NY), half, core)]
        sent.start(remote(block, block, k_c_send.at[slot], k_c_recv.at[slot], sibling))

    def k_copy(way, far, half, hops):
        block = out_ref.at[at(turn(y, -towards(way, hops), NY), half, core)]
        sems = k_y_send.at[way, far - 1, half], k_y_recv.at[way, far - 1, half]
        return remote(block, block, *sems, y_nexts[way])

    def w_copy(way, far, sub, hops):
        first = pl.multiple_of(core * 2 * deep + sub * deep, deep)
        block = wide_ref.at[turn(z, -towards(way, hops), NZ), pl.ds(first, deep)]
        sems = w_send.at[way, far - 1, sub], w_recv.at[way, far - 1, sub]
        return remote(block, block, *sems, z_nexts[way])

    def w_share(by, slot, cc):
        first = pl.multiple_of(cc * 2 * deep, 2 * deep)
        block = wide_ref.at[turn(z, by, NZ), pl.ds(first, 2 * deep)]
        return remote(block, block, wc_send.at[slot], wc_recv.at[slot], sibling)

    def w_forward(far, sub):
        for way in range(2):
            if far < 4 or sub == way:
                w_copy(way, far, sub, far).wait_recv()
            if far < 3 or (far == 3 and sub == way):
                sent.start(w_copy(way, far + 1, sub, far))

    own = out_ref.at[at(y, 0, core)]
    other = out_ref.at[at(y, 1, core)]
    sent.start(remote(own, own, k_x_send, k_x_recv, k_partner))
    for way in range(2):
        sent.start(k_copy(way, 1, 0, 0))
    for sub in range(2):
        for way in range(2):
            sent.start(w_copy(way, 1, sub, 0))
    s_cross = remote(part_ref.at[1 - x_hi], x_got, s_x_send, s_x_recv, s_partner)
    sent.start(s_cross)
    share(0, 0, 0)

    w_forward(1, 0)
    remote(other, other, k_x_send, k_x_recv, k_partner).wait_recv()
    for way in range(2):
        sent.start(k_copy(way, 1, 1, 0))
    share(0, 1, 1)
    w_forward(1, 1)
    for way in range(2):
        sent.start(w_share(towards(way, -1), way, core))
    s_cross.wait_recv()
    z_out[...] = (part_ref[x_hi].astype(F32) + x_got[...].astype(F32)).astype(BF16)
    for by in range(1, NZ):
        sent.start(
            remote(
                z_out.at[turn(z, by, NZ)],
                z_in.at[by - 1],
                s_z_send.at[by - 1],
                s_z_recv.at[by - 1],
                z_peers[by - 1],
            )
        )

    def k_arrivals(half):
        for way in range(2):
            k_copy(way, 1, half, 1).wait_recv()
            if half == way:
                sent.start(k_copy(way, 2, half, 1))
            share(towards(way, -1), half, 2 + 2 * half + way)

    k_arrivals(0)
    w_forward(2, 0)
    w_forward(2, 1)
    for way in range(2):
        sent.start(w_share(towards(way, -2), 2 + way, core))
    k_arrivals(1)
    w_forward(3, 0)
    w_forward(3, 1)
    for way in range(2):
        sent.start(w_share(towards(way, -3), 4 + way, core))
    for way in range(2):
        k_copy(way, 2, way, 2).wait_recv()
        share(2, way, 6 + way)
    total = z_out[z].astype(F32)
    for by in range(1, NZ):
        got = z_in.at[by - 1]
        remote(got, got, s_z_send.at[by - 1], s_z_recv.at[by - 1], z_peers[by - 1]).wait_recv()
        total = total + z_in[by - 1].astype(F32)
    sum_ref[...] = total
    for sub in range(2):
        w_forward(4, sub)
    sent.start(w_share(4, 6, core))
    for slot, (by, half) in enumerate(
        [(0, 0), (0, 1), (-1, 0), (1, 0), (-1, 1), (1, 1), (2, 0), (2, 1)]
    ):
        block = out_ref.at[at(turn(y, by, NY), half, 1 - core)]
        remote(block, block, k_c_send.at[slot], k_c_recv.at[slot], sibling).wait_recv()
    for slot, by in enumerate([-1, 1, -2, 2, -3, 3, 4]):
        w_share(by, slot, 1 - core).wait_recv()
    sent.finish()


def starts_at(begins, position):
    found = jnp.zeros_like(position)
    for begin in begins:
        found = jnp.where(begin <= position, jnp.maximum(found, begin), found)
    return found


def attention_body(tile, begin_ref, query_ref, pair_ref, out_ref):
    rows = query_ref.shape[0]
    span = pair_ref.shape[2]
    mine = begin_ref[8]
    factor = HD ** (-0.5) * 1.4426950408889634
    begins = [begin_ref[index] for index in range(8)]
    tiles = rows // tile
    queries = [query_ref[index * tile : (index + 1) * tile, :] for index in range(tiles)]
    positions = [
        mine * rows + index * tile + lax.broadcasted_iota(jnp.int32, (tile, 1), 0)
        for index in range(tiles)
    ]
    starts = [starts_at(begins, position) for position in positions]
    first = starts_at(begins, mine * rows)
    last = starts_at(begins, mine * rows + rows - 1)
    low = first // span
    inner = jnp.minimum((last + span - 1) // span, mine)

    def step(masked, j, carries):
        found = []
        for query, position, start, (peak, denom, accum) in zip(
            queries, positions, starts, carries, strict=True
        ):
            scores = lax.dot_general(
                query, pair_ref[j, 0], (((1,), (1,)), ((), ())), preferred_element_type=F32
            )
            if masked:
                column = j * span + lax.broadcasted_iota(jnp.int32, (tile, span), 1)
                allowed = (column >= start) & (column <= position)
                scores = jnp.where(allowed, scores, -1e30)
            new_peak = jnp.maximum(peak, jnp.max(scores, axis=1, keepdims=True))
            weights = jnp.exp2((scores - new_peak) * factor)
            if masked:
                weights = jnp.where(allowed, weights, 0.0)
            scale = jnp.exp2((peak - new_peak) * factor)
            denom = denom * scale + jnp.sum(weights, axis=1, keepdims=True)
            accum = accum * scale + jnp.dot(
                weights.astype(BF16), pair_ref[j, 1], preferred_element_type=F32
            )
            found.append((new_peak, denom, accum))
        return tuple(found)

    state = tuple(
        (
            jnp.full((tile, 1), -1e30, F32),
            jnp.zeros((tile, 1), F32),
            jnp.zeros((tile, HD), F32),
        )
        for _ in range(tiles)
    )
    state = lax.fori_loop(low, inner, functools.partial(step, True), state)
    state = lax.fori_loop(inner, mine, functools.partial(step, False), state)
    state = step(True, mine, state)
    for index, (_, denom, accum) in enumerate(state):
        out_ref[index * tile : (index + 1) * tile, :] = (accum / denom).astype(BF16)


def attention(begins, query, pairs):
    return pl.pallas_call(
        functools.partial(attention_body, 256),
        out_shape=jax.ShapeDtypeStruct(query.shape, BF16),
        in_specs=[SM, VM, VM],
        out_specs=VM,
        compiler_params=pltpu.CompilerParams(vmem_limit_bytes=LIMIT),
        name="attention",
    )(begins, query, pairs)


def layer_body(
    total_rows,
    attended_ref,
    wide_ref,
    my_tokens_ref,
    gain_ref,
    w_gate_hbm,
    w_up_hbm,
    w_down_hbm,
    projector_hbm,
    student_ref,
    student_sum_ref,
    teacher_ref,
    scaled_ref,
    w_gate,
    w_up,
    w_down,
    projector,
    load_sem,
    heads,
    a_send,
    a_recv,
    out_send,
    out_recv,
    o_send,
    o_recv,
    partial,
    blocks,
    hidden,
    parts,
    *rest,
):
    gather_sems, scatter = rest[:4], rest[4:]
    dp, tensor, x_hi, z = places()
    own, width = my_tokens_ref.shape
    pair = 2 * own
    partner = (dp, (1 - x_hi) * NZ + z)
    z_peers = [(dp, x_hi * NZ + turn(z, by, NZ)) for by in range(1, NZ)]
    loads = []
    for index, (far, near) in enumerate(
        (
            (w_gate_hbm, w_gate),
            (w_up_hbm, w_up),
            (w_down_hbm, w_down),
            (projector_hbm, projector),
        )
    ):
        load = pltpu.make_async_copy(far, near, load_sem.at[index])
        load.start()
        loads.append(load)
    greet([partner, *z_peers])
    sent = Sent()

    def rows_of(zz):
        return pl.ds(pl.multiple_of(zz * pair, pair), pair)

    for by in range(1, NZ):
        sent.start(
            remote(
                attended_ref.at[rows_of(turn(z, by, NZ))],
                heads.at[z],
                a_send.at[by - 1],
                a_recv.at[by - 1],
                z_peers[by - 1],
            )
        )
    heads[z] = attended_ref[rows_of(z), :]
    for by in range(1, NZ):
        block = heads.at[turn(z, -by, NZ)]
        remote(block, block, a_send.at[by - 1], a_recv.at[by - 1], z_peers[by - 1]).wait_recv()
    chunk = 512
    joined = jnp.concatenate([heads[index] for index in range(NZ)], axis=1)
    depth = joined.shape[1]

    @pl.loop(0, width // chunk)
    def _(step):
        at = pl.ds(pl.multiple_of(step * chunk, chunk), chunk)
        partial[:, at] = jnp.dot(
            joined,
            wide_ref[:, :, at].reshape(depth, chunk),
            preferred_element_type=F32,
        )

    def half_rows(plane):
        return pl.ds(pl.multiple_of(plane * own, own), own)

    out_send[...] = partial[half_rows(1 - x_hi), :].astype(BF16)
    swap = remote(out_send, out_recv, o_send, o_recv, partner)
    sent.start(swap)
    mine = partial[half_rows(x_hi), :] + my_tokens_ref[...].astype(F32)
    swap.wait_recv()
    mixed = (mine + out_recv[...].astype(F32)).astype(BF16)
    blocks[z * 2 + x_hi] = (rms(mixed.astype(F32)) * gain_ref[...]).astype(BF16)

    mix_gather(blocks, lambda zz, plane: zz * 2 + plane, own // 2, gather_sems)
    loads[0].wait()
    loads[1].wait()
    group = 8

    @pl.loop(0, 2 * NZ // group)
    def _(step):
        value = blocks[pl.ds(step * group, group)].reshape(group * own, width)
        gate = jnp.dot(value, w_gate[...], preferred_element_type=F32)
        up = jnp.dot(value, w_up[...], preferred_element_type=F32)
        found = (gate * jax.nn.sigmoid(gate) * up).astype(BF16)
        hidden[pl.ds(step * (group // 2), group // 2)] = found.reshape(group // 2, pair, -1)

    loads[2].wait()

    def make(zs):
        value = jnp.concatenate([hidden[zz] for zz in zs], axis=0)

        @pl.loop(0, width // chunk)
        def _(step):
            at = pl.ds(pl.multiple_of(step * chunk, chunk), chunk)
            out = jnp.dot(value, w_down[:, at], preferred_element_type=F32).astype(BF16)
            for index, zz in enumerate(zs):
                for plane in range(2):
                    first = index * pair + plane * own
                    parts[zz * 2 + plane, :, at] = out[first : first + own]

    first, second, more = mix_scatter(parts, make, scatter)
    teacher = mixed.astype(F32) + jnp.concatenate([first, second], axis=0)
    teacher = teacher.astype(BF16)
    teacher_ref[...] = teacher
    loads[3].wait()
    target = jnp.dot(teacher, projector[...], preferred_element_type=F32)
    difference = student_ref[...].astype(F32) + student_sum_ref[...] - target
    scaled_ref[...] = (difference * total_rows ** (-0.5)).astype(BF16)
    sent.finish()
    more.finish()


def student_body(
    scaled_ref,
    teacher_ref,
    normed_t_ref,
    hidden_t_ref,
    gate_ref,
    up_ref,
    s_down_ref,
    columns_ref,
    sums_ref,
    error_ref,
    gathered,
    parts,
    inbox,
    send_sem,
    recv_sem,
    x_send,
    x_recv,
    t_send,
    t_recv,
    send1,
    recv1,
    send2,
    recv2,
):
    dp, tensor, x_hi, z = places()
    size = 2 * NZ
    row = z * 2 + x_hi
    own = scaled_ref.shape[0]
    partner = (dp, (1 - x_hi) * NZ + z)
    nexts = tuple((dp, x_hi * NZ + turn(z, by, NZ)) for by in (1, -1))
    t_peers = [turn(tensor, by, size) for by in range(1, size)]
    d_peers = [turn(dp, by, size) for by in range(1, size)]
    gathered[row] = scaled_ref[...]
    greet([(dp, peer) for peer in t_peers] + [(peer, tensor) for peer in d_peers])
    sent = Sent()

    def view(zz, half):
        return gathered.at[zz * 2 + (x_hi if half == 0 else 1 - x_hi)]

    def ring(way, far, half, hops):
        block = view(turn(z, -towards(way, hops), NZ), half)
        sems = send_sem.at[way, far - 1, half], recv_sem.at[way, far - 1, half]
        return remote(block, block, *sems, nexts[way])

    sent.start(remote(view(z, 0), view(z, 0), x_send, x_recv, partner))
    for way in range(2):
        sent.start(ring(way, 1, 0, 0))
    remote(view(z, 1), view(z, 1), x_send, x_recv, partner).wait_recv()
    for way in range(2):
        sent.start(ring(way, 1, 1, 0))
    for by, peer in enumerate(t_peers):
        sent.start(
            remote(
                teacher_ref.at[:, pl.ds(pl.multiple_of(peer * HD, HD), HD)],
                columns_ref.at[row],
                t_send.at[by],
                t_recv.at[by],
                (dp, peer),
            )
        )
    columns_ref[row] = teacher_ref[:, pl.ds(pl.multiple_of(tensor * HD, HD), HD)]
    for far in range(2, 5):
        for half in range(2):
            for way in range(2):
                ring(way, far - 1, half, far - 1).wait_recv()
                if far < 4 or half == way:
                    sent.start(ring(way, far, half, far - 1))
    for way in range(2):
        ring(way, 4, way, 4).wait_recv()
    scaled = gathered[...].reshape(size * own, -1)
    gate, up = gate_ref[...], up_ref[...]
    sigmoid = jax.nn.sigmoid(gate)
    grad_hidden = lax.dot_general(
        scaled, s_down_ref[...], (((1,), (1,)), ((), ())), preferred_element_type=F32
    )
    grad_up = (grad_hidden * gate * sigmoid).astype(BF16)
    grad_gate = (grad_hidden * up * sigmoid * (1.0 + gate * (1.0 - sigmoid))).astype(BF16)
    both = jnp.concatenate([grad_gate, grad_up], axis=1)
    both = jnp.dot(normed_t_ref[...], both, preferred_element_type=F32).astype(BF16)
    down = jnp.dot(hidden_t_ref[...], scaled, preferred_element_type=F32).astype(BF16)
    units = gate.shape[1]
    parts[:, :own] = both[:, :units].reshape(size, own, units)
    parts[:, own : 2 * own] = both[:, units:].reshape(size, own, units)
    down = jnp.concatenate([down[:, at : at + HD] for at in range(0, down.shape[1], HD)], axis=0)
    parts[:, 2 * own : 3 * own] = down.reshape(size, own, HD)
    squares = scaled.astype(F32)
    squares = jnp.sum((squares * squares).reshape(-1, 8, scaled.shape[1]), axis=0)
    squares = sum(squares[:, at : at + HD] for at in range(0, scaled.shape[1], HD))
    high = squares.astype(BF16)
    low = (squares - high.astype(F32)).astype(BF16)
    both = jnp.concatenate([high, low], axis=0)
    parts[:, 3 * own :] = jnp.broadcast_to(both[None], (size,) + both.shape)

    def origin(by):
        return turn(dp, -(by + 1), size)

    inbox[dp] = parts[dp]
    for by, peer in enumerate(d_peers):
        sent.start(
            remote(parts.at[peer], inbox.at[dp], send1.at[by], recv1.at[by], (peer, tensor))
        )
    for by, peer in enumerate(d_peers):
        block = inbox.at[origin(by)]
        remote(block, block, send1.at[by], recv1.at[by], (peer, tensor)).wait_recv()
    total = inbox[0].astype(F32)
    for index in range(1, size):
        total = total + inbox[index].astype(F32)
    sums_ref[dp] = total[: 3 * own].astype(BF16)
    error_ref[...] = total[3 * own : 3 * own + 8] + total[3 * own + 8 :]
    for by, peer in enumerate(d_peers):
        block = sums_ref.at[dp]
        sent.start(remote(block, block, send2.at[by], recv2.at[by], (peer, tensor)))
    for by, peer in enumerate(t_peers):
        source = turn(tensor, -(by + 1), size)
        block = columns_ref.at[lax.rem(source, NZ) * 2 + source // NZ]
        remote(block, block, t_send.at[by], t_recv.at[by], (dp, peer)).wait_recv()
    for by, peer in enumerate(d_peers):
        block = sums_ref.at[origin(by)]
        remote(block, block, send2.at[by], recv2.at[by], (peer, tensor)).wait_recv()
    sent.finish()


def finish_body(columns_ref, sums_ref, squares_ref, teacher_ref, gate_ref, up_ref, down_ref, error_ref):
    rows, width = teacher_ref.shape
    own = rows // (2 * NZ)
    teacher_ref[...] = columns_ref[...].reshape(rows, width)
    sums = sums_ref[...].astype(F32)
    gate_ref[...] = sums[:, :own].reshape(-1, width)
    up_ref[...] = sums[:, own : 2 * own].reshape(-1, width)
    down = sums[:, 2 * own :].reshape(-1, width)
    for index in range(down.shape[0] // width):
        lanes = slice(index * width, (index + 1) * width)
        down_ref[:, lanes] = down[lanes]
    total = jnp.sum(jnp.sum(squares_ref[...], axis=0, keepdims=True), axis=1, keepdims=True)
    error_ref[...] = total / down_ref.shape[1]


def finish(columns, sums, squares):
    own, units = columns.shape[1:]
    rows = 2 * NZ * own
    shapes = (
        ((rows, units), BF16),
        ((rows, units), F32),
        ((rows, units), F32),
        ((units, rows), F32),
        ((1, 1), F32),
    )
    return pl.pallas_call(
        finish_body,
        out_shape=tuple(jax.ShapeDtypeStruct(shape, kind) for shape, kind in shapes),
        in_specs=[VM] * 3,
        out_specs=(VM,) * 5,
        compiler_params=pltpu.CompilerParams(vmem_limit_bytes=LIMIT),
        name="finish",
    )(columns, sums, squares)


def frequencies(head_dim):
    indices = jnp.arange(head_dim // 2).astype(F32)
    return jnp.exp(-jnp.log(500000.0) * 2.0 * indices / head_dim)


def local(
    tokens,
    series_ids,
    offsets,
    norm_gain,
    mlp_gain,
    w_query,
    w_key,
    w_value,
    w_out,
    w_gate,
    w_up,
    w_down,
    projector,
    student_in,
    s_gate,
    s_up,
    s_down,
):
    rows = tokens.shape[0]
    size = 2 * NZ
    own = rows // size
    width = projector.shape[0]
    narrow = student_in.shape[1]
    units = s_gate.shape[1]
    ff = w_gate.shape[1]
    dp, tensor, x_hi, z = places()
    my_rows = (z * 2 + x_hi) * own

    angles = offsets.astype(F32)[:, None] * frequencies(HD)[None, :]
    cosine, sine = jnp.cos(angles), jnp.sin(angles)
    cosine = jnp.concatenate([cosine, cosine], axis=1)
    sine = jnp.concatenate([-sine, sine], axis=1)
    series = jnp.arange(8, dtype=jnp.int32)
    begins = jnp.sum((series_ids[None, :] < series[:, None]).astype(jnp.int32), axis=1)
    begins = jnp.concatenate([begins, dp[None].astype(jnp.int32)])
    my_student = lax.dynamic_slice_in_dim(student_in, my_rows, own, 0)

    query, pair, my_tokens, part, normed_t, hidden_t, gate, up = call(
        project_body,
        "project",
        1,
        (
            tokens,
            norm_gain[None],
            cosine,
            sine,
            w_query,
            w_key,
            w_value,
            student_in,
            s_gate,
            s_up,
            s_down,
        ),
        (
            ((rows, HD), BF16),
            ((2, rows, HD), BF16),
            ((own, width), BF16),
            ((2, NZ, own, narrow), BF16),
            ((narrow, rows), BF16),
            ((units, rows), BF16),
            ((rows, units), F32),
            ((rows, units), F32),
        ),
        [
            pltpu.VMEM((size, rows, HD), BF16),
            pltpu.VMEM((rows, width), BF16),
            pltpu.VMEM((width, 3 * HD), BF16),
            *RING_SEMS,
        ],
    )
    pairs, wide, student_sum = call(
        exchange_body,
        "exchange",
        2,
        (pair, w_out, part),
        (
            ((4 * NY, 2, rows, HD), BF16),
            ((NZ,) + w_out.shape, BF16),
            ((own, narrow), F32),
        ),
        [
            pltpu.VMEM((NZ, own, narrow), BF16),
            pltpu.VMEM((NZ, own, narrow), BF16),
            pltpu.VMEM((NZ - 1, own, narrow), BF16),
            pltpu.SemaphoreType.DMA,
            pltpu.SemaphoreType.DMA,
            dma(2, 2, 2),
            dma(2, 2, 2),
            dma(8),
            dma(8),
            dma(2, 4, 2),
            dma(2, 4, 2),
            dma(7),
            dma(7),
            pltpu.SemaphoreType.DMA,
            pltpu.SemaphoreType.DMA,
            dma(7),
            dma(7),
        ],
    )
    attended = attention(begins, query, pairs)
    teacher, scaled = call(
        functools.partial(layer_body, rows * lax.axis_size("dp")),
        "layer",
        3,
        (
            attended,
            wide,
            my_tokens,
            mlp_gain[None],
            w_gate,
            w_up,
            w_down,
            projector,
            my_student,
            student_sum,
        ),
        (((own, width), BF16), ((own, narrow), BF16)),
        [
            pltpu.VMEM(w_gate.shape, BF16),
            pltpu.VMEM(w_up.shape, BF16),
            pltpu.VMEM(w_down.shape, BF16),
            pltpu.VMEM(projector.shape, BF16),
            dma(4),
            pltpu.VMEM((NZ, 2 * own, HD), BF16),
            dma(7),
            dma(7),
            pltpu.VMEM((own, width), BF16),
            pltpu.VMEM((own, width), BF16),
            pltpu.SemaphoreType.DMA,
            pltpu.SemaphoreType.DMA,
            pltpu.VMEM((2 * own, width), F32),
            pltpu.VMEM((size, own, width), BF16),
            pltpu.VMEM((NZ, 2 * own, ff), BF16),
            pltpu.VMEM((size, own, width), BF16),
            *RING_SEMS,
            *scatter_scratch(own // 2, width),
        ],
        [VM] * 4 + [pl.BlockSpec(memory_space=pl.ANY)] * 4 + [VM] * 2,
    )
    columns, sums, squares = call(
        student_body,
        "student",
        4,
        (scaled, teacher, normed_t, hidden_t, gate, up, s_down),
        (
            ((size, own, HD), BF16),
            ((size, 3 * own, units), BF16),
            ((8, HD), F32),
        ),
        [
            pltpu.VMEM((size, own, narrow), BF16),
            pltpu.VMEM((size, 3 * own + 16, units), BF16),
            pltpu.VMEM((size, 3 * own + 16, units), BF16),
            dma(2, 4, 2),
            dma(2, 4, 2),
            pltpu.SemaphoreType.DMA,
            pltpu.SemaphoreType.DMA,
            dma(size - 1),
            dma(size - 1),
            dma(size - 1),
            dma(size - 1),
            dma(size - 1),
            dma(size - 1),
        ],
    )
    teacher_out, grad_gate, grad_up, grad_down, error = finish(columns, sums, squares)
    return (teacher_out, grad_gate, grad_up, grad_down, error.reshape(()))


def solution(mesh):
    in_specs = (
        P("dp", "tensor"),
        P(),
        P("dp"),
        P(),
        P(),
        P(None, "tensor"),
        P(None, "tensor"),
        P(None, "tensor"),
        P("tensor", None),
        P(None, "tensor"),
        P(None, "tensor"),
        P("tensor", None),
        P(),
        P("dp", None),
        P(None, "tensor"),
        P(None, "tensor"),
        P("tensor", None),
    )
    out_specs = (P("dp", "tensor"), P(None, "tensor"), P(None, "tensor"), P("tensor", None), P())
    return jax.shard_map(local, mesh=mesh, in_specs=in_specs, out_specs=out_specs, check_vma=False)
```

```python
import functools

import jax
import jax.numpy as jnp
from jax import lax
from jax.experimental import pallas as pl
from jax.experimental.pallas import tpu as pltpu
from jax.sharding import PartitionSpec as P

HD = 128
NZ = 8
NY = 4
MESH = pl.DeviceIdType.MESH
VM = pl.BlockSpec(memory_space=pltpu.VMEM)
SM = pl.BlockSpec(memory_space=pltpu.SMEM)
LIMIT = 56 * 1024 * 1024
F32 = jnp.float32
BF16 = jnp.bfloat16


def params(collective_id):
    return pltpu.CompilerParams(
        collective_id=collective_id, has_side_effects=True, vmem_limit_bytes=LIMIT
    )


def remote(src, dst, send_sem, recv_sem, device):
    return pltpu.make_async_remote_copy(
        src_ref=src,
        dst_ref=dst,
        send_sem=send_sem,
        recv_sem=recv_sem,
        device_id=device,
        device_id_type=MESH,
    )


def greet(devices, meanwhile=None):
    barrier = pltpu.get_barrier_semaphore()
    for device in devices:
        pl.semaphore_signal(barrier, inc=1, device_id=device, device_id_type=MESH)
    if meanwhile is not None:
        meanwhile()
    pl.semaphore_wait(barrier, len(devices))


def places():
    dp, tensor = lax.axis_index("dp"), lax.axis_index("tensor")
    x_hi, z = tensor // NZ, lax.rem(tensor, NZ)
    return dp, tensor, x_hi, z


def turn(z, by, size):
    return lax.rem(z + by + size, size)


def dma(*shape):
    return pltpu.SemaphoreType.DMA(shape)


def call(body, name, collective_id, inputs, outputs, scratch, specs=None):
    return pl.pallas_call(
        body,
        out_shape=tuple(jax.ShapeDtypeStruct(shape, kind) for shape, kind in outputs),
        in_specs=specs or [VM] * len(inputs),
        out_specs=tuple([VM] * len(outputs)),
        scratch_shapes=scratch,
        compiler_params=params(collective_id),
        name=name,
    )(*inputs)


class Sent:
    def __init__(self):
        self.copies = []

    def start(self, copy):
        copy.start()
        self.copies.append(copy)

    def finish(self):
        for copy in self.copies:
            copy.wait_send()


def on_ring(way, far, sub):
    return far < 4 or (way == 1) == (sub == 1)


def towards(way, by):
    return by if way == 0 else -by


RING_SEMS = [dma(2, 4, 3), dma(2, 4, 3), dma(9), dma(9)]


def mix_gather(ref, at, half, sems, hook=lambda step: None, ready=None):
    ring_send, ring_recv, x_send, x_recv = sems
    dp, tensor, x_hi, z = places()
    partner = (dp, (1 - x_hi) * NZ + z)
    nexts = tuple((dp, x_hi * NZ + turn(z, by, NZ)) for by in (1, -1))
    sent = Sent()

    def view(zz, sub):
        plane = x_hi if sub < 2 else 1 - x_hi
        return ref.at[at(zz, plane), pl.ds((sub % 2) * half, half)]

    def ring(way, far, sub, hops):
        block = view(turn(z, -towards(way, hops), NZ), sub)
        sems = ring_send.at[way, far - 1, sub], ring_recv.at[way, far - 1, sub]
        return remote(block, block, *sems, nexts[way])

    def cross(zz, sub, slot):
        block = view(zz, sub)
        return remote(block, block, x_send.at[slot], x_recv.at[slot], partner)

    def slot(way, far):
        return 1 + far + 3 * way if way == 0 else 4 + far

    def crossed(far):
        if far == 0:
            cross(z, 3, 1).wait_recv()
        for way in range(2):
            if 0 < far < 4 + way:
                cross(turn(z, -towards(way, far), NZ), 3, slot(way, far)).wait_recv()

    sent.start(cross(z, 0, 0))
    for sub in range(2):
        for way in range(2):
            sent.start(ring(way, 1, sub, 0))
    sent.start(cross(z, 1, 1))
    hook(0)
    cross(z, 2, 0).wait_recv()
    for way in range(2):
        sent.start(ring(way, 1, 2, 0))
    for far in range(2, 5):
        hook(far - 1)
        for sub in range(3):
            for way in range(2):
                ring(way, far - 1, sub, far - 1).wait_recv()
                if on_ring(way, far, sub):
                    sent.start(ring(way, far, sub, far - 1))
                if sub == 1:
                    origin = turn(z, -towards(way, far - 1), NZ)
                    sent.start(cross(origin, 1, slot(way, far - 1)))
        if far == 3:
            crossed(0)
            crossed(1)
            if ready:
                ready((0, 1))
        if far == 4:
            crossed(2)
            if ready:
                ready((2,))
    ring(1, 4, 1, 4).wait_recv()
    sent.start(cross(turn(z, 4, NZ), 1, slot(1, 4)))
    for sub in (0, 2):
        ring(0, 4, sub, 4).wait_recv()
    crossed(4)
    crossed(3)
    sent.finish()


def scatter_scratch(half, width):
    return [
        pltpu.VMEM((2, 4, 3, half, width), BF16),
        pltpu.VMEM((2, 4, 3, half, width), BF16),
        pltpu.VMEM((8, half, width), BF16),
        pltpu.VMEM((half, width), BF16),
        pltpu.VMEM((half, width), BF16),
        dma(2, 4, 3),
        dma(2, 4, 3),
        dma(9),
        dma(9),
    ]


def mix_scatter(part, make, scratch):
    sbuf, rbuf, xbuf, xlast, xgot, ring_send, ring_recv, x_send, x_recv = scratch
    half = sbuf.shape[3]
    dp, tensor, x_hi, z = places()
    partner = (dp, (1 - x_hi) * NZ + z)
    nexts = tuple((dp, x_hi * NZ + turn(z, by, NZ)) for by in (1, -1))
    sent = Sent()

    def view(zz, sub):
        plane = x_hi if sub < 2 else 1 - x_hi
        return part.at[zz * 2 + plane, pl.ds((sub % 2) * half, half)]

    def slot(way, far):
        return 7 if far == 4 else 1 + 3 * way + far - 1

    def cross(zz, at):
        return remote(view(zz, 3), xbuf.at[at], x_send.at[at], x_recv.at[at], partner)

    def ring(way, far, sub, source):
        sems = ring_send.at[way, far - 1, sub], ring_recv.at[way, far - 1, sub]
        return remote(source, rbuf.at[way, far - 1, sub], *sems, nexts[way])

    def arrived(way, far, sub):
        ring(way, far, sub, rbuf.at[way, far - 1, sub]).wait_recv()
        return rbuf[way, far - 1, sub].astype(F32)

    def crossed(at):
        cross(z, at).wait_recv()
        return xbuf[at].astype(F32)

    def send(way, far, sub):
        source = view(turn(z, towards(way, far), NZ), sub)
        extra = []
        if far < 4 and on_ring(way, far + 1, sub):
            extra.append(arrived(way, far + 1, sub))
        if sub == 1:
            extra.append(crossed(slot(way, far)))
        if extra:
            total = source[...].astype(F32)
            for one in extra:
                total = total + one
            sbuf[way, far - 1, sub] = total.astype(BF16)
            source = sbuf.at[way, far - 1, sub]
        sent.start(ring(way, far, sub, source))

    far4 = turn(z, 4, NZ)
    make([far4])
    sent.start(cross(far4, 7))
    for sub in (0, 2):
        send(0, 4, sub)
    for far in (3, 2, 1):
        places_now = [turn(z, by, NZ) for by in (far, -far)]
        make(places_now)
        for way in range(2):
            sent.start(cross(places_now[way], slot(way, far)))
        if far == 3:
            for sub in (0, 2):
                send(1, 3, sub)
            send(1, 4, 1)
        for sub in (2, 0, 1):
            for way in range(2):
                if not (far == 3 and way == 1 and sub != 1):
                    send(way, far, sub)
    make([z])
    sent.start(cross(z, 0))

    def total(sub):
        return view(z, sub)[...].astype(F32) + arrived(0, 1, sub) + arrived(1, 1, sub)

    xlast[...] = total(2).astype(BF16)
    last = remote(xlast, xgot, x_send.at[8], x_recv.at[8], partner)
    sent.start(last)
    second = total(1) + crossed(0)
    first = total(0)
    last.wait_recv()
    first = first + xgot[...].astype(F32)
    return first, second, sent


def rms(values):
    return values * lax.rsqrt(jnp.mean(values * values, axis=-1, keepdims=True) + 1e-05)


def project_body(
    tokens_ref,
    gain_ref,
    cos_ref,
    sin_ref,
    wq_ref,
    wk_ref,
    wv_ref,
    student_ref,
    s_gate_ref,
    s_up_ref,
    s_down_ref,
    query_ref,
    pair_ref,
    my_tokens_ref,
    part_ref,
    normed_t_ref,
    hidden_t_ref,
    gate_ref,
    up_ref,
    blocks,
    normed,
    weights,
    *sems,
):
    dp, tensor, x_hi, z = places()
    rows = tokens_ref.shape[0]
    own = rows // (2 * NZ)
    blocks[tensor] = tokens_ref[...]
    greet(
        [
            (dp, (1 - x_hi) * NZ + z),
            (dp, x_hi * NZ + turn(z, 1, NZ)),
            (dp, x_hi * NZ + turn(z, -1, NZ)),
        ]
    )

    def student(step):
        at = pl.ds(step * 128, 128)
        values = rms(student_ref[at, :].astype(F32))
        normed_t_ref[:, at] = values.T.astype(BF16)
        values = values.astype(BF16)
        gate = jnp.dot(values, s_gate_ref[...], preferred_element_type=F32)
        up = jnp.dot(values, s_up_ref[...], preferred_element_type=F32)
        sigmoid = jax.nn.sigmoid(gate)
        gate_ref[at, :] = up * sigmoid * (1.0 + gate * (1.0 - sigmoid))
        up_ref[at, :] = gate * sigmoid
        hidden = gate * sigmoid * up
        hidden_t_ref[:, at] = hidden.T.astype(BF16)
        out = jnp.dot(hidden.astype(BF16), s_down_ref[...], preferred_element_type=F32)
        for index in range(128 // own):
            block = out[index * own : (index + 1) * own].astype(BF16)
            part_ref[index % 2, step * (64 // own) + index // 2] = block

    def hook(step):
        if step == 0:
            weights[:, :HD] = wq_ref[...]
            weights[:, HD : 2 * HD] = wk_ref[...]
            weights[:, 2 * HD :] = wv_ref[...]
        student(step)

    mix_gather(blocks, lambda zz, plane: plane * NZ + zz, rows // 2, sems, hook)
    my_rows = pl.multiple_of((z * 2 + x_hi) * own, own)
    for index in range(2 * NZ):
        my_tokens_ref[:, index * HD : (index + 1) * HD] = blocks[index, pl.ds(my_rows, own)]
    tile = 128

    @pl.loop(0, rows // tile)
    def _(step):
        at = pl.ds(pl.multiple_of(step * tile, tile), tile)
        square = jnp.zeros((tile, HD), F32)
        for index in range(2 * NZ):
            value = blocks[index, at].astype(F32)
            square = square + value * value
        mean = jnp.sum(square, axis=1, keepdims=True) / (2 * NZ * HD)
        scale = lax.rsqrt(mean + 1e-05)
        for index in range(2 * NZ):
            lanes = slice(index * HD, (index + 1) * HD)
            value = blocks[index, at].astype(F32) * scale * gain_ref[:, lanes]
            normed[at, lanes] = value.astype(BF16)

    tile = 256

    @pl.loop(0, rows // tile)
    def _(step):
        at = pl.ds(pl.multiple_of(step * tile, tile), tile)
        out = jnp.dot(normed[at, :], weights[...], preferred_element_type=F32)
        cosine, sine = cos_ref[at, :], sin_ref[at, :]

        def rotary(values):
            return (values * cosine + pltpu.roll(values, HD // 2, 1) * sine).astype(BF16)

        query_ref[at, :] = rotary(out[:, :HD])
        pair_ref[0, at, :] = rotary(out[:, HD : 2 * HD])
        pair_ref[1, at, :] = out[:, 2 * HD :].astype(BF16)


def starts_at(begins, position):
    found = jnp.zeros_like(position)
    for begin in begins:
        found = jnp.where(begin <= position, jnp.maximum(found, begin), found)
    return found


R1, R2, R3, X0, X1, H1, H2, H3, OWN = range(9)


class Refs:
    def __init__(self, names, refs):
        for name, ref in zip(names, refs, strict=True):
            setattr(self, name, ref)


def attend(r, mine, j, diagonal, tile=256):
    rows, span = r.query.shape[0], r.pairs.shape[2]
    factor = HD ** (-0.5) * 1.4426950408889634
    key, value = r.pairs[j, 0], r.pairs[j, 1]
    for index in range(rows // tile):
        at = slice(index * tile, (index + 1) * tile)
        scores = lax.dot_general(
            r.query[at, :], key, (((1,), (1,)), ((), ())), preferred_element_type=F32
        )
        column = lax.broadcasted_iota(jnp.int32, (tile, span), 1)
        allowed = column >= r.start[at, :1] - j * span
        if diagonal:
            row = index * tile + lax.broadcasted_iota(jnp.int32, (tile, span), 0)
            allowed = allowed & (column <= row)
        scores = jnp.where(allowed, scores, -1e30)
        top = jnp.max(scores, axis=1, keepdims=True)
        if not diagonal:
            old = r.peak[at, :1]
            top = jnp.maximum(old, top)
        weights = jnp.exp2((scores - top) * factor)
        denom = jnp.sum(weights, axis=1, keepdims=True)
        accum = jnp.dot(weights.astype(BF16), value, preferred_element_type=F32)
        if not diagonal:
            scale = jnp.exp2((old - top) * factor)
            denom = denom + r.denom[at, :1] * scale
            accum = accum + r.accum[at, :] * scale
        r.peak[at, :] = jnp.broadcast_to(top, (tile, HD))
        r.denom[at, :] = jnp.broadcast_to(denom, (tile, HD))
        r.accum[at, :] = accum


def exchange(r, sent):
    dp, tensor, x_hi, z = places()
    x_lo, y, core = dp // (2 * NY), lax.rem(dp // 2, NY), lax.rem(dp, 2)

    def index(xx, yy, cc):
        return xx * 2 * NY + yy * 2 + cc

    k_partner = (index(1 - x_lo, y, core), tensor)
    sibling = (index(x_lo, y, 1 - core), tensor)
    up, down = ((index(x_lo, turn(y, by, NY), core), tensor) for by in (1, -1))
    z_peers = [(dp, x_hi * NZ + turn(z, by, NZ)) for by in range(1, NZ)]
    z_nexts = (z_peers[0], z_peers[-1])
    s_partner = (dp, (1 - x_hi) * NZ + z)
    deep = r.w_out.shape[0] // 4
    first, second = x_lo == 0, x_lo == 1

    def chip(by):
        return turn(y, by, NY)

    arrives = {
        R1: (y >= 1, x_lo, chip(-1)),
        R2: (y >= 2, x_lo, chip(-2)),
        R3: (y == 3, x_lo, chip(1)),
        X0: (second, 0, y),
        X1: (second & (y >= 1), 0, chip(-1)),
        H1: (second & (y <= 2), 0, chip(1)),
        H2: (second & (y <= 1), 0, chip(2)),
        H3: (second & (y == 0), 0, chip(-1)),
        OWN: (None, x_lo, y),
    }

    def k_copy(event, part, xx, yy, device):
        block = r.pairs.at[index(xx, yy, core), part]
        return remote(block, block, r.k_send.at[event, part], r.k_recv.at[event, part], device)

    later = []

    def when(condition, copy):
        @pl.when(condition)
        def _():
            copy.start()

        later.append((condition, copy))

    def k_wait(event, part):
        condition, xx, yy = arrives[event]

        @pl.when(condition)
        def _():
            k_copy(event, part, xx, yy, up).wait_recv()

    def c_copy(event, cc):
        _, xx, yy = arrives[event]
        block = r.pairs.at[index(xx, yy, cc)]
        return remote(block, block, r.c_send.at[event], r.c_recv.at[event], sibling)

    def share(event):
        condition = arrives[event][0]
        if condition is None:
            sent.start(c_copy(event, core))
        else:
            when(condition, c_copy(event, core))

    def shared(*events):
        for event in events:
            condition = arrives[event][0]
            if condition is None:
                c_copy(event, 1 - core).wait_recv()
            else:

                @pl.when(condition)
                def _(event=event):
                    c_copy(event, 1 - core).wait_recv()

    def work(*events):
        found = []
        for event in events:
            condition, xx, yy = arrives[event]
            for cc in (core, 1 - core):
                if event == OWN and cc is core:
                    continue
                j = index(xx, yy, cc)
                needed = (j < dp) & (j >= dp - 10)
                found.append((j, needed if condition is None else needed & condition))

        @pl.loop(0, len(found))
        def _(step):
            j, needed = found[0]
            needed = needed.astype(jnp.int32)
            for number, (jj, wanted) in enumerate(found[1:], 1):
                j = jnp.where(step == number, jj, j)
                needed = jnp.where(step == number, wanted.astype(jnp.int32), needed)

            @pl.when(needed == 1)
            def _():
                attend(r, dp, j, False)

    def w_copy(way, far, sub, hops):
        top = pl.multiple_of(core * 2 * deep + sub * deep, deep)
        block = r.wide.at[turn(z, -towards(way, hops), NZ), pl.ds(top, deep)]
        sems = r.w_send.at[way, far - 1, sub], r.w_recv.at[way, far - 1, sub]
        return remote(block, block, *sems, z_nexts[way])

    def w_share(by, slot, cc):
        top = pl.multiple_of(cc * 2 * deep, 2 * deep)
        block = r.wide.at[turn(z, by, NZ), pl.ds(top, 2 * deep)]
        return remote(block, block, r.wc_send.at[slot], r.wc_recv.at[slot], sibling)

    def w_forward(far, sub):
        for way in range(2):
            if far < 4 or sub == way:
                w_copy(way, far, sub, far).wait_recv()
            if far < 3 or (far == 3 and sub == way):
                sent.start(w_copy(way, far + 1, sub, far))

    def w_spread(far):
        for way in range(2):
            sent.start(w_share(towards(way, -far), 2 * (far - 1) + way, core))

    for part in range(2):
        when(y <= 2, k_copy(R1, part, x_lo, y, up))
        when(y == 0, k_copy(R3, part, x_lo, y, down))
        when(first, k_copy(X0, part, 0, y, k_partner))
    share(OWN)
    for sub in range(2):
        for way in range(2):
            sent.start(w_copy(way, 1, sub, 0))
    s_cross = remote(r.part.at[1 - x_hi], r.s_got, r.sx_send, r.sx_recv, s_partner)
    sent.start(s_cross)
    for part in range(2):
        k_wait(R1, part)
        when((y >= 1) & (y <= 2), k_copy(R2, part, x_lo, chip(-1), up))
        when(first & (y >= 1), k_copy(X1, part, 0, chip(-1), k_partner))
        k_wait(X0, part)
        when(second & (y >= 1), k_copy(H1, part, 0, y, down))
        when(second & (y == 3), k_copy(H3, part, 0, y, up))
        w_forward(1, part)
    share(R1)
    share(X0)
    w_spread(1)
    s_cross.wait_recv()
    r.s_out[...] = (r.part[x_hi].astype(F32) + r.s_got[...].astype(F32)).astype(BF16)
    k_wait(R3, 0)
    k_wait(R3, 1)
    share(R3)
    shared(OWN, R1)
    work(OWN, R1)
    w_forward(2, 0)
    for part in range(2):
        k_wait(H1, part)
        when(second & (y >= 1) & (y <= 2), k_copy(H2, part, 0, chip(1), down))
    share(H1)
    w_forward(2, 1)
    w_spread(2)
    shared(X0, R3)
    work(X0, R3)
    for event in (X1, R2, H3):
        k_wait(event, 0)
        k_wait(event, 1)
        share(event)
    w_forward(3, 0)
    shared(H1)
    work(H1)
    w_forward(3, 1)
    w_spread(3)
    k_wait(H2, 0)
    k_wait(H2, 1)
    share(H2)
    shared(X1, R2, H3)
    work(X1, R2, H3)
    w_forward(4, 0)
    w_forward(4, 1)
    sent.start(w_share(4, 6, core))
    shared(H2)
    work(H2)
    r.attended[...] = (r.accum[...] / r.denom[...]).astype(BF16)

    def finish():
        for condition, copy in later:

            @pl.when(condition)
            def _(copy=copy):
                copy.wait_send()

    def wide_whole():
        for slot, by in enumerate([-1, 1, -2, 2, -3, 3, 4]):
            w_share(by, slot, 1 - core).wait_recv()

    return wide_whole, finish


def layer_body(names, total_rows, *refs):
    r = Refs(names, refs)
    dp, tensor, x_hi, z = places()
    size = 2 * NZ
    own, width = r.my_tokens.shape
    pair = 2 * own
    rows = size * own
    row = z * 2 + x_hi
    partner = (dp, (1 - x_hi) * NZ + z)
    z_peers = [(dp, x_hi * NZ + turn(z, by, NZ)) for by in range(1, NZ)]
    t_peers = [turn(tensor, by, size) for by in range(1, size)]
    d_peers = [turn(dp, by, size) for by in range(1, size)]
    loads = []
    for index, name in enumerate(("w_gate", "w_up", "w_down", "projector")):
        far, near = getattr(r, name + "_hbm"), getattr(r, name)
        loads.append(pltpu.make_async_copy(far, near, r.load_sem.at[index]))
        loads[-1].start()
    r.pairs[dp] = r.pair[...]
    r.wide[z] = r.w_out[...]

    def diagonal():
        position = dp * rows + lax.broadcasted_iota(jnp.int32, (rows, HD), 0)
        r.start[...] = starts_at([r.begin[at] for at in range(8)], position)
        attend(r, dp, dp, True)

    greet([(dp, peer) for peer in t_peers] + [(peer, tensor) for peer in d_peers], diagonal)
    sent = Sent()
    wide_whole, finish_exchange = exchange(r, sent)

    def rows_of(zz):
        return pl.ds(pl.multiple_of(zz * pair, pair), pair)

    for by in range(1, NZ):
        sent.start(
            remote(
                r.attended.at[rows_of(turn(z, by, NZ))],
                r.heads.at[z],
                r.a_send.at[by - 1],
                r.a_recv.at[by - 1],
                z_peers[by - 1],
            )
        )
    for by in range(1, NZ):
        sent.start(
            remote(
                r.s_out.at[turn(z, by, NZ)],
                r.s_in.at[by - 1],
                r.sz_send.at[by - 1],
                r.sz_recv.at[by - 1],
                z_peers[by - 1],
            )
        )
    r.heads[z] = r.attended[rows_of(z), :]
    wide_whole()
    for by in range(1, NZ):
        block = r.heads.at[turn(z, -by, NZ)]
        remote(block, block, r.a_send.at[by - 1], r.a_recv.at[by - 1], z_peers[by - 1]).wait_recv()
    chunk = 512
    joined = jnp.concatenate([r.heads[index] for index in range(NZ)], axis=1)
    depth = joined.shape[1]

    @pl.loop(0, width // chunk)
    def _(step):
        at = pl.ds(pl.multiple_of(step * chunk, chunk), chunk)
        r.partial[:, at] = jnp.dot(
            joined, r.wide[:, :, at].reshape(depth, chunk), preferred_element_type=F32
        )

    def half_rows(plane):
        return pl.ds(pl.multiple_of(plane * own, own), own)

    r.out_send[...] = r.partial[half_rows(1 - x_hi), :].astype(BF16)
    swap = remote(r.out_send, r.out_recv, r.o_send, r.o_recv, partner)
    sent.start(swap)
    mine = r.partial[half_rows(x_hi), :] + r.my_tokens[...].astype(F32)
    swap.wait_recv()
    mixed = (mine + r.out_recv[...].astype(F32)).astype(BF16)
    r.mixed[...] = mixed
    r.blocks[row] = (rms(mixed.astype(F32)) * r.mlp_gain[...]).astype(BF16)

    waited = []

    def units(zs):
        if not waited:
            loads[0].wait()
            loads[1].wait()
            waited.append(True)
        value = jnp.concatenate(
            [r.blocks[pl.ds(zz * 2, 2)].reshape(pair, width) for zz in zs], axis=0
        )
        gate = jnp.dot(value, r.w_gate[...], preferred_element_type=F32)
        up = jnp.dot(value, r.w_up[...], preferred_element_type=F32)
        found = (gate * jax.nn.sigmoid(gate) * up).astype(BF16)
        for at, zz in enumerate(zs):
            r.hidden[zz] = found[at * pair : (at + 1) * pair]

    def ready(distances):
        zs = []
        for by in distances:
            zs += [z] if by == 0 else [turn(z, by, NZ), turn(z, -by, NZ)]
        units(zs)

    mix_gather(
        r.blocks,
        lambda zz, plane: zz * 2 + plane,
        own // 2,
        (r.g_send, r.g_recv, r.gx_send, r.gx_recv),
        ready=ready,
    )
    student_sum = r.s_out[z].astype(F32)
    for by in range(1, NZ):
        got = r.s_in.at[by - 1]
        remote(got, got, r.sz_send.at[by - 1], r.sz_recv.at[by - 1], z_peers[by - 1]).wait_recv()
        student_sum = student_sum + r.s_in[by - 1].astype(F32)
    r.predicted[...] = r.student[...].astype(F32) + student_sum
    loads[2].wait()
    fresh = [2]

    def make(zs):
        if fresh:
            fresh.pop() if len(zs) == 2 else None
            units(zs)
        value = jnp.concatenate([r.hidden[zz] for zz in zs], axis=0)

        @pl.loop(0, width // chunk)
        def _(step):
            at = pl.ds(pl.multiple_of(step * chunk, chunk), chunk)
            out = jnp.dot(value, r.w_down[:, at], preferred_element_type=F32).astype(BF16)
            for index, zz in enumerate(zs):
                for plane in range(2):
                    top = index * pair + plane * own
                    r.parts[zz * 2 + plane, :, at] = out[top : top + own]

    scratch = (r.sbuf, r.rbuf, r.xbuf, r.xlast, r.xgot, r.r_send, r.r_recv, r.rx_send, r.rx_recv)
    top, bottom, more = mix_scatter(r.parts, make, scratch)
    teacher = r.mixed[...].astype(F32) + jnp.concatenate([top, bottom], axis=0)
    teacher = teacher.astype(BF16)
    r.teacher[...] = teacher
    loads[3].wait()
    target = jnp.dot(teacher, r.projector[...], preferred_element_type=F32)
    scaled = ((r.predicted[...] - target) * total_rows ** (-0.5)).astype(BF16)

    def place(by, plane):
        return r.gathered.at[turn(z, by, NZ) * 2 + plane]

    def across(by, plane):
        block = place(by, plane)
        at = by % NZ
        return remote(block, block, r.px_send.at[at], r.px_recv.at[at], partner)

    def along(by, device):
        block = place(-by if device is None else 0, x_hi)
        sems = r.p_send.at[by - 1], r.p_recv.at[by - 1]
        return remote(block, block, *sems, z_peers[by - 1])

    r.gathered[row] = scaled
    for by in (4, 3, 5, 2, 6, 1, 7):
        sent.start(along(by, True))
    sent.start(across(0, x_hi))
    for by, peer in enumerate(t_peers):
        sent.start(
            remote(
                r.teacher.at[:, pl.ds(pl.multiple_of(peer * HD, HD), HD)],
                r.columns.at[row],
                r.t_send.at[by],
                r.t_recv.at[by],
                (dp, peer),
            )
        )
    r.columns[row] = r.teacher[:, pl.ds(pl.multiple_of(tensor * HD, HD), HD)]
    for by in (1, 7, 2, 6, 3, 5, 4):
        along(by, None).wait_recv()
        sent.start(across(-by, x_hi))
    for by in (0, 1, 7, 2, 6, 3, 5, 4):
        across(-by, 1 - x_hi).wait_recv()

    scaled = r.gathered[...].reshape(rows, -1)
    grad_hidden = lax.dot_general(
        scaled, r.s_down[...], (((1,), (1,)), ((), ())), preferred_element_type=F32
    )
    both = jnp.concatenate(
        [(grad_hidden * r.by_gate[...]).astype(BF16), (grad_hidden * r.by_up[...]).astype(BF16)],
        axis=1,
    )
    both = jnp.dot(r.normed_t[...], both, preferred_element_type=F32).astype(BF16)
    down = jnp.dot(r.hidden_t[...], scaled, preferred_element_type=F32).astype(BF16)
    count = grad_hidden.shape[1]
    r.grads[:, :own] = both[:, :count].reshape(size, own, count)
    r.grads[:, own:pair] = both[:, count:].reshape(size, own, count)
    down = jnp.concatenate([down[:, at : at + HD] for at in range(0, down.shape[1], HD)], axis=0)
    r.grads[:, pair : 3 * own] = down.reshape(size, own, HD)
    squares = scaled.astype(F32)
    squares = jnp.sum((squares * squares).reshape(-1, 8, scaled.shape[1]), axis=0)
    squares = sum(squares[:, at : at + HD] for at in range(0, scaled.shape[1], HD))
    high = squares.astype(BF16)
    low = (squares - high.astype(F32)).astype(BF16)
    both = jnp.concatenate([high, low], axis=0)
    r.grads[:, 3 * own :] = jnp.broadcast_to(both[None], (size,) + both.shape)

    def origin(by):
        return turn(dp, -(by + 1), size)

    r.inbox[dp] = r.grads[dp]
    for by, peer in enumerate(d_peers):
        sems = r.send1.at[by], r.recv1.at[by]
        sent.start(remote(r.grads.at[peer], r.inbox.at[dp], *sems, (peer, tensor)))
    for by, peer in enumerate(d_peers):
        block = r.inbox.at[origin(by)]
        remote(block, block, r.send1.at[by], r.recv1.at[by], (peer, tensor)).wait_recv()
    total = r.inbox[0].astype(F32)
    for index in range(1, size):
        total = total + r.inbox[index].astype(F32)
    r.sums[dp] = total[: 3 * own].astype(BF16)
    r.error[...] = total[3 * own : 3 * own + 8] + total[3 * own + 8 :]
    for by, peer in enumerate(d_peers):
        block = r.sums.at[dp]
        sent.start(remote(block, block, r.send2.at[by], r.recv2.at[by], (peer, tensor)))
    for by, peer in enumerate(t_peers):
        source = turn(tensor, -(by + 1), size)
        block = r.columns.at[lax.rem(source, NZ) * 2 + source // NZ]
        remote(block, block, r.t_send.at[by], r.t_recv.at[by], (dp, peer)).wait_recv()
    for by, peer in enumerate(d_peers):
        block = r.sums.at[origin(by)]
        remote(block, block, r.send2.at[by], r.recv2.at[by], (peer, tensor)).wait_recv()
    finish_exchange()
    sent.finish()
    more.finish()


def finish_body(columns_ref, sums_ref, squares_ref, teacher_ref, gate_ref, up_ref, down_ref, error_ref):
    rows, width = teacher_ref.shape
    own = rows // (2 * NZ)
    teacher_ref[...] = columns_ref[...].reshape(rows, width)
    sums = sums_ref[...].astype(F32)
    gate_ref[...] = sums[:, :own].reshape(-1, width)
    up_ref[...] = sums[:, own : 2 * own].reshape(-1, width)
    down = sums[:, 2 * own :].reshape(-1, width)
    for index in range(down.shape[0] // width):
        lanes = slice(index * width, (index + 1) * width)
        down_ref[:, lanes] = down[lanes]
    total = jnp.sum(jnp.sum(squares_ref[...], axis=0, keepdims=True), axis=1, keepdims=True)
    error_ref[...] = total / down_ref.shape[1]


def finish(columns, sums, squares):
    own, units = columns.shape[1:]
    rows = 2 * NZ * own
    shapes = (
        ((rows, units), BF16),
        ((rows, units), F32),
        ((rows, units), F32),
        ((units, rows), F32),
        ((1, 1), F32),
    )
    return pl.pallas_call(
        finish_body,
        out_shape=tuple(jax.ShapeDtypeStruct(shape, kind) for shape, kind in shapes),
        in_specs=[VM] * 3,
        out_specs=(VM,) * 5,
        compiler_params=pltpu.CompilerParams(vmem_limit_bytes=LIMIT),
        name="finish",
    )(columns, sums, squares)


def frequencies(head_dim):
    indices = jnp.arange(head_dim // 2).astype(F32)
    return jnp.exp(-jnp.log(500000.0) * 2.0 * indices / head_dim)


def local(
    tokens,
    series_ids,
    offsets,
    norm_gain,
    mlp_gain,
    w_query,
    w_key,
    w_value,
    w_out,
    w_gate,
    w_up,
    w_down,
    projector,
    student_in,
    s_gate,
    s_up,
    s_down,
):
    rows = tokens.shape[0]
    size = 2 * NZ
    own = rows // size
    width = projector.shape[0]
    narrow = student_in.shape[1]
    units = s_gate.shape[1]
    ff = w_gate.shape[1]
    dp, tensor, x_hi, z = places()
    my_rows = (z * 2 + x_hi) * own

    angles = offsets.astype(F32)[:, None] * frequencies(HD)[None, :]
    cosine, sine = jnp.cos(angles), jnp.sin(angles)
    cosine = jnp.concatenate([cosine, cosine], axis=1)
    sine = jnp.concatenate([-sine, sine], axis=1)
    series = jnp.arange(8, dtype=jnp.int32)
    begins = jnp.sum((series_ids[None, :] < series[:, None]).astype(jnp.int32), axis=1)
    begins = jnp.concatenate([begins, dp[None].astype(jnp.int32)])
    my_student = lax.dynamic_slice_in_dim(student_in, my_rows, own, 0)

    query, pair, my_tokens, part, normed_t, hidden_t, by_gate, by_up = call(
        project_body,
        "project",
        1,
        (
            tokens,
            norm_gain[None],
            cosine,
            sine,
            w_query,
            w_key,
            w_value,
            student_in,
            s_gate,
            s_up,
            s_down,
        ),
        (
            ((rows, HD), BF16),
            ((2, rows, HD), BF16),
            ((own, width), BF16),
            ((2, NZ, own, narrow), BF16),
            ((narrow, rows), BF16),
            ((units, rows), BF16),
            ((rows, units), F32),
            ((rows, units), F32),
        ),
        [
            pltpu.VMEM((size, rows, HD), BF16),
            pltpu.VMEM((rows, width), BF16),
            pltpu.VMEM((width, 3 * HD), BF16),
            *RING_SEMS,
        ],
    )
    inputs = {
        "begin": begins,
        "query": query,
        "pair": pair,
        "w_out": w_out,
        "part": part,
        "my_tokens": my_tokens,
        "mlp_gain": mlp_gain[None],
        "w_gate_hbm": w_gate,
        "w_up_hbm": w_up,
        "w_down_hbm": w_down,
        "projector_hbm": projector,
        "student": my_student,
        "normed_t": normed_t,
        "hidden_t": hidden_t,
        "by_gate": by_gate,
        "by_up": by_up,
        "s_down": s_down,
    }
    outputs = {
        "columns": ((size, own, HD), BF16),
        "sums": ((size, 3 * own, units), BF16),
        "error": ((8, HD), F32),
    }
    one = pltpu.SemaphoreType.DMA
    half = own // 2
    scratch = {
        "pairs": pltpu.VMEM((4 * NY, 2, rows, HD), BF16),
        "wide": pltpu.VMEM((NZ,) + w_out.shape, BF16),
        "start": pltpu.VMEM((rows, HD), jnp.int32),
        "peak": pltpu.VMEM((rows, HD), F32),
        "denom": pltpu.VMEM((rows, HD), F32),
        "accum": pltpu.VMEM((rows, HD), F32),
        "attended": pltpu.VMEM((rows, HD), BF16),
        "k_send": dma(9, 2),
        "k_recv": dma(9, 2),
        "c_send": dma(9),
        "c_recv": dma(9),
        "w_send": dma(2, 4, 2),
        "w_recv": dma(2, 4, 2),
        "wc_send": dma(7),
        "wc_recv": dma(7),
        "s_got": pltpu.VMEM((NZ, own, narrow), BF16),
        "s_out": pltpu.VMEM((NZ, own, narrow), BF16),
        "s_in": pltpu.VMEM((NZ - 1, own, narrow), BF16),
        "sx_send": one,
        "sx_recv": one,
        "sz_send": dma(7),
        "sz_recv": dma(7),
        "w_gate": pltpu.VMEM(w_gate.shape, BF16),
        "w_up": pltpu.VMEM(w_up.shape, BF16),
        "w_down": pltpu.VMEM(w_down.shape, BF16),
        "projector": pltpu.VMEM(projector.shape, BF16),
        "load_sem": dma(4),
        "heads": pltpu.VMEM((NZ, 2 * own, HD), BF16),
        "a_send": dma(7),
        "a_recv": dma(7),
        "out_send": pltpu.VMEM((own, width), BF16),
        "out_recv": pltpu.VMEM((own, width), BF16),
        "o_send": one,
        "o_recv": one,
        "partial": pltpu.VMEM((2 * own, width), F32),
        "mixed": pltpu.VMEM((own, width), BF16),
        "blocks": pltpu.VMEM((size, own, width), BF16),
        "hidden": pltpu.VMEM((NZ, 2 * own, ff), BF16),
        "parts": pltpu.VMEM((size, own, width), BF16),
        "predicted": pltpu.VMEM((own, narrow), F32),
        "g_send": dma(2, 4, 3),
        "g_recv": dma(2, 4, 3),
        "gx_send": dma(9),
        "gx_recv": dma(9),
    }
    names = ("sbuf", "rbuf", "xbuf", "xlast", "xgot", "r_send", "r_recv", "rx_send", "rx_recv")
    scratch.update(zip(names, scatter_scratch(half, width), strict=True))
    scratch.update(
        {
            "teacher": pltpu.VMEM((own, width), BF16),
            "gathered": pltpu.VMEM((size, own, narrow), BF16),
            "px_send": dma(8),
            "px_recv": dma(8),
            "p_send": dma(7),
            "p_recv": dma(7),
            "t_send": dma(size - 1),
            "t_recv": dma(size - 1),
            "grads": pltpu.VMEM((size, 3 * own + 16, units), BF16),
            "inbox": pltpu.VMEM((size, 3 * own + 16, units), BF16),
            "send1": dma(size - 1),
            "recv1": dma(size - 1),
            "send2": dma(size - 1),
            "recv2": dma(size - 1),
        }
    )
    specs = {"begin": SM}
    far = pl.BlockSpec(memory_space=pl.ANY)
    columns, sums, squares = call(
        functools.partial(
            layer_body, (*inputs, *outputs, *scratch), rows * lax.axis_size("dp")
        ),
        "layer",
        2,
        tuple(inputs.values()),
        tuple(outputs.values()),
        list(scratch.values()),
        [far if name.endswith("_hbm") else specs.get(name, VM) for name in inputs],
    )
    teacher_out, grad_gate, grad_up, grad_down, error = finish(columns, sums, squares)
    return (teacher_out, grad_gate, grad_up, grad_down, error.reshape(()))


def solution(mesh):
    in_specs = (
        P("dp", "tensor"),
        P(),
        P("dp"),
        P(),
        P(),
        P(None, "tensor"),
        P(None, "tensor"),
        P(None, "tensor"),
        P("tensor", None),
        P(None, "tensor"),
        P(None, "tensor"),
        P("tensor", None),
        P(),
        P("dp", None),
        P(None, "tensor"),
        P(None, "tensor"),
        P("tensor", None),
    )
    out_specs = (P("dp", "tensor"), P(None, "tensor"), P(None, "tensor"), P("tensor", None), P())
    return jax.shard_map(local, mesh=mesh, in_specs=in_specs, out_specs=out_specs, check_vma=False)
```

```python
import functools

import jax
import jax.numpy as jnp
from jax import lax
from jax.experimental import pallas as pl
from jax.experimental.pallas import tpu as pltpu
from jax.sharding import PartitionSpec as P

HD = 128
NZ = 8
NY = 4
MESH = pl.DeviceIdType.MESH
VM = pl.BlockSpec(memory_space=pltpu.VMEM)
LIMIT = 56 * 1024 * 1024
F32 = jnp.float32
BF16 = jnp.bfloat16


def params(collective_id):
    return pltpu.CompilerParams(
        collective_id=collective_id, has_side_effects=True, vmem_limit_bytes=LIMIT
    )


def remote(src, dst, send_sem, recv_sem, device):
    return pltpu.make_async_remote_copy(
        src_ref=src,
        dst_ref=dst,
        send_sem=send_sem,
        recv_sem=recv_sem,
        device_id=device,
        device_id_type=MESH,
    )


def greet(devices, meanwhile=None):
    barrier = pltpu.get_barrier_semaphore()
    for device in devices:
        pl.semaphore_signal(barrier, inc=1, device_id=device, device_id_type=MESH)
    if meanwhile is not None:
        meanwhile()
    pl.semaphore_wait(barrier, len(devices))


def places():
    dp, tensor = lax.axis_index("dp"), lax.axis_index("tensor")
    x_hi, z = tensor // NZ, lax.rem(tensor, NZ)
    return dp, tensor, x_hi, z


def turn(z, by, size):
    return lax.rem(z + by + size, size)


def dma(*shape):
    return pltpu.SemaphoreType.DMA(shape)


def call(body, name, collective_id, inputs, outputs, scratch, specs=None):
    return pl.pallas_call(
        body,
        out_shape=tuple(jax.ShapeDtypeStruct(shape, kind) for shape, kind in outputs),
        in_specs=specs or [VM] * len(inputs),
        out_specs=tuple([VM] * len(outputs)),
        scratch_shapes=scratch,
        compiler_params=params(collective_id),
        name=name,
    )(*inputs)


class Sent:
    def __init__(self):
        self.copies = []

    def start(self, copy):
        copy.start()
        self.copies.append(copy)

    def finish(self):
        for copy in self.copies:
            copy.wait_send()


def on_ring(way, far, sub):
    return far < 4 or (way == 1) == (sub == 1)


def towards(way, by):
    return by if way == 0 else -by


def mix_gather(ref, at, half, sems, hook=lambda step: None, ready=None):
    ring_send, ring_recv, x_send, x_recv = sems
    dp, tensor, x_hi, z = places()
    partner = (dp, (1 - x_hi) * NZ + z)
    nexts = tuple((dp, x_hi * NZ + turn(z, by, NZ)) for by in (1, -1))
    sent = Sent()

    def view(zz, sub):
        plane = x_hi if sub < 2 else 1 - x_hi
        return ref.at[at(zz, plane), pl.ds((sub % 2) * half, half)]

    def ring(way, far, sub, hops):
        block = view(turn(z, -towards(way, hops), NZ), sub)
        sems = ring_send.at[way, far - 1, sub], ring_recv.at[way, far - 1, sub]
        return remote(block, block, *sems, nexts[way])

    def cross(zz, sub, slot):
        block = view(zz, sub)
        return remote(block, block, x_send.at[slot], x_recv.at[slot], partner)

    def slot(way, far):
        return 1 + far + 3 * way if way == 0 else 4 + far

    def crossed(far):
        if far == 0:
            cross(z, 3, 1).wait_recv()
        for way in range(2):
            if 0 < far < 4 + way:
                cross(turn(z, -towards(way, far), NZ), 3, slot(way, far)).wait_recv()

    sent.start(cross(z, 0, 0))
    for sub in range(2):
        for way in range(2):
            sent.start(ring(way, 1, sub, 0))
    sent.start(cross(z, 1, 1))
    hook(0)
    cross(z, 2, 0).wait_recv()
    for way in range(2):
        sent.start(ring(way, 1, 2, 0))
    for far in range(2, 5):
        hook(far - 1)
        for sub in range(3):
            for way in range(2):
                ring(way, far - 1, sub, far - 1).wait_recv()
                if on_ring(way, far, sub):
                    sent.start(ring(way, far, sub, far - 1))
                if sub == 1:
                    origin = turn(z, -towards(way, far - 1), NZ)
                    sent.start(cross(origin, 1, slot(way, far - 1)))
        if far == 3:
            crossed(0)
            crossed(1)
            if ready:
                ready((0, 1))
        if far == 4:
            crossed(2)
            if ready:
                ready((2,))
    ring(1, 4, 1, 4).wait_recv()
    sent.start(cross(turn(z, 4, NZ), 1, slot(1, 4)))
    for sub in (0, 2):
        ring(0, 4, sub, 4).wait_recv()
    crossed(4)
    crossed(3)
    sent.finish()


def scatter_scratch(half, width):
    return [
        pltpu.VMEM((2, 4, 3, half, width), BF16),
        pltpu.VMEM((2, 4, 3, half, width), BF16),
        pltpu.VMEM((8, half, width), BF16),
        pltpu.VMEM((half, width), BF16),
        pltpu.VMEM((half, width), BF16),
        dma(2, 4, 3),
        dma(2, 4, 3),
        dma(9),
        dma(9),
    ]


def mix_scatter(part, make, scratch):
    sbuf, rbuf, xbuf, xlast, xgot, ring_send, ring_recv, x_send, x_recv = scratch
    half = sbuf.shape[3]
    dp, tensor, x_hi, z = places()
    partner = (dp, (1 - x_hi) * NZ + z)
    nexts = tuple((dp, x_hi * NZ + turn(z, by, NZ)) for by in (1, -1))
    sent = Sent()

    def view(zz, sub):
        plane = x_hi if sub < 2 else 1 - x_hi
        return part.at[zz * 2 + plane, pl.ds((sub % 2) * half, half)]

    def slot(way, far):
        return 7 if far == 4 else 1 + 3 * way + far - 1

    def cross(zz, at):
        return remote(view(zz, 3), xbuf.at[at], x_send.at[at], x_recv.at[at], partner)

    def ring(way, far, sub, source):
        sems = ring_send.at[way, far - 1, sub], ring_recv.at[way, far - 1, sub]
        return remote(source, rbuf.at[way, far - 1, sub], *sems, nexts[way])

    def arrived(way, far, sub):
        ring(way, far, sub, rbuf.at[way, far - 1, sub]).wait_recv()
        return rbuf[way, far - 1, sub].astype(F32)

    def crossed(at):
        cross(z, at).wait_recv()
        return xbuf[at].astype(F32)

    def send(way, far, sub):
        source = view(turn(z, towards(way, far), NZ), sub)
        extra = []
        if far < 4 and on_ring(way, far + 1, sub):
            extra.append(arrived(way, far + 1, sub))
        if sub == 1:
            extra.append(crossed(slot(way, far)))
        if extra:
            total = source[...].astype(F32)
            for one in extra:
                total = total + one
            sbuf[way, far - 1, sub] = total.astype(BF16)
            source = sbuf.at[way, far - 1, sub]
        sent.start(ring(way, far, sub, source))

    far4 = turn(z, 4, NZ)
    make([far4])
    sent.start(cross(far4, 7))
    for sub in (0, 2):
        send(0, 4, sub)
    for far in (3, 2, 1):
        places_now = [turn(z, by, NZ) for by in (far, -far)]
        make(places_now)
        for way in range(2):
            sent.start(cross(places_now[way], slot(way, far)))
        if far == 3:
            for sub in (0, 2):
                send(1, 3, sub)
            send(1, 4, 1)
        for sub in (2, 0, 1):
            for way in range(2):
                if not (far == 3 and way == 1 and sub != 1):
                    send(way, far, sub)
    make([z])
    sent.start(cross(z, 0))

    def total(sub):
        return view(z, sub)[...].astype(F32) + arrived(0, 1, sub) + arrived(1, 1, sub)

    xlast[...] = total(2).astype(BF16)
    last = remote(xlast, xgot, x_send.at[8], x_recv.at[8], partner)
    sent.start(last)
    second = total(1) + crossed(0)
    first = total(0)
    last.wait_recv()
    first = first + xgot[...].astype(F32)
    return first, second, sent


def rms(values):
    return values * lax.rsqrt(jnp.mean(values * values, axis=-1, keepdims=True) + 1e-05)


def project(r, after):
    dp, tensor, x_hi, z = places()
    rows = r.tokens.shape[0]
    own = rows // (2 * NZ)

    def student(step):
        at = pl.ds(step * 128, 128)
        values = rms(r.student[at, :].astype(F32))
        r.normed_t[:, at] = values.T.astype(BF16)
        values = values.astype(BF16)
        gate = jnp.dot(values, r.s_gate[...], preferred_element_type=F32)
        up = jnp.dot(values, r.s_up[...], preferred_element_type=F32)
        sigmoid = jax.nn.sigmoid(gate)
        r.by_gate[at, :] = up * sigmoid * (1.0 + gate * (1.0 - sigmoid))
        r.by_up[at, :] = gate * sigmoid
        hidden = gate * sigmoid * up
        r.hidden_t[:, at] = hidden.T.astype(BF16)
        out = jnp.dot(hidden.astype(BF16), r.s_down[...], preferred_element_type=F32)
        for index in range(128 // own):
            block = out[index * own : (index + 1) * own].astype(BF16)
            r.part[index % 2, step * (64 // own) + index // 2] = block

    def hook(step):
        if step == 0:
            r.weights[:, :HD] = r.w_query[...]
            r.weights[:, HD : 2 * HD] = r.w_key[...]
            r.weights[:, 2 * HD :] = r.w_value[...]
        student(step)

    mix_gather(r.tok, lambda zz, plane: plane * NZ + zz, rows // 2, (r.q_send, r.q_recv, r.qx_send, r.qx_recv), hook)
    after()
    my_rows = pl.multiple_of((z * 2 + x_hi) * own, own)
    for index in range(2 * NZ):
        r.my_tokens[:, index * HD : (index + 1) * HD] = r.tok[index, pl.ds(my_rows, own)]
    tile = 128

    @pl.loop(0, rows // tile)
    def _(step):
        at = pl.ds(pl.multiple_of(step * tile, tile), tile)
        square = jnp.zeros((tile, HD), F32)
        for index in range(2 * NZ):
            value = r.tok[index, at].astype(F32)
            square = square + value * value
        mean = jnp.sum(square, axis=1, keepdims=True) / (2 * NZ * HD)
        scale = lax.rsqrt(mean + 1e-05)
        for index in range(2 * NZ):
            lanes = slice(index * HD, (index + 1) * HD)
            value = r.tok[index, at].astype(F32) * scale * r.norm_gain[:, lanes]
            r.normed[at, lanes] = value.astype(BF16)

    tile = 256

    @pl.loop(0, rows // tile)
    def _(step):
        at = pl.ds(pl.multiple_of(step * tile, tile), tile)
        out = jnp.dot(r.normed[at, :], r.weights[...], preferred_element_type=F32)
        cosine, sine = r.cosine[at, :], r.sine[at, :]

        def rotary(values):
            return (values * cosine + pltpu.roll(values, HD // 2, 1) * sine).astype(BF16)

        r.query[at, :] = rotary(out[:, :HD])
        r.pairs[dp, 0, at, :] = rotary(out[:, HD : 2 * HD])
        r.pairs[dp, 1, at, :] = out[:, 2 * HD :].astype(BF16)


def find_starts(r):
    dp = lax.axis_index("dp")
    rows = r.start.shape[0]
    position = (dp * rows + lax.broadcasted_iota(jnp.int32, r.start.shape, 0)).astype(F32)
    found = jnp.zeros(r.start.shape, F32)
    for number in range(1, 8):
        before = jnp.where(r.series[...] < number, 1.0, 0.0)
        begin = jnp.sum(jnp.sum(before, axis=0, keepdims=True), axis=1, keepdims=True)
        found = jnp.where(begin <= position, jnp.maximum(found, begin), found)
    r.start[...] = found.astype(jnp.int32)


R1, R2, R3, X0, X1, H1, H2, H3, OWN = range(9)


class Refs:
    def __init__(self, names, refs):
        for name, ref in zip(names, refs, strict=True):
            setattr(self, name, ref)


def attend(r, mine, j, diagonal, tile=256):
    rows, span = r.query.shape[0], r.pairs.shape[2]
    factor = HD ** (-0.5) * 1.4426950408889634
    key, value = r.pairs[j, 0], r.pairs[j, 1]
    for index in range(rows // tile):
        at = slice(index * tile, (index + 1) * tile)
        scores = lax.dot_general(
            r.query[at, :], key, (((1,), (1,)), ((), ())), preferred_element_type=F32
        )
        column = lax.broadcasted_iota(jnp.int32, (tile, span), 1)
        allowed = column >= r.start[at, :1] - j * span
        if diagonal:
            row = index * tile + lax.broadcasted_iota(jnp.int32, (tile, span), 0)
            allowed = allowed & (column <= row)
        scores = jnp.where(allowed, scores, -1e30)
        top = jnp.max(scores, axis=1, keepdims=True)
        if not diagonal:
            old = r.peak[at, :1]
            top = jnp.maximum(old, top)
        weights = jnp.exp2((scores - top) * factor)
        denom = jnp.sum(weights, axis=1, keepdims=True)
        accum = jnp.dot(weights.astype(BF16), value, preferred_element_type=F32)
        if not diagonal:
            scale = jnp.exp2((old - top) * factor)
            denom = denom + r.denom[at, :1] * scale
            accum = accum + r.accum[at, :] * scale
        r.peak[at, :] = jnp.broadcast_to(top, (tile, HD))
        r.denom[at, :] = jnp.broadcast_to(denom, (tile, HD))
        r.accum[at, :] = accum


def exchange(r, sent):
    dp, tensor, x_hi, z = places()
    x_lo, y, core = dp // (2 * NY), lax.rem(dp // 2, NY), lax.rem(dp, 2)

    def index(xx, yy, cc):
        return xx * 2 * NY + yy * 2 + cc

    k_partner = (index(1 - x_lo, y, core), tensor)
    sibling = (index(x_lo, y, 1 - core), tensor)
    up, down = ((index(x_lo, turn(y, by, NY), core), tensor) for by in (1, -1))
    z_peers = [(dp, x_hi * NZ + turn(z, by, NZ)) for by in range(1, NZ)]
    z_nexts = (z_peers[0], z_peers[-1])
    s_partner = (dp, (1 - x_hi) * NZ + z)
    deep = r.w_out.shape[0] // 4
    first, second = x_lo == 0, x_lo == 1

    def chip(by):
        return turn(y, by, NY)

    arrives = {
        R1: (y >= 1, x_lo, chip(-1)),
        R2: (y >= 2, x_lo, chip(-2)),
        R3: (y == 3, x_lo, chip(1)),
        X0: (second, 0, y),
        X1: (second & (y >= 1), 0, chip(-1)),
        H1: (second & (y <= 2), 0, chip(1)),
        H2: (second & (y <= 1), 0, chip(2)),
        H3: (second & (y == 0), 0, chip(-1)),
        OWN: (None, x_lo, y),
    }

    def k_copy(event, part, xx, yy, device):
        block = r.pairs.at[index(xx, yy, core), part]
        return remote(block, block, r.k_send.at[event, part], r.k_recv.at[event, part], device)

    later = []

    def when(condition, copy):
        @pl.when(condition)
        def _():
            copy.start()

        later.append((condition, copy))

    def k_wait(event, part):
        condition, xx, yy = arrives[event]

        @pl.when(condition)
        def _():
            k_copy(event, part, xx, yy, up).wait_recv()

    def c_copy(event, cc):
        _, xx, yy = arrives[event]
        block = r.pairs.at[index(xx, yy, cc)]
        return remote(block, block, r.c_send.at[event], r.c_recv.at[event], sibling)

    def share(event):
        condition = arrives[event][0]
        if condition is None:
            sent.start(c_copy(event, core))
        else:
            when(condition, c_copy(event, core))

    def shared(*events):
        for event in events:
            condition = arrives[event][0]
            if condition is None:
                c_copy(event, 1 - core).wait_recv()
            else:

                @pl.when(condition)
                def _(event=event):
                    c_copy(event, 1 - core).wait_recv()

    def work(*events):
        found = []
        for event in events:
            condition, xx, yy = arrives[event]
            for cc in (core, 1 - core):
                if event == OWN and cc is core:
                    continue
                j = index(xx, yy, cc)
                needed = (j < dp) & (j >= dp - 10)
                found.append((j, needed if condition is None else needed & condition))

        @pl.loop(0, len(found))
        def _(step):
            j, needed = found[0]
            needed = needed.astype(jnp.int32)
            for number, (jj, wanted) in enumerate(found[1:], 1):
                j = jnp.where(step == number, jj, j)
                needed = jnp.where(step == number, wanted.astype(jnp.int32), needed)

            @pl.when(needed == 1)
            def _():
                attend(r, dp, j, False)

    def w_copy(way, far, sub, hops):
        top = pl.multiple_of(core * 2 * deep + sub * deep, deep)
        block = r.wide.at[turn(z, -towards(way, hops), NZ), pl.ds(top, deep)]
        sems = r.w_send.at[way, far - 1, sub], r.w_recv.at[way, far - 1, sub]
        return remote(block, block, *sems, z_nexts[way])

    def w_share(by, slot, cc):
        top = pl.multiple_of(cc * 2 * deep, 2 * deep)
        block = r.wide.at[turn(z, by, NZ), pl.ds(top, 2 * deep)]
        return remote(block, block, r.wc_send.at[slot], r.wc_recv.at[slot], sibling)

    def w_forward(far, sub):
        for way in range(2):
            if far < 4 or sub == way:
                w_copy(way, far, sub, far).wait_recv()
            if far < 3 or (far == 3 and sub == way):
                sent.start(w_copy(way, far + 1, sub, far))

    def w_spread(far):
        for way in range(2):
            sent.start(w_share(towards(way, -far), 2 * (far - 1) + way, core))

    def begin_wide():
        for sub in range(2):
            for way in range(2):
                sent.start(w_copy(way, 1, sub, 0))

    def arrive():
        for part in range(2):
            when(y <= 2, k_copy(R1, part, x_lo, y, up))
            when(y == 0, k_copy(R3, part, x_lo, y, down))
            when(first, k_copy(X0, part, 0, y, k_partner))
        share(OWN)
        s_cross = remote(r.part.at[1 - x_hi], r.s_got, r.sx_send, r.sx_recv, s_partner)
        sent.start(s_cross)
        w_forward(1, 0)
        w_forward(1, 1)
        w_spread(1)
        attend(r, dp, dp, True)
        for part in range(2):
            k_wait(R1, part)
            when((y >= 1) & (y <= 2), k_copy(R2, part, x_lo, chip(-1), up))
            when(first & (y >= 1), k_copy(X1, part, 0, chip(-1), k_partner))
            k_wait(X0, part)
            when(second & (y >= 1), k_copy(H1, part, 0, y, down))
            when(second & (y == 3), k_copy(H3, part, 0, y, up))
            w_forward(2, part)
        share(R1)
        share(X0)
        w_spread(2)
        k_wait(R3, 0)
        k_wait(R3, 1)
        share(R3)
        s_cross.wait_recv()
        r.s_out[...] = (r.part[x_hi].astype(F32) + r.s_got[...].astype(F32)).astype(BF16)
        shared(OWN, R1)
        work(OWN, R1)
        for part in range(2):
            k_wait(H1, part)
            when(second & (y >= 1) & (y <= 2), k_copy(H2, part, 0, chip(1), down))
        share(H1)
        w_forward(3, 0)
        shared(X0)
        work(X0)
        w_forward(3, 1)
        w_spread(3)
        for event in (X1, R2, H3):
            k_wait(event, 0)
            k_wait(event, 1)
            share(event)
        shared(R3, H1)
        work(R3, H1)
        w_forward(4, 0)
        w_forward(4, 1)
        sent.start(w_share(4, 6, core))
        k_wait(H2, 0)
        k_wait(H2, 1)
        share(H2)
        shared(X1, R2, H3)
        work(X1, R2, H3)
        shared(H2)
        work(H2)
        r.attended[...] = (r.accum[...] / r.denom[...]).astype(BF16)

    def finish():
        for condition, copy in later:

            @pl.when(condition)
            def _(copy=copy):
                copy.wait_send()

    def wide_whole():
        for slot, by in enumerate([-1, 1, -2, 2, -3, 3, 4]):
            w_share(by, slot, 1 - core).wait_recv()

    return begin_wide, arrive, wide_whole, finish


def layer_body(names, total_rows, *refs):
    r = Refs(names, refs)
    dp, tensor, x_hi, z = places()
    size = 2 * NZ
    rows, width = r.tokens.shape[0], r.w_query.shape[0]
    own = rows // size
    pair = 2 * own
    row = z * 2 + x_hi
    my_rows = pl.ds(pl.multiple_of(row * own, own), own)
    partner = (dp, (1 - x_hi) * NZ + z)
    z_peers = [(dp, x_hi * NZ + turn(z, by, NZ)) for by in range(1, NZ)]
    t_peers = [turn(tensor, by, size) for by in range(1, size)]
    d_peers = [turn(dp, by, size) for by in range(1, size)]
    loads = []
    for index, name in enumerate(("w_gate", "w_up", "w_down", "projector")):
        far, near = getattr(r, name + "_hbm"), getattr(r, name)
        loads.append(pltpu.make_async_copy(far, near, r.load_sem.at[index]))
        loads[-1].start()
    r.wide[z] = r.w_out[...]
    r.tok[tensor] = r.tokens[...]
    greet(
        [(dp, peer) for peer in t_peers] + [(peer, tensor) for peer in d_peers],
        lambda: find_starts(r),
    )
    sent = Sent()
    begin_wide, arrive, wide_whole, finish_exchange = exchange(r, sent)
    project(r, begin_wide)
    arrive()

    def rows_of(zz):
        return pl.ds(pl.multiple_of(zz * pair, pair), pair)

    for by in range(1, NZ):
        sent.start(
            remote(
                r.attended.at[rows_of(turn(z, by, NZ))],
                r.heads.at[z],
                r.a_send.at[by - 1],
                r.a_recv.at[by - 1],
                z_peers[by - 1],
            )
        )
    for by in range(1, NZ):
        sent.start(
            remote(
                r.s_out.at[turn(z, by, NZ)],
                r.s_in.at[by - 1],
                r.sz_send.at[by - 1],
                r.sz_recv.at[by - 1],
                z_peers[by - 1],
            )
        )
    r.heads[z] = r.attended[rows_of(z), :]
    wide_whole()
    for by in range(1, NZ):
        block = r.heads.at[turn(z, -by, NZ)]
        remote(block, block, r.a_send.at[by - 1], r.a_recv.at[by - 1], z_peers[by - 1]).wait_recv()
    chunk = 512
    joined = jnp.concatenate([r.heads[index] for index in range(NZ)], axis=1)
    depth = joined.shape[1]

    @pl.loop(0, width // chunk)
    def _(step):
        at = pl.ds(pl.multiple_of(step * chunk, chunk), chunk)
        r.partial[:, at] = jnp.dot(
            joined, r.wide[:, :, at].reshape(depth, chunk), preferred_element_type=F32
        )

    def half_rows(plane):
        return pl.ds(pl.multiple_of(plane * own, own), own)

    r.out_send[...] = r.partial[half_rows(1 - x_hi), :].astype(BF16)
    swap = remote(r.out_send, r.out_recv, r.o_send, r.o_recv, partner)
    sent.start(swap)
    mine = r.partial[half_rows(x_hi), :] + r.my_tokens[...].astype(F32)
    swap.wait_recv()
    mixed = (mine + r.out_recv[...].astype(F32)).astype(BF16)
    r.mixed[...] = mixed
    r.blocks[row] = (rms(mixed.astype(F32)) * r.mlp_gain[...]).astype(BF16)

    waited = []

    def units(zs):
        if not waited:
            loads[0].wait()
            loads[1].wait()
            waited.append(True)
        value = jnp.concatenate(
            [r.blocks[pl.ds(zz * 2, 2)].reshape(pair, width) for zz in zs], axis=0
        )
        gate = jnp.dot(value, r.w_gate[...], preferred_element_type=F32)
        up = jnp.dot(value, r.w_up[...], preferred_element_type=F32)
        found = (gate * jax.nn.sigmoid(gate) * up).astype(BF16)
        for at, zz in enumerate(zs):
            r.hidden[zz] = found[at * pair : (at + 1) * pair]

    def ready(distances):
        zs = []
        for by in distances:
            zs += [z] if by == 0 else [turn(z, by, NZ), turn(z, -by, NZ)]
        units(zs)

    mix_gather(
        r.blocks,
        lambda zz, plane: zz * 2 + plane,
        own // 2,
        (r.g_send, r.g_recv, r.gx_send, r.gx_recv),
        ready=ready,
    )
    student_sum = r.s_out[z].astype(F32)
    for by in range(1, NZ):
        got = r.s_in.at[by - 1]
        remote(got, got, r.sz_send.at[by - 1], r.sz_recv.at[by - 1], z_peers[by - 1]).wait_recv()
        student_sum = student_sum + r.s_in[by - 1].astype(F32)
    r.predicted[...] = r.student[my_rows, :].astype(F32) + student_sum
    loads[2].wait()
    fresh = [2]

    def make(zs):
        if fresh:
            fresh.pop() if len(zs) == 2 else None
            units(zs)
        value = jnp.concatenate([r.hidden[zz] for zz in zs], axis=0)

        @pl.loop(0, width // chunk)
        def _(step):
            at = pl.ds(pl.multiple_of(step * chunk, chunk), chunk)
            out = jnp.dot(value, r.w_down[:, at], preferred_element_type=F32).astype(BF16)
            for index, zz in enumerate(zs):
                for plane in range(2):
                    top = index * pair + plane * own
                    r.parts[zz * 2 + plane, :, at] = out[top : top + own]

    scratch = (r.sbuf, r.rbuf, r.xbuf, r.xlast, r.xgot, r.r_send, r.r_recv, r.rx_send, r.rx_recv)
    top, bottom, more = mix_scatter(r.parts, make, scratch)
    teacher = r.mixed[...].astype(F32) + jnp.concatenate([top, bottom], axis=0)
    teacher = teacher.astype(BF16)
    r.teacher[...] = teacher
    loads[3].wait()
    target = jnp.dot(teacher, r.projector[...], preferred_element_type=F32)
    scaled = ((r.predicted[...] - target) * total_rows ** (-0.5)).astype(BF16)

    def place(by, plane):
        return r.gathered.at[turn(z, by, NZ) * 2 + plane]

    def across(by, plane):
        block = place(by, plane)
        at = by % NZ
        return remote(block, block, r.px_send.at[at], r.px_recv.at[at], partner)

    def along(by, device):
        block = place(-by if device is None else 0, x_hi)
        sems = r.p_send.at[by - 1], r.p_recv.at[by - 1]
        return remote(block, block, *sems, z_peers[by - 1])

    r.gathered[row] = scaled
    for by in (4, 3, 5, 2, 6, 1, 7):
        sent.start(along(by, True))
    sent.start(across(0, x_hi))
    for by, peer in enumerate(t_peers):
        sent.start(
            remote(
                r.teacher.at[:, pl.ds(pl.multiple_of(peer * HD, HD), HD)],
                r.columns.at[row],
                r.t_send.at[by],
                r.t_recv.at[by],
                (dp, peer),
            )
        )
    r.columns[row] = r.teacher[:, pl.ds(pl.multiple_of(tensor * HD, HD), HD)]
    for by in (1, 7, 2, 6, 3, 5, 4):
        along(by, None).wait_recv()
        sent.start(across(-by, x_hi))
    for by in (0, 1, 7, 2, 6, 3, 5, 4):
        across(-by, 1 - x_hi).wait_recv()

    scaled = r.gathered[...].reshape(rows, -1)
    grad_hidden = lax.dot_general(
        scaled, r.s_down[...], (((1,), (1,)), ((), ())), preferred_element_type=F32
    )
    both = jnp.concatenate(
        [(grad_hidden * r.by_gate[...]).astype(BF16), (grad_hidden * r.by_up[...]).astype(BF16)],
        axis=1,
    )
    both = jnp.dot(r.normed_t[...], both, preferred_element_type=F32).astype(BF16)
    down = jnp.dot(r.hidden_t[...], scaled, preferred_element_type=F32).astype(BF16)
    count = grad_hidden.shape[1]
    r.grads[:, :own] = both[:, :count].reshape(size, own, count)
    r.grads[:, own:pair] = both[:, count:].reshape(size, own, count)
    down = jnp.concatenate([down[:, at : at + HD] for at in range(0, down.shape[1], HD)], axis=0)
    r.grads[:, pair : 3 * own] = down.reshape(size, own, HD)
    squares = scaled.astype(F32)
    squares = jnp.sum((squares * squares).reshape(-1, 8, scaled.shape[1]), axis=0)
    squares = sum(squares[:, at : at + HD] for at in range(0, scaled.shape[1], HD))
    high = squares.astype(BF16)
    low = (squares - high.astype(F32)).astype(BF16)
    both = jnp.concatenate([high, low], axis=0)
    r.grads[:, 3 * own :] = jnp.broadcast_to(both[None], (size,) + both.shape)

    def origin(by):
        return turn(dp, -(by + 1), size)

    r.inbox[dp] = r.grads[dp]
    for by, peer in enumerate(d_peers):
        sems = r.send1.at[by], r.recv1.at[by]
        sent.start(remote(r.grads.at[peer], r.inbox.at[dp], *sems, (peer, tensor)))
    for by, peer in enumerate(d_peers):
        block = r.inbox.at[origin(by)]
        remote(block, block, r.send1.at[by], r.recv1.at[by], (peer, tensor)).wait_recv()
    total = r.inbox[0].astype(F32)
    for index in range(1, size):
        total = total + r.inbox[index].astype(F32)
    r.sums[dp] = total[: 3 * own].astype(BF16)
    r.error[...] = total[3 * own : 3 * own + 8] + total[3 * own + 8 :]
    for by, peer in enumerate(d_peers):
        block = r.sums.at[dp]
        sent.start(remote(block, block, r.send2.at[by], r.recv2.at[by], (peer, tensor)))
    for by, peer in enumerate(t_peers):
        source = turn(tensor, -(by + 1), size)
        block = r.columns.at[lax.rem(source, NZ) * 2 + source // NZ]
        remote(block, block, r.t_send.at[by], r.t_recv.at[by], (dp, peer)).wait_recv()
    for by, peer in enumerate(d_peers):
        block = r.sums.at[origin(by)]
        remote(block, block, r.send2.at[by], r.recv2.at[by], (peer, tensor)).wait_recv()
    finish_exchange()
    sent.finish()
    more.finish()


def finish_body(columns_ref, sums_ref, squares_ref, teacher_ref, gate_ref, up_ref, down_ref, error_ref):
    rows, width = teacher_ref.shape
    own = rows // (2 * NZ)
    teacher_ref[...] = columns_ref[...].reshape(rows, width)
    sums = sums_ref[...].astype(F32)
    gate_ref[...] = sums[:, :own].reshape(-1, width)
    up_ref[...] = sums[:, own : 2 * own].reshape(-1, width)
    down = sums[:, 2 * own :].reshape(-1, width)
    for index in range(down.shape[0] // width):
        lanes = slice(index * width, (index + 1) * width)
        down_ref[:, lanes] = down[lanes]
    total = jnp.sum(jnp.sum(squares_ref[...], axis=0, keepdims=True), axis=1, keepdims=True)
    error_ref[...] = total / down_ref.shape[1]


def finish(columns, sums, squares):
    own, units = columns.shape[1:]
    rows = 2 * NZ * own
    shapes = (
        ((rows, units), BF16),
        ((rows, units), F32),
        ((rows, units), F32),
        ((units, rows), F32),
        ((1, 1), F32),
    )
    return pl.pallas_call(
        finish_body,
        out_shape=tuple(jax.ShapeDtypeStruct(shape, kind) for shape, kind in shapes),
        in_specs=[VM] * 3,
        out_specs=(VM,) * 5,
        compiler_params=pltpu.CompilerParams(vmem_limit_bytes=LIMIT),
        name="finish",
    )(columns, sums, squares)


def frequencies(head_dim):
    indices = jnp.arange(head_dim // 2).astype(F32)
    return jnp.exp(-jnp.log(500000.0) * 2.0 * indices / head_dim)


def local(
    tokens,
    series_ids,
    offsets,
    norm_gain,
    mlp_gain,
    w_query,
    w_key,
    w_value,
    w_out,
    w_gate,
    w_up,
    w_down,
    projector,
    student_in,
    s_gate,
    s_up,
    s_down,
):
    rows = tokens.shape[0]
    size = 2 * NZ
    own = rows // size
    width = projector.shape[0]
    narrow = student_in.shape[1]
    units = s_gate.shape[1]
    ff = w_gate.shape[1]
    angles = offsets.astype(F32)[:, None] * frequencies(HD)[None, :]
    cosine, sine = jnp.cos(angles), jnp.sin(angles)
    cosine = jnp.concatenate([cosine, cosine], axis=1)
    sine = jnp.concatenate([-sine, sine], axis=1)
    inputs = {
        "tokens": tokens,
        "series": series_ids.reshape(-1, HD),
        "norm_gain": norm_gain[None],
        "cosine": cosine,
        "sine": sine,
        "w_query": w_query,
        "w_key": w_key,
        "w_value": w_value,
        "w_out": w_out,
        "mlp_gain": mlp_gain[None],
        "w_gate_hbm": w_gate,
        "w_up_hbm": w_up,
        "w_down_hbm": w_down,
        "projector_hbm": projector,
        "student": student_in,
        "s_gate": s_gate,
        "s_up": s_up,
        "s_down": s_down,
    }
    outputs = {
        "columns": ((size, own, HD), BF16),
        "sums": ((size, 3 * own, units), BF16),
        "error": ((8, HD), F32),
    }
    one = pltpu.SemaphoreType.DMA
    half = own // 2
    scratch = {
        "tok": pltpu.VMEM((size, rows, HD), BF16),
        "normed": pltpu.VMEM((rows, width), BF16),
        "weights": pltpu.VMEM((width, 3 * HD), BF16),
        "query": pltpu.VMEM((rows, HD), BF16),
        "my_tokens": pltpu.VMEM((own, width), BF16),
        "part": pltpu.VMEM((2, NZ, own, narrow), BF16),
        "normed_t": pltpu.VMEM((narrow, rows), BF16),
        "hidden_t": pltpu.VMEM((units, rows), BF16),
        "by_gate": pltpu.VMEM((rows, units), F32),
        "by_up": pltpu.VMEM((rows, units), F32),
        "q_send": dma(2, 4, 3),
        "q_recv": dma(2, 4, 3),
        "qx_send": dma(9),
        "qx_recv": dma(9),
        "pairs": pltpu.VMEM((4 * NY, 2, rows, HD), BF16),
        "wide": pltpu.VMEM((NZ,) + w_out.shape, BF16),
        "start": pltpu.VMEM((rows, HD), jnp.int32),
        "peak": pltpu.VMEM((rows, HD), F32),
        "denom": pltpu.VMEM((rows, HD), F32),
        "accum": pltpu.VMEM((rows, HD), F32),
        "attended": pltpu.VMEM((rows, HD), BF16),
        "k_send": dma(9, 2),
        "k_recv": dma(9, 2),
        "c_send": dma(9),
        "c_recv": dma(9),
        "w_send": dma(2, 4, 2),
        "w_recv": dma(2, 4, 2),
        "wc_send": dma(7),
        "wc_recv": dma(7),
        "s_got": pltpu.VMEM((NZ, own, narrow), BF16),
        "s_out": pltpu.VMEM((NZ, own, narrow), BF16),
        "s_in": pltpu.VMEM((NZ - 1, own, narrow), BF16),
        "sx_send": one,
        "sx_recv": one,
        "sz_send": dma(7),
        "sz_recv": dma(7),
        "w_gate": pltpu.VMEM(w_gate.shape, BF16),
        "w_up": pltpu.VMEM(w_up.shape, BF16),
        "w_down": pltpu.VMEM(w_down.shape, BF16),
        "projector": pltpu.VMEM(projector.shape, BF16),
        "load_sem": dma(4),
        "heads": pltpu.VMEM((NZ, 2 * own, HD), BF16),
        "a_send": dma(7),
        "a_recv": dma(7),
        "out_send": pltpu.VMEM((own, width), BF16),
        "out_recv": pltpu.VMEM((own, width), BF16),
        "o_send": one,
        "o_recv": one,
        "partial": pltpu.VMEM((2 * own, width), F32),
        "mixed": pltpu.VMEM((own, width), BF16),
        "blocks": pltpu.VMEM((size, own, width), BF16),
        "hidden": pltpu.VMEM((NZ, 2 * own, ff), BF16),
        "parts": pltpu.VMEM((size, own, width), BF16),
        "predicted": pltpu.VMEM((own, narrow), F32),
        "g_send": dma(2, 4, 3),
        "g_recv": dma(2, 4, 3),
        "gx_send": dma(9),
        "gx_recv": dma(9),
    }
    names = ("sbuf", "rbuf", "xbuf", "xlast", "xgot", "r_send", "r_recv", "rx_send", "rx_recv")
    scratch.update(zip(names, scatter_scratch(half, width), strict=True))
    scratch.update(
        {
            "teacher": pltpu.VMEM((own, width), BF16),
            "gathered": pltpu.VMEM((size, own, narrow), BF16),
            "px_send": dma(8),
            "px_recv": dma(8),
            "p_send": dma(7),
            "p_recv": dma(7),
            "t_send": dma(size - 1),
            "t_recv": dma(size - 1),
            "grads": pltpu.VMEM((size, 3 * own + 16, units), BF16),
            "inbox": pltpu.VMEM((size, 3 * own + 16, units), BF16),
            "send1": dma(size - 1),
            "recv1": dma(size - 1),
            "send2": dma(size - 1),
            "recv2": dma(size - 1),
        }
    )
    far = pl.BlockSpec(memory_space=pl.ANY)
    columns, sums, squares = call(
        functools.partial(
            layer_body, (*inputs, *outputs, *scratch), rows * lax.axis_size("dp")
        ),
        "layer",
        1,
        tuple(inputs.values()),
        tuple(outputs.values()),
        list(scratch.values()),
        [far if name.endswith("_hbm") else VM for name in inputs],
    )
    teacher_out, grad_gate, grad_up, grad_down, error = finish(columns, sums, squares)
    return (teacher_out, grad_gate, grad_up, grad_down, error.reshape(()))


def solution(mesh):
    in_specs = (
        P("dp", "tensor"),
        P(),
        P("dp"),
        P(),
        P(),
        P(None, "tensor"),
        P(None, "tensor"),
        P(None, "tensor"),
        P("tensor", None),
        P(None, "tensor"),
        P(None, "tensor"),
        P("tensor", None),
        P(),
        P("dp", None),
        P(None, "tensor"),
        P(None, "tensor"),
        P("tensor", None),
    )
    out_specs = (P("dp", "tensor"), P(None, "tensor"), P(None, "tensor"), P("tensor", None), P())
    return jax.shard_map(local, mesh=mesh, in_specs=in_specs, out_specs=out_specs, check_vma=False)
```

```python
import functools

import jax
import jax.numpy as jnp
from jax import lax
from jax.experimental import pallas as pl
from jax.experimental.pallas import tpu as pltpu
from jax.sharding import PartitionSpec as P

HD = 128
NZ = 8
NY = 4
MESH = pl.DeviceIdType.MESH
VM = pl.BlockSpec(memory_space=pltpu.VMEM)
LIMIT = 56 * 1024 * 1024
F32 = jnp.float32
BF16 = jnp.bfloat16


def params(collective_id):
    return pltpu.CompilerParams(
        collective_id=collective_id, has_side_effects=True, vmem_limit_bytes=LIMIT
    )


def remote(src, dst, send_sem, recv_sem, device):
    return pltpu.make_async_remote_copy(
        src_ref=src,
        dst_ref=dst,
        send_sem=send_sem,
        recv_sem=recv_sem,
        device_id=device,
        device_id_type=MESH,
    )


def greet(devices, meanwhile=None):
    barrier = pltpu.get_barrier_semaphore()
    for device in devices:
        pl.semaphore_signal(barrier, inc=1, device_id=device, device_id_type=MESH)
    if meanwhile is not None:
        meanwhile()
    pl.semaphore_wait(barrier, len(devices))


def places():
    dp, tensor = lax.axis_index("dp"), lax.axis_index("tensor")
    x_hi, z = tensor // NZ, lax.rem(tensor, NZ)
    return dp, tensor, x_hi, z


def turn(z, by, size):
    return lax.rem(z + by + size, size)


def dma(*shape):
    return pltpu.SemaphoreType.DMA(shape)


def call(body, name, collective_id, inputs, outputs, scratch, specs=None):
    return pl.pallas_call(
        body,
        out_shape=tuple(jax.ShapeDtypeStruct(shape, kind) for shape, kind in outputs),
        in_specs=specs or [VM] * len(inputs),
        out_specs=tuple([VM] * len(outputs)),
        scratch_shapes=scratch,
        compiler_params=params(collective_id),
        name=name,
    )(*inputs)


class Sent:
    def __init__(self):
        self.copies = []

    def start(self, copy):
        copy.start()
        self.copies.append(copy)

    def finish(self):
        for copy in self.copies:
            copy.wait_send()


def on_ring(way, far, sub):
    return far < 4 or (way == 1) == (sub == 1)


def towards(way, by):
    return by if way == 0 else -by


def mix_gather(ref, at, half, sems, hook=lambda step: None, ready=None, tail=None):
    ring_send, ring_recv, x_send, x_recv = sems
    dp, tensor, x_hi, z = places()
    partner = (dp, (1 - x_hi) * NZ + z)
    nexts = tuple((dp, x_hi * NZ + turn(z, by, NZ)) for by in (1, -1))
    sent = Sent()

    def view(zz, sub):
        plane = x_hi if sub < 2 else 1 - x_hi
        return ref.at[at(zz, plane), pl.ds((sub % 2) * half, half)]

    def ring(way, far, sub, hops):
        block = view(turn(z, -towards(way, hops), NZ), sub)
        sems = ring_send.at[way, far - 1, sub], ring_recv.at[way, far - 1, sub]
        return remote(block, block, *sems, nexts[way])

    def cross(zz, sub, slot):
        block = view(zz, sub)
        return remote(block, block, x_send.at[slot], x_recv.at[slot], partner)

    def slot(way, far):
        return 1 + far + 3 * way if way == 0 else 4 + far

    def crossed(far):
        if far == 0:
            cross(z, 3, 1).wait_recv()
        for way in range(2):
            if 0 < far < 4 + way:
                cross(turn(z, -towards(way, far), NZ), 3, slot(way, far)).wait_recv()

    sent.start(cross(z, 0, 0))
    for sub in range(2):
        for way in range(2):
            sent.start(ring(way, 1, sub, 0))
    sent.start(cross(z, 1, 1))
    hook(0)
    cross(z, 2, 0).wait_recv()
    for way in range(2):
        sent.start(ring(way, 1, 2, 0))
    for far in range(2, 5):
        hook(far - 1)
        for sub in range(3):
            for way in range(2):
                ring(way, far - 1, sub, far - 1).wait_recv()
                if on_ring(way, far, sub):
                    sent.start(ring(way, far, sub, far - 1))
                if sub == 1:
                    origin = turn(z, -towards(way, far - 1), NZ)
                    sent.start(cross(origin, 1, slot(way, far - 1)))
        if far == 3:
            crossed(0)
            crossed(1)
            if ready:
                ready((0, 1))
        if far == 4:
            crossed(2)
            if ready:
                ready((2,))
    ring(1, 4, 1, 4).wait_recv()
    sent.start(cross(turn(z, 4, NZ), 1, slot(1, 4)))
    crossed(3)
    if tail:
        tail()
    for sub in (0, 2):
        ring(0, 4, sub, 4).wait_recv()
    crossed(4)
    sent.finish()


def scatter_scratch(half, width):
    return [
        pltpu.VMEM((2, 4, 3, half, width), BF16),
        pltpu.VMEM((2, 4, 3, half, width), BF16),
        pltpu.VMEM((8, half, width), BF16),
        pltpu.VMEM((half, width), BF16),
        pltpu.VMEM((half, width), BF16),
        dma(2, 4, 3),
        dma(2, 4, 3),
        dma(9),
        dma(9),
    ]


def mix_scatter(part, make, scratch):
    sbuf, rbuf, xbuf, xlast, xgot, ring_send, ring_recv, x_send, x_recv = scratch
    half = sbuf.shape[3]
    dp, tensor, x_hi, z = places()
    partner = (dp, (1 - x_hi) * NZ + z)
    nexts = tuple((dp, x_hi * NZ + turn(z, by, NZ)) for by in (1, -1))
    sent = Sent()

    def view(zz, sub):
        plane = x_hi if sub < 2 else 1 - x_hi
        return part.at[zz * 2 + plane, pl.ds((sub % 2) * half, half)]

    def slot(way, far):
        return 7 if far == 4 else 1 + 3 * way + far - 1

    def cross(zz, at):
        return remote(view(zz, 3), xbuf.at[at], x_send.at[at], x_recv.at[at], partner)

    def ring(way, far, sub, source):
        sems = ring_send.at[way, far - 1, sub], ring_recv.at[way, far - 1, sub]
        return remote(source, rbuf.at[way, far - 1, sub], *sems, nexts[way])

    def arrived(way, far, sub):
        ring(way, far, sub, rbuf.at[way, far - 1, sub]).wait_recv()
        return rbuf[way, far - 1, sub].astype(F32)

    def crossed(at):
        cross(z, at).wait_recv()
        return xbuf[at].astype(F32)

    def send(way, far, sub):
        source = view(turn(z, towards(way, far), NZ), sub)
        extra = []
        if far < 4 and on_ring(way, far + 1, sub):
            extra.append(arrived(way, far + 1, sub))
        if sub == 1:
            extra.append(crossed(slot(way, far)))
        if extra:
            total = source[...].astype(F32)
            for one in extra:
                total = total + one
            sbuf[way, far - 1, sub] = total.astype(BF16)
            source = sbuf.at[way, far - 1, sub]
        sent.start(ring(way, far, sub, source))

    def make_pair(far):
        pair = [turn(z, by, NZ) for by in (far, -far)]
        make(pair)
        for way in range(2):
            sent.start(cross(pair[way], slot(way, far)))

    def begin():
        make_pair(3)
        for sub in (0, 2):
            send(1, 3, sub)

    def rest():
        far4 = turn(z, 4, NZ)
        make([far4])
        sent.start(cross(far4, 7))
        for sub in (0, 2):
            send(0, 4, sub)
        make_pair(2)
        send(1, 4, 1)
        for sub in (1, 2, 0):
            send(0, 3, sub)
        send(1, 3, 1)
        make_pair(1)
        for sub in (2, 0, 1):
            for way in range(2):
                send(way, 2, sub)
        make([z])
        sent.start(cross(z, 0))
        for sub in (2, 0, 1):
            for way in range(2):
                send(way, 1, sub)
        return last_sums()

    def total(sub):
        return view(z, sub)[...].astype(F32) + arrived(0, 1, sub) + arrived(1, 1, sub)

    def last_sums():
        xlast[...] = total(2).astype(BF16)
        last = remote(xlast, xgot, x_send.at[8], x_recv.at[8], partner)
        sent.start(last)
        second = total(1) + crossed(0)
        first = total(0)
        last.wait_recv()
        first = first + xgot[...].astype(F32)
        return first, second, sent

    return begin, rest


def rms(values):
    return values * lax.rsqrt(jnp.mean(values * values, axis=-1, keepdims=True) + 1e-05)


def student(r, step):
    own = r.tokens.shape[0] // (2 * NZ)
    at = pl.ds(step * 128, 128)
    values = rms(r.student[at, :].astype(F32))
    r.normed_t[:, at] = values.T.astype(BF16)
    values = values.astype(BF16)
    gate = jnp.dot(values, r.s_gate[...], preferred_element_type=F32)
    up = jnp.dot(values, r.s_up[...], preferred_element_type=F32)
    sigmoid = jax.nn.sigmoid(gate)
    r.by_gate[at, :] = up * sigmoid * (1.0 + gate * (1.0 - sigmoid))
    r.by_up[at, :] = gate * sigmoid
    hidden = gate * sigmoid * up
    r.hidden_t[:, at] = hidden.T.astype(BF16)
    out = jnp.dot(hidden.astype(BF16), r.s_down[...], preferred_element_type=F32)
    for index in range(128 // own):
        block = out[index * own : (index + 1) * own].astype(BF16)
        r.part[index % 2, step * (64 // own) + index // 2] = block


def project(r, after):
    dp, tensor, x_hi, z = places()
    rows = r.tokens.shape[0]
    own = rows // (2 * NZ)

    def hook(step):
        if step == 3:
            student(r, 3)

    mix_gather(r.tok, lambda zz, plane: plane * NZ + zz, rows // 2, (r.q_send, r.q_recv, r.qx_send, r.qx_recv), hook)
    after()
    my_rows = pl.multiple_of((z * 2 + x_hi) * own, own)
    for index in range(2 * NZ):
        r.my_tokens[:, index * HD : (index + 1) * HD] = r.tok[index, pl.ds(my_rows, own)]
    tile = 128

    @pl.loop(0, rows // tile)
    def _(step):
        at = pl.ds(pl.multiple_of(step * tile, tile), tile)
        square = jnp.zeros((tile, HD), F32)
        for index in range(2 * NZ):
            value = r.tok[index, at].astype(F32)
            square = square + value * value
        mean = jnp.sum(square, axis=1, keepdims=True) / (2 * NZ * HD)
        scale = lax.rsqrt(mean + 1e-05)
        for index in range(2 * NZ):
            lanes = slice(index * HD, (index + 1) * HD)
            value = r.tok[index, at].astype(F32) * scale * r.norm_gain[:, lanes]
            r.normed[at, lanes] = value.astype(BF16)

    tile = 256

    @pl.loop(0, rows // tile)
    def _(step):
        at = pl.ds(pl.multiple_of(step * tile, tile), tile)
        out = jnp.dot(r.normed[at, :], r.weights[...], preferred_element_type=F32)
        cosine, sine = r.cosine[at, :], r.sine[at, :]

        def rotary(values):
            return (values * cosine + pltpu.roll(values, HD // 2, 1) * sine).astype(BF16)

        r.query[at, :] = rotary(out[:, :HD])
        r.pairs[dp, 0, at, :] = rotary(out[:, HD : 2 * HD])
        r.pairs[dp, 1, at, :] = out[:, 2 * HD :].astype(BF16)


def find_starts(r):
    dp = lax.axis_index("dp")
    rows = r.start.shape[0]
    position = (dp * rows + lax.broadcasted_iota(jnp.int32, r.start.shape, 0)).astype(F32)
    found = jnp.zeros(r.start.shape, F32)
    for number in range(1, 8):
        before = jnp.where(r.series[...] < number, 1.0, 0.0)
        begin = jnp.sum(jnp.sum(before, axis=0, keepdims=True), axis=1, keepdims=True)
        found = jnp.where(begin <= position, jnp.maximum(found, begin), found)
    r.start[...] = found.astype(jnp.int32)


def prepare(r):
    find_starts(r)
    r.weights[:, :HD] = r.w_query[...]
    r.weights[:, HD : 2 * HD] = r.w_key[...]
    r.weights[:, 2 * HD :] = r.w_value[...]
    for step in range(r.offsets.shape[0]):
        at = pl.ds(step * HD, HD)
        offset = jnp.broadcast_to(r.offsets[step : step + 1, :].astype(F32), (HD, HD)).T
        angle = offset * r.frequency[...]
        lane = lax.broadcasted_iota(jnp.int32, (HD, HD), 1)
        r.cosine[at, :] = jnp.cos(angle)
        sine = jnp.sin(angle)
        r.sine[at, :] = jnp.where(lane < HD // 2, -sine, sine)
    for step in range(3):
        student(r, step)


R1, R2, R3, X0, X1, H1, H2, H3, OWN = range(9)


class Refs:
    def __init__(self, names, refs):
        for name, ref in zip(names, refs, strict=True):
            setattr(self, name, ref)


def attend(r, mine, j, diagonal, tile=256):
    rows, span = r.query.shape[0], r.pairs.shape[2]
    factor = HD ** (-0.5) * 1.4426950408889634
    key, value = r.pairs[j, 0], r.pairs[j, 1]
    for index in range(rows // tile):
        at = slice(index * tile, (index + 1) * tile)
        scores = lax.dot_general(
            r.query[at, :], key, (((1,), (1,)), ((), ())), preferred_element_type=F32
        )
        column = lax.broadcasted_iota(jnp.int32, (tile, span), 1)
        allowed = column >= r.start[at, :1] - j * span
        if diagonal:
            row = index * tile + lax.broadcasted_iota(jnp.int32, (tile, span), 0)
            allowed = allowed & (column <= row)
        scores = jnp.where(allowed, scores, -1e30)
        top = jnp.max(scores, axis=1, keepdims=True)
        if not diagonal:
            old = r.peak[at, :1]
            top = jnp.maximum(old, top)
        weights = jnp.exp2((scores - top) * factor)
        denom = jnp.sum(weights, axis=1, keepdims=True)
        accum = jnp.dot(weights.astype(BF16), value, preferred_element_type=F32)
        if not diagonal:
            scale = jnp.exp2((old - top) * factor)
            denom = denom + r.denom[at, :1] * scale
            accum = accum + r.accum[at, :] * scale
        r.peak[at, :] = jnp.broadcast_to(top, (tile, HD))
        r.denom[at, :] = jnp.broadcast_to(denom, (tile, HD))
        r.accum[at, :] = accum


def exchange(r, sent):
    dp, tensor, x_hi, z = places()
    x_lo, y, core = dp // (2 * NY), lax.rem(dp // 2, NY), lax.rem(dp, 2)

    def index(xx, yy, cc):
        return xx * 2 * NY + yy * 2 + cc

    k_partner = (index(1 - x_lo, y, core), tensor)
    sibling = (index(x_lo, y, 1 - core), tensor)
    up, down = ((index(x_lo, turn(y, by, NY), core), tensor) for by in (1, -1))
    z_peers = [(dp, x_hi * NZ + turn(z, by, NZ)) for by in range(1, NZ)]
    z_nexts = (z_peers[0], z_peers[-1])
    s_partner = (dp, (1 - x_hi) * NZ + z)
    deep = r.w_out.shape[0] // 4
    first, second = x_lo == 0, x_lo == 1

    def chip(by):
        return turn(y, by, NY)

    arrives = {
        R1: (y >= 1, x_lo, chip(-1)),
        R2: (y >= 2, x_lo, chip(-2)),
        R3: (y == 3, x_lo, chip(1)),
        X0: (second, 0, y),
        X1: (second & (y >= 1), 0, chip(-1)),
        H1: (second & (y <= 2), 0, chip(1)),
        H2: (second & (y <= 1), 0, chip(2)),
        H3: (second & (y == 0), 0, chip(-1)),
        OWN: (None, x_lo, y),
    }

    def k_copy(event, part, xx, yy, device):
        block = r.pairs.at[index(xx, yy, core), part]
        return remote(block, block, r.k_send.at[event, part], r.k_recv.at[event, part], device)

    later = []

    def when(condition, copy):
        @pl.when(condition)
        def _():
            copy.start()

        later.append((condition, copy))

    def k_wait(event, part):
        condition, xx, yy = arrives[event]

        @pl.when(condition)
        def _():
            k_copy(event, part, xx, yy, up).wait_recv()

    def c_copy(event, cc):
        _, xx, yy = arrives[event]
        block = r.pairs.at[index(xx, yy, cc)]
        return remote(block, block, r.c_send.at[event], r.c_recv.at[event], sibling)

    def share(event):
        condition = arrives[event][0]
        if condition is None:
            sent.start(c_copy(event, core))
        else:
            when(condition, c_copy(event, core))

    def shared(*events):
        for event in events:
            condition = arrives[event][0]
            if condition is None:
                c_copy(event, 1 - core).wait_recv()
            else:

                @pl.when(condition)
                def _(event=event):
                    c_copy(event, 1 - core).wait_recv()

    def work(*events):
        found = []
        for event in events:
            condition, xx, yy = arrives[event]
            for cc in (core, 1 - core):
                if event == OWN and cc is core:
                    continue
                j = index(xx, yy, cc)
                needed = (j < dp) & (j >= dp - 10)
                found.append((j, needed if condition is None else needed & condition))

        @pl.loop(0, len(found))
        def _(step):
            j, needed = found[0]
            needed = needed.astype(jnp.int32)
            for number, (jj, wanted) in enumerate(found[1:], 1):
                j = jnp.where(step == number, jj, j)
                needed = jnp.where(step == number, wanted.astype(jnp.int32), needed)

            @pl.when(needed == 1)
            def _():
                attend(r, dp, j, False)

    def w_copy(way, far, sub, hops):
        top = pl.multiple_of(core * 2 * deep + sub * deep, deep)
        block = r.wide.at[turn(z, -towards(way, hops), NZ), pl.ds(top, deep)]
        sems = r.w_send.at[way, far - 1, sub], r.w_recv.at[way, far - 1, sub]
        return remote(block, block, *sems, z_nexts[way])

    def w_share(by, slot, cc):
        top = pl.multiple_of(cc * 2 * deep, 2 * deep)
        block = r.wide.at[turn(z, by, NZ), pl.ds(top, 2 * deep)]
        return remote(block, block, r.wc_send.at[slot], r.wc_recv.at[slot], sibling)

    def w_forward(far, sub):
        for way in range(2):
            if far < 4 or sub == way:
                w_copy(way, far, sub, far).wait_recv()
            if far < 3 or (far == 3 and sub == way):
                sent.start(w_copy(way, far + 1, sub, far))

    def w_spread(far):
        for way in range(2):
            sent.start(w_share(towards(way, -far), 2 * (far - 1) + way, core))

    def begin_wide():
        for sub in range(2):
            for way in range(2):
                sent.start(w_copy(way, 1, sub, 0))

    def arrive():
        for part in range(2):
            when(y <= 2, k_copy(R1, part, x_lo, y, up))
            when(y == 0, k_copy(R3, part, x_lo, y, down))
            when(first, k_copy(X0, part, 0, y, k_partner))
        share(OWN)
        s_cross = remote(r.part.at[1 - x_hi], r.s_got, r.sx_send, r.sx_recv, s_partner)
        sent.start(s_cross)
        w_forward(1, 0)
        w_forward(1, 1)
        w_spread(1)
        attend(r, dp, dp, True)
        for part in range(2):
            k_wait(R1, part)
            when((y >= 1) & (y <= 2), k_copy(R2, part, x_lo, chip(-1), up))
            when(first & (y >= 1), k_copy(X1, part, 0, chip(-1), k_partner))
            k_wait(X0, part)
            when(second & (y >= 1), k_copy(H1, part, 0, y, down))
            when(second & (y == 3), k_copy(H3, part, 0, y, up))
            w_forward(2, part)
        share(R1)
        share(X0)
        w_spread(2)
        k_wait(R3, 0)
        k_wait(R3, 1)
        share(R3)
        s_cross.wait_recv()
        r.s_out[...] = (r.part[x_hi].astype(F32) + r.s_got[...].astype(F32)).astype(BF16)
        shared(OWN, R1)
        work(OWN, R1)
        for part in range(2):
            k_wait(H1, part)
            when(second & (y >= 1) & (y <= 2), k_copy(H2, part, 0, chip(1), down))
        share(H1)
        w_forward(3, 0)
        shared(X0)
        work(X0)
        w_forward(3, 1)
        w_spread(3)
        for event in (X1, R2, H3):
            k_wait(event, 0)
            k_wait(event, 1)
            share(event)
        shared(R3, H1)
        work(R3, H1)
        w_forward(4, 0)
        w_forward(4, 1)
        sent.start(w_share(4, 6, core))
        k_wait(H2, 0)
        k_wait(H2, 1)
        share(H2)
        shared(X1, R2, H3)
        work(X1, R2, H3)
        shared(H2)
        work(H2)
        r.attended[...] = (r.accum[...] / r.denom[...]).astype(BF16)

    def finish():
        for condition, copy in later:

            @pl.when(condition)
            def _(copy=copy):
                copy.wait_send()

    def wide_whole():
        for slot, by in enumerate([-1, 1, -2, 2, -3, 3, 4]):
            w_share(by, slot, 1 - core).wait_recv()

    return begin_wide, arrive, wide_whole, finish


def layer_body(names, total_rows, *refs):
    r = Refs(names, refs)
    dp, tensor, x_hi, z = places()
    size = 2 * NZ
    rows, width = r.tokens.shape[0], r.w_query.shape[0]
    own = rows // size
    pair = 2 * own
    row = z * 2 + x_hi
    my_rows = pl.ds(pl.multiple_of(row * own, own), own)
    partner = (dp, (1 - x_hi) * NZ + z)
    z_peers = [(dp, x_hi * NZ + turn(z, by, NZ)) for by in range(1, NZ)]
    t_peers = [turn(tensor, by, size) for by in range(1, size)]
    d_peers = [turn(dp, by, size) for by in range(1, size)]
    loads = []
    for index, name in enumerate(("w_gate", "w_up", "w_down", "projector")):
        far, near = getattr(r, name + "_hbm"), getattr(r, name)
        loads.append(pltpu.make_async_copy(far, near, r.load_sem.at[index]))
        loads[-1].start()
    r.wide[z] = r.w_out[...]
    r.tok[tensor] = r.tokens[...]
    greet(
        [(dp, peer) for peer in t_peers] + [(peer, tensor) for peer in d_peers],
        lambda: prepare(r),
    )
    sent = Sent()
    begin_wide, arrive, wide_whole, finish_exchange = exchange(r, sent)
    project(r, begin_wide)
    arrive()

    def rows_of(zz):
        return pl.ds(pl.multiple_of(zz * pair, pair), pair)

    for by in range(1, NZ):
        sent.start(
            remote(
                r.attended.at[rows_of(turn(z, by, NZ))],
                r.heads.at[z],
                r.a_send.at[by - 1],
                r.a_recv.at[by - 1],
                z_peers[by - 1],
            )
        )
    def send_student():
        for by in range(1, NZ):
            sent.start(
                remote(
                    r.s_out.at[turn(z, by, NZ)],
                    r.s_in.at[by - 1],
                    r.sz_send.at[by - 1],
                    r.sz_recv.at[by - 1],
                    z_peers[by - 1],
                )
            )

    r.heads[z] = r.attended[rows_of(z), :]
    wide_whole()
    for by in range(1, NZ):
        block = r.heads.at[turn(z, -by, NZ)]
        remote(block, block, r.a_send.at[by - 1], r.a_recv.at[by - 1], z_peers[by - 1]).wait_recv()
    chunk = width // 4
    joined = jnp.concatenate([r.heads[index] for index in range(NZ)], axis=1)
    depth = joined.shape[1]

    def half_rows(plane):
        return pl.ds(pl.multiple_of(plane * own, own), own)

    def swap(step):
        sems = r.o_send.at[step], r.o_recv.at[step]
        return remote(r.out_send.at[step], r.out_recv.at[step], *sems, partner)

    for step in range(width // chunk):
        at = slice(step * chunk, (step + 1) * chunk)
        r.partial[step] = jnp.dot(
            joined, r.wide[:, :, at].reshape(depth, chunk), preferred_element_type=F32
        )
        r.out_send[step] = r.partial[step, half_rows(1 - x_hi), :].astype(BF16)
        sent.start(swap(step))
    send_student()
    for step in range(width // chunk):
        at = slice(step * chunk, (step + 1) * chunk)
        mine = r.partial[step, half_rows(x_hi), :] + r.my_tokens[:, at].astype(F32)
        swap(step).wait_recv()
        r.mixed[:, at] = (mine + r.out_recv[step].astype(F32)).astype(BF16)
    mixed = r.mixed[...]
    r.blocks[row] = (rms(mixed.astype(F32)) * r.mlp_gain[...]).astype(BF16)

    waited = []

    def units(zs):
        if not waited:
            loads[0].wait()
            loads[1].wait()
            waited.append(True)
        value = jnp.concatenate(
            [r.blocks[pl.ds(zz * 2, 2)].reshape(pair, width) for zz in zs], axis=0
        )
        gate = jnp.dot(value, r.w_gate[...], preferred_element_type=F32)
        up = jnp.dot(value, r.w_up[...], preferred_element_type=F32)
        found = (gate * jax.nn.sigmoid(gate) * up).astype(BF16)
        for at, zz in enumerate(zs):
            r.hidden[zz] = found[at * pair : (at + 1) * pair]

    def ready(distances):
        zs = []
        for by in distances:
            zs += [z] if by == 0 else [turn(z, by, NZ), turn(z, -by, NZ)]
        units(zs)

    fresh = [3, 4]

    def make(zs):
        if fresh:
            fresh.pop()
            units(zs)
        value = jnp.concatenate([r.hidden[zz] for zz in zs], axis=0)

        @pl.loop(0, width // chunk)
        def _(step):
            at = pl.ds(pl.multiple_of(step * chunk, chunk), chunk)
            out = jnp.dot(value, r.w_down[:, at], preferred_element_type=F32).astype(BF16)
            for index, zz in enumerate(zs):
                for plane in range(2):
                    top = index * pair + plane * own
                    r.parts[zz * 2 + plane, :, at] = out[top : top + own]

    scratch = (r.sbuf, r.rbuf, r.xbuf, r.xlast, r.xgot, r.r_send, r.r_recv, r.rx_send, r.rx_recv)
    begin_sum, rest_of_sum = mix_scatter(r.parts, make, scratch)
    loads[2].wait()
    mix_gather(
        r.blocks,
        lambda zz, plane: zz * 2 + plane,
        own // 2,
        (r.g_send, r.g_recv, r.gx_send, r.gx_recv),
        ready=ready,
        tail=begin_sum,
    )
    top, bottom, more = rest_of_sum()
    student_sum = r.s_out[z].astype(F32)
    for by in range(1, NZ):
        got = r.s_in.at[by - 1]
        remote(got, got, r.sz_send.at[by - 1], r.sz_recv.at[by - 1], z_peers[by - 1]).wait_recv()
        student_sum = student_sum + r.s_in[by - 1].astype(F32)
    predicted = r.student[my_rows, :].astype(F32) + student_sum
    teacher = r.mixed[...].astype(F32) + jnp.concatenate([top, bottom], axis=0)
    teacher = teacher.astype(BF16)
    r.teacher[...] = teacher
    loads[3].wait()
    target = jnp.dot(teacher, r.projector[...], preferred_element_type=F32)
    scaled = ((predicted - target) * total_rows ** (-0.5)).astype(BF16)

    def place(by, plane):
        return r.gathered.at[turn(z, by, NZ) * 2 + plane]

    def across(by, plane):
        block = place(by, plane)
        at = by % NZ
        return remote(block, block, r.px_send.at[at], r.px_recv.at[at], partner)

    def along(by, device):
        block = place(-by if device is None else 0, x_hi)
        sems = r.p_send.at[by - 1], r.p_recv.at[by - 1]
        return remote(block, block, *sems, z_peers[by - 1])

    r.gathered[row] = scaled
    for by in (4, 3, 5, 2, 6, 1, 7):
        sent.start(along(by, True))
    sent.start(across(0, x_hi))
    for by in (1, 7, 2, 6, 3, 5, 4):
        along(by, None).wait_recv()
        sent.start(across(-by, x_hi))
    for by, peer in enumerate(t_peers):
        sent.start(
            remote(
                r.teacher.at[:, pl.ds(pl.multiple_of(peer * HD, HD), HD)],
                r.columns.at[row],
                r.t_send.at[by],
                r.t_recv.at[by],
                (dp, peer),
            )
        )
    r.columns[row] = r.teacher[:, pl.ds(pl.multiple_of(tensor * HD, HD), HD)]
    for by in (0, 1, 7, 2, 6, 3, 5, 4):
        across(-by, 1 - x_hi).wait_recv()

    scaled = r.gathered[...].reshape(rows, -1)
    grad_hidden = lax.dot_general(
        scaled, r.s_down[...], (((1,), (1,)), ((), ())), preferred_element_type=F32
    )
    both = jnp.concatenate(
        [(grad_hidden * r.by_gate[...]).astype(BF16), (grad_hidden * r.by_up[...]).astype(BF16)],
        axis=1,
    )
    both = jnp.dot(r.normed_t[...], both, preferred_element_type=F32).astype(BF16)
    down = jnp.dot(r.hidden_t[...], scaled, preferred_element_type=F32).astype(BF16)
    count = grad_hidden.shape[1]
    r.grads[:, :own] = both[:, :count].reshape(size, own, count)
    r.grads[:, own:pair] = both[:, count:].reshape(size, own, count)
    down = jnp.concatenate([down[:, at : at + HD] for at in range(0, down.shape[1], HD)], axis=0)
    r.grads[:, pair : 3 * own] = down.reshape(size, own, HD)
    squares = scaled.astype(F32)
    squares = jnp.sum((squares * squares).reshape(-1, 8, scaled.shape[1]), axis=0)
    squares = sum(squares[:, at : at + HD] for at in range(0, scaled.shape[1], HD))
    high = squares.astype(BF16)
    low = (squares - high.astype(F32)).astype(BF16)
    both = jnp.concatenate([high, low], axis=0)
    r.grads[:, 3 * own :] = jnp.broadcast_to(both[None], (size,) + both.shape)

    def origin(by):
        return turn(dp, -(by + 1), size)

    r.inbox[dp] = r.grads[dp]
    for by, peer in enumerate(d_peers):
        sems = r.send1.at[by], r.recv1.at[by]
        sent.start(remote(r.grads.at[peer], r.inbox.at[dp], *sems, (peer, tensor)))
    for by, peer in enumerate(d_peers):
        block = r.inbox.at[origin(by)]
        remote(block, block, r.send1.at[by], r.recv1.at[by], (peer, tensor)).wait_recv()
    total = r.inbox[0].astype(F32)
    for index in range(1, size):
        total = total + r.inbox[index].astype(F32)
    r.sums[dp] = total[: 3 * own].astype(BF16)
    r.error[...] = total[3 * own : 3 * own + 8] + total[3 * own + 8 :]
    for by, peer in enumerate(d_peers):
        block = r.sums.at[dp]
        sent.start(remote(block, block, r.send2.at[by], r.recv2.at[by], (peer, tensor)))
    for by, peer in enumerate(t_peers):
        source = turn(tensor, -(by + 1), size)
        block = r.columns.at[lax.rem(source, NZ) * 2 + source // NZ]
        remote(block, block, r.t_send.at[by], r.t_recv.at[by], (dp, peer)).wait_recv()
    for by, peer in enumerate(d_peers):
        block = r.sums.at[origin(by)]
        remote(block, block, r.send2.at[by], r.recv2.at[by], (peer, tensor)).wait_recv()
    finish_exchange()
    sent.finish()
    more.finish()


def finish_body(columns_ref, sums_ref, squares_ref, teacher_ref, gate_ref, up_ref, down_ref, error_ref):
    rows, width = teacher_ref.shape
    own = rows // (2 * NZ)
    teacher_ref[...] = columns_ref[...].reshape(rows, width)
    sums = sums_ref[...].astype(F32)
    gate_ref[...] = sums[:, :own].reshape(-1, width)
    up_ref[...] = sums[:, own : 2 * own].reshape(-1, width)
    down = sums[:, 2 * own :].reshape(-1, width)
    for index in range(down.shape[0] // width):
        lanes = slice(index * width, (index + 1) * width)
        down_ref[:, lanes] = down[lanes]
    total = jnp.sum(jnp.sum(squares_ref[...], axis=0, keepdims=True), axis=1, keepdims=True)
    error_ref[...] = total / down_ref.shape[1]


def finish(columns, sums, squares):
    own, units = columns.shape[1:]
    rows = 2 * NZ * own
    shapes = (
        ((rows, units), BF16),
        ((rows, units), F32),
        ((rows, units), F32),
        ((units, rows), F32),
        ((1, 1), F32),
    )
    return pl.pallas_call(
        finish_body,
        out_shape=tuple(jax.ShapeDtypeStruct(shape, kind) for shape, kind in shapes),
        in_specs=[VM] * 3,
        out_specs=(VM,) * 5,
        compiler_params=pltpu.CompilerParams(vmem_limit_bytes=LIMIT),
        name="finish",
    )(columns, sums, squares)


def frequencies(head_dim):
    indices = jnp.arange(head_dim // 2).astype(F32)
    return jnp.exp(-jnp.log(500000.0) * 2.0 * indices / head_dim)


def local(
    tokens,
    series_ids,
    offsets,
    norm_gain,
    mlp_gain,
    w_query,
    w_key,
    w_value,
    w_out,
    w_gate,
    w_up,
    w_down,
    projector,
    student_in,
    s_gate,
    s_up,
    s_down,
):
    rows = tokens.shape[0]
    size = 2 * NZ
    own = rows // size
    width = projector.shape[0]
    narrow = student_in.shape[1]
    units = s_gate.shape[1]
    ff = w_gate.shape[1]
    frequency = frequencies(HD)
    frequency = jnp.concatenate([frequency, frequency])[None]
    inputs = {
        "tokens": tokens,
        "series": series_ids.reshape(-1, HD),
        "norm_gain": norm_gain[None],
        "offsets": offsets.reshape(-1, HD),
        "frequency": frequency,
        "w_query": w_query,
        "w_key": w_key,
        "w_value": w_value,
        "w_out": w_out,
        "mlp_gain": mlp_gain[None],
        "w_gate_hbm": w_gate,
        "w_up_hbm": w_up,
        "w_down_hbm": w_down,
        "projector_hbm": projector,
        "student": student_in,
        "s_gate": s_gate,
        "s_up": s_up,
        "s_down": s_down,
    }
    outputs = {
        "columns": ((size, own, HD), BF16),
        "sums": ((size, 3 * own, units), BF16),
        "error": ((8, HD), F32),
    }
    one = pltpu.SemaphoreType.DMA
    half = own // 2
    scratch = {
        "tok": pltpu.VMEM((size, rows, HD), BF16),
        "cosine": pltpu.VMEM((rows, HD), F32),
        "sine": pltpu.VMEM((rows, HD), F32),
        "normed": pltpu.VMEM((rows, width), BF16),
        "weights": pltpu.VMEM((width, 3 * HD), BF16),
        "query": pltpu.VMEM((rows, HD), BF16),
        "my_tokens": pltpu.VMEM((own, width), BF16),
        "part": pltpu.VMEM((2, NZ, own, narrow), BF16),
        "normed_t": pltpu.VMEM((narrow, rows), BF16),
        "hidden_t": pltpu.VMEM((units, rows), BF16),
        "by_gate": pltpu.VMEM((rows, units), F32),
        "by_up": pltpu.VMEM((rows, units), F32),
        "q_send": dma(2, 4, 3),
        "q_recv": dma(2, 4, 3),
        "qx_send": dma(9),
        "qx_recv": dma(9),
        "pairs": pltpu.VMEM((4 * NY, 2, rows, HD), BF16),
        "wide": pltpu.VMEM((NZ,) + w_out.shape, BF16),
        "start": pltpu.VMEM((rows, HD), jnp.int32),
        "peak": pltpu.VMEM((rows, HD), F32),
        "denom": pltpu.VMEM((rows, HD), F32),
        "accum": pltpu.VMEM((rows, HD), F32),
        "attended": pltpu.VMEM((rows, HD), BF16),
        "k_send": dma(9, 2),
        "k_recv": dma(9, 2),
        "c_send": dma(9),
        "c_recv": dma(9),
        "w_send": dma(2, 4, 2),
        "w_recv": dma(2, 4, 2),
        "wc_send": dma(7),
        "wc_recv": dma(7),
        "s_got": pltpu.VMEM((NZ, own, narrow), BF16),
        "s_out": pltpu.VMEM((NZ, own, narrow), BF16),
        "s_in": pltpu.VMEM((NZ - 1, own, narrow), BF16),
        "sx_send": one,
        "sx_recv": one,
        "sz_send": dma(7),
        "sz_recv": dma(7),
        "w_gate": pltpu.VMEM(w_gate.shape, BF16),
        "w_up": pltpu.VMEM(w_up.shape, BF16),
        "w_down": pltpu.VMEM(w_down.shape, BF16),
        "projector": pltpu.VMEM(projector.shape, BF16),
        "load_sem": dma(4),
        "heads": pltpu.VMEM((NZ, 2 * own, HD), BF16),
        "a_send": dma(7),
        "a_recv": dma(7),
        "out_send": pltpu.VMEM((4, own, width // 4), BF16),
        "out_recv": pltpu.VMEM((4, own, width // 4), BF16),
        "o_send": dma(4),
        "o_recv": dma(4),
        "partial": pltpu.VMEM((4, 2 * own, width // 4), F32),
        "mixed": pltpu.VMEM((own, width), BF16),
        "blocks": pltpu.VMEM((size, own, width), BF16),
        "hidden": pltpu.VMEM((NZ, 2 * own, ff), BF16),
        "parts": pltpu.VMEM((size, own, width), BF16),
        "g_send": dma(2, 4, 3),
        "g_recv": dma(2, 4, 3),
        "gx_send": dma(9),
        "gx_recv": dma(9),
    }
    names = ("sbuf", "rbuf", "xbuf", "xlast", "xgot", "r_send", "r_recv", "rx_send", "rx_recv")
    scratch.update(zip(names, scatter_scratch(half, width), strict=True))
    scratch.update(
        {
            "teacher": pltpu.VMEM((own, width), BF16),
            "gathered": pltpu.VMEM((size, own, narrow), BF16),
            "px_send": dma(8),
            "px_recv": dma(8),
            "p_send": dma(7),
            "p_recv": dma(7),
            "t_send": dma(size - 1),
            "t_recv": dma(size - 1),
            "grads": pltpu.VMEM((size, 3 * own + 16, units), BF16),
            "inbox": pltpu.VMEM((size, 3 * own + 16, units), BF16),
            "send1": dma(size - 1),
            "recv1": dma(size - 1),
            "send2": dma(size - 1),
            "recv2": dma(size - 1),
        }
    )
    far = pl.BlockSpec(memory_space=pl.ANY)
    columns, sums, squares = call(
        functools.partial(
            layer_body, (*inputs, *outputs, *scratch), rows * lax.axis_size("dp")
        ),
        "layer",
        1,
        tuple(inputs.values()),
        tuple(outputs.values()),
        list(scratch.values()),
        [far if name.endswith("_hbm") else VM for name in inputs],
    )
    teacher_out, grad_gate, grad_up, grad_down, error = finish(columns, sums, squares)
    return (teacher_out, grad_gate, grad_up, grad_down, error.reshape(()))


def solution(mesh):
    in_specs = (
        P("dp", "tensor"),
        P(),
        P("dp"),
        P(),
        P(),
        P(None, "tensor"),
        P(None, "tensor"),
        P(None, "tensor"),
        P("tensor", None),
        P(None, "tensor"),
        P(None, "tensor"),
        P("tensor", None),
        P(),
        P("dp", None),
        P(None, "tensor"),
        P(None, "tensor"),
        P("tensor", None),
    )
    out_specs = (P("dp", "tensor"), P(None, "tensor"), P(None, "tensor"), P("tensor", None), P())
    return jax.shard_map(local, mesh=mesh, in_specs=in_specs, out_specs=out_specs, check_vma=False)
```

```python
import functools

import jax
import jax.numpy as jnp
import numpy as np
from jax import lax
from jax.experimental import pallas as pl
from jax.experimental.pallas import tpu as pltpu
from jax.sharding import PartitionSpec as P

HD = 128
NZ = 8
NY = 4
MESH = pl.DeviceIdType.MESH
VM = pl.BlockSpec(memory_space=pltpu.VMEM)
LIMIT = 56 * 1024 * 1024
F32 = jnp.float32
BF16 = jnp.bfloat16


def params(collective_id):
    return pltpu.CompilerParams(
        collective_id=collective_id, has_side_effects=True, vmem_limit_bytes=LIMIT
    )


def remote(src, dst, send_sem, recv_sem, device):
    return pltpu.make_async_remote_copy(
        src_ref=src,
        dst_ref=dst,
        send_sem=send_sem,
        recv_sem=recv_sem,
        device_id=device,
        device_id_type=MESH,
    )


def greet(devices, meanwhile=None):
    barrier = pltpu.get_barrier_semaphore()
    for device in devices:
        pl.semaphore_signal(barrier, inc=1, device_id=device, device_id_type=MESH)
    if meanwhile is not None:
        meanwhile()
    pl.semaphore_wait(barrier, len(devices))


def places():
    dp, tensor = lax.axis_index("dp"), lax.axis_index("tensor")
    x_hi, z = tensor // NZ, lax.rem(tensor, NZ)
    return dp, tensor, x_hi, z


def turn(z, by, size):
    return lax.rem(z + by + size, size)


def dma(*shape):
    return pltpu.SemaphoreType.DMA(shape)


def call(body, name, collective_id, inputs, outputs, scratch, specs=None):
    return pl.pallas_call(
        body,
        out_shape=tuple(jax.ShapeDtypeStruct(shape, kind) for shape, kind in outputs),
        in_specs=specs or [VM] * len(inputs),
        out_specs=tuple([VM] * len(outputs)),
        scratch_shapes=scratch,
        compiler_params=params(collective_id),
        name=name,
    )(*inputs)


class Sent:
    def __init__(self):
        self.copies = []

    def start(self, copy):
        copy.start()
        self.copies.append(copy)

    def finish(self):
        for copy in self.copies:
            copy.wait_send()


def on_ring(way, far, sub):
    return far < 4 or (way == 1) == (sub == 1)


def towards(way, by):
    return by if way == 0 else -by


def mix_gather(ref, at, half, sems, hook=lambda step: None, ready=None, tail=None):
    ring_send, ring_recv, x_send, x_recv = sems
    dp, tensor, x_hi, z = places()
    partner = (dp, (1 - x_hi) * NZ + z)
    nexts = tuple((dp, x_hi * NZ + turn(z, by, NZ)) for by in (1, -1))
    sent = Sent()

    def view(zz, sub):
        plane = x_hi if sub < 2 else 1 - x_hi
        return ref.at[at(zz, plane), pl.ds((sub % 2) * half, half)]

    def ring(way, far, sub, hops):
        block = view(turn(z, -towards(way, hops), NZ), sub)
        sems = ring_send.at[way, far - 1, sub], ring_recv.at[way, far - 1, sub]
        return remote(block, block, *sems, nexts[way])

    def cross(zz, sub, slot):
        block = view(zz, sub)
        return remote(block, block, x_send.at[slot], x_recv.at[slot], partner)

    def slot(way, far):
        return 1 + far + 3 * way if way == 0 else 4 + far

    def crossed(far):
        if far == 0:
            cross(z, 3, 1).wait_recv()
        for way in range(2):
            if 0 < far < 4 + way:
                cross(turn(z, -towards(way, far), NZ), 3, slot(way, far)).wait_recv()

    sent.start(cross(z, 0, 0))
    for sub in range(2):
        for way in range(2):
            sent.start(ring(way, 1, sub, 0))
    sent.start(cross(z, 1, 1))
    hook(0)
    cross(z, 2, 0).wait_recv()
    for way in range(2):
        sent.start(ring(way, 1, 2, 0))
    for far in range(2, 5):
        hook(far - 1)
        for sub in range(3):
            for way in range(2):
                ring(way, far - 1, sub, far - 1).wait_recv()
                if on_ring(way, far, sub):
                    sent.start(ring(way, far, sub, far - 1))
                if sub == 1:
                    origin = turn(z, -towards(way, far - 1), NZ)
                    sent.start(cross(origin, 1, slot(way, far - 1)))
        if far == 3:
            crossed(0)
            crossed(1)
            if ready:
                ready((0, 1))
        if far == 4:
            crossed(2)
            if ready:
                ready((2,))
    ring(1, 4, 1, 4).wait_recv()
    sent.start(cross(turn(z, 4, NZ), 1, slot(1, 4)))
    crossed(3)
    if tail:
        tail()
    for sub in (0, 2):
        ring(0, 4, sub, 4).wait_recv()
    crossed(4)
    sent.finish()


def scatter_scratch(half, width):
    return [
        pltpu.VMEM((2, 4, 3, half, width), BF16),
        pltpu.VMEM((2, 4, 3, half, width), BF16),
        pltpu.VMEM((8, half, width), BF16),
        pltpu.VMEM((half, width), BF16),
        pltpu.VMEM((half, width), BF16),
        dma(2, 4, 3),
        dma(2, 4, 3),
        dma(9),
        dma(9),
    ]


def mix_scatter(part, make, scratch):
    sbuf, rbuf, xbuf, xlast, xgot, ring_send, ring_recv, x_send, x_recv = scratch
    half = sbuf.shape[3]
    dp, tensor, x_hi, z = places()
    partner = (dp, (1 - x_hi) * NZ + z)
    nexts = tuple((dp, x_hi * NZ + turn(z, by, NZ)) for by in (1, -1))
    sent = Sent()

    def view(zz, sub):
        plane = x_hi if sub < 2 else 1 - x_hi
        return part.at[zz * 2 + plane, pl.ds((sub % 2) * half, half)]

    def slot(way, far):
        return 7 if far == 4 else 1 + 3 * way + far - 1

    def cross(zz, at):
        return remote(view(zz, 3), xbuf.at[at], x_send.at[at], x_recv.at[at], partner)

    def ring(way, far, sub, source):
        sems = ring_send.at[way, far - 1, sub], ring_recv.at[way, far - 1, sub]
        return remote(source, rbuf.at[way, far - 1, sub], *sems, nexts[way])

    def arrived(way, far, sub):
        ring(way, far, sub, rbuf.at[way, far - 1, sub]).wait_recv()
        return rbuf[way, far - 1, sub].astype(F32)

    def crossed(at):
        cross(z, at).wait_recv()
        return xbuf[at].astype(F32)

    def send(way, far, sub):
        source = view(turn(z, towards(way, far), NZ), sub)
        extra = []
        if far < 4 and on_ring(way, far + 1, sub):
            extra.append(arrived(way, far + 1, sub))
        if sub == 1:
            extra.append(crossed(slot(way, far)))
        if extra:
            total = source[...].astype(F32)
            for one in extra:
                total = total + one
            sbuf[way, far - 1, sub] = total.astype(BF16)
            source = sbuf.at[way, far - 1, sub]
        sent.start(ring(way, far, sub, source))

    def make_pair(far):
        pair = [turn(z, by, NZ) for by in (far, -far)]
        make(pair)
        for way in range(2):
            sent.start(cross(pair[way], slot(way, far)))

    def begin():
        make_pair(3)
        for sub in (0, 2):
            send(1, 3, sub)

    def rest():
        far4 = turn(z, 4, NZ)
        make([far4])
        sent.start(cross(far4, 7))
        for sub in (0, 2):
            send(0, 4, sub)
        make_pair(2)
        send(1, 4, 1)
        for sub in (1, 2, 0):
            send(0, 3, sub)
        send(1, 3, 1)
        make_pair(1)
        for sub in (2, 0, 1):
            for way in range(2):
                send(way, 2, sub)
        make([z])
        sent.start(cross(z, 0))
        for sub in (2, 0, 1):
            for way in range(2):
                send(way, 1, sub)
        return last_sums()

    def total(sub):
        return view(z, sub)[...].astype(F32) + arrived(0, 1, sub) + arrived(1, 1, sub)

    def last_sums():
        xlast[...] = total(2).astype(BF16)
        last = remote(xlast, xgot, x_send.at[8], x_recv.at[8], partner)
        sent.start(last)
        second = total(1) + crossed(0)
        first = total(0)

        def other():
            last.wait_recv()
            return first + xgot[...].astype(F32)

        return other, second, sent

    return begin, rest


def rms(values):
    return values * lax.rsqrt(jnp.mean(values * values, axis=-1, keepdims=True) + 1e-05)


def student(r, step):
    own = r.student.shape[0] // (2 * NZ)
    at = pl.ds(step * 128, 128)
    values = rms(r.student[at, :].astype(F32))
    r.normed_t[:, at] = values.T.astype(BF16)
    values = values.astype(BF16)
    gate = jnp.dot(values, r.s_gate[...], preferred_element_type=F32)
    up = jnp.dot(values, r.s_up[...], preferred_element_type=F32)
    sigmoid = jax.nn.sigmoid(gate)
    r.by_gate[at, :] = up * sigmoid * (1.0 + gate * (1.0 - sigmoid))
    r.by_up[at, :] = gate * sigmoid
    hidden = gate * sigmoid * up
    r.hidden_t[:, at] = hidden.T.astype(BF16)
    out = jnp.dot(hidden.astype(BF16), r.s_down[...], preferred_element_type=F32)
    for index in range(128 // own):
        block = out[index * own : (index + 1) * own].astype(BF16)
        r.part[index % 2, step * (64 // own) + index // 2] = block


def project(r, after, weights_there):
    dp, tensor, x_hi, z = places()
    rows = r.tok.shape[1]
    own = rows // (2 * NZ)

    def hook(step):
        if step == 0:
            weights_there()
        if step == 3:
            student(r, 3)

    tile = 256
    started = []

    def add(distances):
        places_now = []
        for by in distances:
            for zz in [z] if by == 0 else [turn(z, 4, NZ)] if by == 4 else [turn(z, by, NZ), turn(z, -by, NZ)]:
                places_now += [zz, NZ + zz]
        weights = jnp.concatenate(
            [r.weights[pl.ds(pl.multiple_of(at * HD, HD), HD), :] for at in places_now], axis=0
        )
        for step in range(rows // tile):
            at = pl.ds(step * tile, tile)
            square = None if not started else r.square[at, :]
            values = []
            for index in places_now:
                value = r.tok[index, at, :].astype(F32)
                square = value * value if square is None else square + value * value
                values.append((value * r.norm_gain[pl.ds(index, 1), :]).astype(BF16))
            r.square[at, :] = square
            out = jnp.dot(jnp.concatenate(values, axis=1), weights, preferred_element_type=F32)
            r.product[at, :] = out if not started else r.product[at, :] + out
        started.append(True)

    mix_gather(
        r.tok,
        lambda zz, plane: plane * NZ + zz,
        rows // 2,
        (r.q_send, r.q_recv, r.qx_send, r.qx_recv),
        hook,
        ready=add,
        tail=lambda: add((3,)),
    )
    after()
    add((4,))
    for step in range(rows // tile):
        at = pl.ds(step * tile, tile)
        mean = jnp.sum(r.square[at, :], axis=1, keepdims=True) / (2 * NZ * HD)
        out = r.product[at, :] * lax.rsqrt(mean + 1e-05)
        cosine, sine = r.cosine[at, :], r.sine[at, :]

        def rotary(values):
            return (values * cosine + pltpu.roll(values, HD // 2, 1) * sine).astype(BF16)

        r.pairs[dp, 0, at, :] = rotary(out[:, HD : 2 * HD])
        r.pairs[dp, 1, at, :] = out[:, 2 * HD :].astype(BF16)
        r.query[at, :] = rotary(out[:, :HD])


def keep_tokens(r):
    _, _, x_hi, z = places()
    own = r.my_tokens.shape[0]
    my_rows = pl.multiple_of((z * 2 + x_hi) * own, own)
    for index in range(2 * NZ):
        r.my_tokens[:, index * HD : (index + 1) * HD] = r.tok[index, pl.ds(my_rows, own)]


def find_starts(r):
    dp = lax.axis_index("dp")
    rows = r.start.shape[0]
    position = (dp * rows + lax.broadcasted_iota(jnp.int32, r.start.shape, 0)).astype(F32)
    found = jnp.zeros(r.start.shape, F32)
    for number in range(1, 8):
        before = jnp.where(r.series[...] < number, 1.0, 0.0)
        begin = jnp.sum(jnp.sum(before, axis=0, keepdims=True), axis=1, keepdims=True)
        found = jnp.where(begin <= position, jnp.maximum(found, begin), found)
    r.start[...] = found.astype(jnp.int32)


def prepare(r, loaded):
    loaded("series")
    find_starts(r)
    loaded("offsets", "frequency")
    for step in range(r.offsets.shape[0]):
        at = pl.ds(step * HD, HD)
        offset = jnp.broadcast_to(r.offsets[step : step + 1, :].astype(F32), (HD, HD)).T
        angle = offset * r.frequency[...]
        lane = lax.broadcasted_iota(jnp.int32, (HD, HD), 1)
        r.cosine[at, :] = jnp.cos(angle)
        sine = jnp.sin(angle)
        r.sine[at, :] = jnp.where(lane < HD // 2, -sine, sine)
    loaded("student", "s_gate", "s_up", "s_down")
    for step in range(3):
        student(r, step)


R1, R2, R3, X0, X1, H1, H2, H3, OWN = range(9)


class Refs:
    def __init__(self, names, refs):
        for name, ref in zip(names, refs, strict=True):
            setattr(self, name, ref)


def attend(r, mine, j, diagonal, tile=256):
    rows, span = r.query.shape[0], r.pairs.shape[2]
    factor = HD ** (-0.5) * 1.4426950408889634
    key, value = r.pairs[j, 0], r.pairs[j, 1]
    for index in range(rows // tile):
        at = slice(index * tile, (index + 1) * tile)
        scores = lax.dot_general(
            r.query[at, :], key, (((1,), (1,)), ((), ())), preferred_element_type=F32
        )
        column = lax.broadcasted_iota(jnp.int32, (tile, span), 1)
        allowed = column >= r.start[at, :1] - j * span
        if diagonal:
            row = index * tile + lax.broadcasted_iota(jnp.int32, (tile, span), 0)
            allowed = allowed & (column <= row)
        scores = jnp.where(allowed, scores, -1e30)
        top = jnp.max(scores, axis=1, keepdims=True)
        if not diagonal:
            old = r.peak[at, :1]
            top = jnp.maximum(old, top)
        weights = jnp.exp2((scores - top) * factor)
        denom = jnp.sum(weights, axis=1, keepdims=True)
        accum = jnp.dot(weights.astype(BF16), value, preferred_element_type=F32)
        if not diagonal:
            scale = jnp.exp2((old - top) * factor)
            denom = denom + r.denom[at, :1] * scale
            accum = accum + r.accum[at, :] * scale
        r.peak[at, :] = jnp.broadcast_to(top, (tile, HD))
        r.denom[at, :] = jnp.broadcast_to(denom, (tile, HD))
        r.accum[at, :] = accum


def exchange(r, sent):
    dp, tensor, x_hi, z = places()
    x_lo, y, core = dp // (2 * NY), lax.rem(dp // 2, NY), lax.rem(dp, 2)

    def index(xx, yy, cc):
        return xx * 2 * NY + yy * 2 + cc

    k_partner = (index(1 - x_lo, y, core), tensor)
    sibling = (index(x_lo, y, 1 - core), tensor)
    up, down = ((index(x_lo, turn(y, by, NY), core), tensor) for by in (1, -1))
    z_peers = [(dp, x_hi * NZ + turn(z, by, NZ)) for by in range(1, NZ)]
    z_nexts = (z_peers[0], z_peers[-1])
    s_partner = (dp, (1 - x_hi) * NZ + z)
    deep = r.wide.shape[1] // 4
    first, second = x_lo == 0, x_lo == 1

    def chip(by):
        return turn(y, by, NY)

    arrives = {
        R1: (y >= 1, x_lo, chip(-1)),
        R2: (y >= 2, x_lo, chip(-2)),
        R3: (y == 3, x_lo, chip(1)),
        X0: (second, 0, y),
        X1: (second & (y >= 1), 0, chip(-1)),
        H1: (second & (y <= 2), 0, chip(1)),
        H2: (second & (y <= 1), 0, chip(2)),
        H3: (second & (y == 0), 0, chip(-1)),
        OWN: (None, x_lo, y),
    }

    def k_copy(event, part, xx, yy, device):
        block = r.pairs.at[index(xx, yy, core), part]
        return remote(block, block, r.k_send.at[event, part], r.k_recv.at[event, part], device)

    later = []

    def when(condition, copy):
        @pl.when(condition)
        def _():
            copy.start()

        later.append((condition, copy))

    def k_wait(event, part):
        condition, xx, yy = arrives[event]

        @pl.when(condition)
        def _():
            k_copy(event, part, xx, yy, up).wait_recv()

    def c_copy(event, cc):
        _, xx, yy = arrives[event]
        block = r.pairs.at[index(xx, yy, cc)]
        return remote(block, block, r.c_send.at[event], r.c_recv.at[event], sibling)

    def share(event):
        condition = arrives[event][0]
        if condition is None:
            sent.start(c_copy(event, core))
        else:
            when(condition, c_copy(event, core))

    def shared(*events):
        for event in events:
            condition = arrives[event][0]
            if condition is None:
                c_copy(event, 1 - core).wait_recv()
            else:

                @pl.when(condition)
                def _(event=event):
                    c_copy(event, 1 - core).wait_recv()

    def work(*events):
        found = []
        for event in events:
            condition, xx, yy = arrives[event]
            for cc in (core, 1 - core):
                if event == OWN and cc is core:
                    continue
                j = index(xx, yy, cc)
                needed = (j < dp) & (j >= dp - 10)
                found.append((j, needed if condition is None else needed & condition))

        @pl.loop(0, len(found))
        def _(step):
            j, needed = found[0]
            needed = needed.astype(jnp.int32)
            for number, (jj, wanted) in enumerate(found[1:], 1):
                j = jnp.where(step == number, jj, j)
                needed = jnp.where(step == number, wanted.astype(jnp.int32), needed)

            @pl.when(needed == 1)
            def _():
                attend(r, dp, j, False)

    def w_copy(way, far, sub, hops):
        top = pl.multiple_of(core * 2 * deep + sub * deep, deep)
        block = r.wide.at[turn(z, -towards(way, hops), NZ), pl.ds(top, deep)]
        sems = r.w_send.at[way, far - 1, sub], r.w_recv.at[way, far - 1, sub]
        return remote(block, block, *sems, z_nexts[way])

    def w_share(by, slot, cc):
        top = pl.multiple_of(cc * 2 * deep, 2 * deep)
        block = r.wide.at[turn(z, by, NZ), pl.ds(top, 2 * deep)]
        return remote(block, block, r.wc_send.at[slot], r.wc_recv.at[slot], sibling)

    def w_forward(far, sub):
        for way in range(2):
            if far < 4 or sub == way:
                w_copy(way, far, sub, far).wait_recv()
            if far < 3 or (far == 3 and sub == way):
                sent.start(w_copy(way, far + 1, sub, far))

    def w_spread(far):
        for way in range(2):
            sent.start(w_share(towards(way, -far), 2 * (far - 1) + way, core))

    def begin_wide():
        for sub in range(2):
            for way in range(2):
                sent.start(w_copy(way, 1, sub, 0))

    def arrive():
        for part in range(2):
            when(y <= 2, k_copy(R1, part, x_lo, y, up))
            when(y == 0, k_copy(R3, part, x_lo, y, down))
            when(first, k_copy(X0, part, 0, y, k_partner))
        share(OWN)
        s_cross = remote(r.part.at[1 - x_hi], r.s_got, r.sx_send, r.sx_recv, s_partner)
        sent.start(s_cross)
        w_forward(1, 0)
        w_forward(1, 1)
        w_spread(1)
        attend(r, dp, dp, True)
        for part in range(2):
            k_wait(R1, part)
            when((y >= 1) & (y <= 2), k_copy(R2, part, x_lo, chip(-1), up))
            when(first & (y >= 1), k_copy(X1, part, 0, chip(-1), k_partner))
            k_wait(X0, part)
            when(second & (y >= 1), k_copy(H1, part, 0, y, down))
            when(second & (y == 3), k_copy(H3, part, 0, y, up))
            w_forward(2, part)
        share(R1)
        share(X0)
        w_spread(2)
        k_wait(R3, 0)
        k_wait(R3, 1)
        share(R3)
        s_cross.wait_recv()
        r.s_out[...] = (r.part[x_hi].astype(F32) + r.s_got[...].astype(F32)).astype(BF16)
        shared(OWN, R1)
        work(OWN, R1)
        for part in range(2):
            k_wait(H1, part)
            when(second & (y >= 1) & (y <= 2), k_copy(H2, part, 0, chip(1), down))
        share(H1)
        w_forward(3, 0)
        shared(X0)
        work(X0)
        w_forward(3, 1)
        w_spread(3)
        for event in (X1, R2, H3):
            k_wait(event, 0)
            k_wait(event, 1)
            share(event)
        shared(R3, H1)
        work(R3, H1)
        w_forward(4, 0)
        w_forward(4, 1)
        sent.start(w_share(4, 6, core))
        k_wait(H2, 0)
        k_wait(H2, 1)
        share(H2)
        shared(X1, R2, H3)
        work(X1, R2, H3)
        shared(H2)
        work(H2)
        r.attended[...] = (r.accum[...] / r.denom[...]).astype(BF16)

    def finish():
        for condition, copy in later:

            @pl.when(condition)
            def _(copy=copy):
                copy.wait_send()

    def wide_whole():
        for slot, by in enumerate([-1, 1, -2, 2, -3, 3, 4]):
            w_share(by, slot, 1 - core).wait_recv()

    return begin_wide, arrive, wide_whole, finish


ORDER = (
    "tokens",
    "series",
    "offsets",
    "frequency",
    "student",
    "s_gate",
    "s_up",
    "s_down",
    "w_query",
    "w_key",
    "w_value",
    "norm_gain",
    "w_out",
    "mlp_gain",
    "w_gate",
    "w_up",
    "w_down",
    "projector",
)


def layer_body(names, total_rows, *refs):
    r = Refs(names, refs)
    dp, tensor, x_hi, z = places()
    size = 2 * NZ
    rows, width = r.tok.shape[1], r.w_gate.shape[0]
    own = rows // size
    pair = 2 * own
    row = z * 2 + x_hi
    my_rows = pl.ds(pl.multiple_of(row * own, own), own)
    partner = (dp, (1 - x_hi) * NZ + z)
    z_peers = [(dp, x_hi * NZ + turn(z, by, NZ)) for by in range(1, NZ)]
    t_peers = [turn(tensor, by, size) for by in range(1, size)]
    d_peers = [turn(dp, by, size) for by in range(1, size)]
    loads = {}
    near = {
        "tokens": r.tok.at[tensor],
        "w_query": r.weights.at[:, pl.ds(0, HD)],
        "w_key": r.weights.at[:, pl.ds(HD, HD)],
        "w_value": r.weights.at[:, pl.ds(2 * HD, HD)],
        "w_out": r.wide.at[z],
    }
    for index, name in enumerate(ORDER):
        target = near[name] if name in near else getattr(r, name)
        loads[name] = pltpu.make_async_copy(
            getattr(r, name + "_hbm"), target, r.load_sem.at[index]
        )
        loads[name].start()

    def loaded(*names):
        for name in names:
            loads.pop(name).wait()

    greet(
        [(dp, peer) for peer in t_peers] + [(peer, tensor) for peer in d_peers],
        lambda: prepare(r, loaded),
    )
    sent = Sent()
    begin_wide, arrive, wide_whole, finish_exchange = exchange(r, sent)
    loaded("tokens")

    def after():
        loaded("w_out")
        begin_wide()

    project(r, after, lambda: loaded("w_query", "w_key", "w_value", "norm_gain"))
    arrive()

    def rows_of(zz):
        return pl.ds(pl.multiple_of(zz * pair, pair), pair)

    for by in range(1, NZ):
        sent.start(
            remote(
                r.attended.at[rows_of(turn(z, by, NZ))],
                r.heads.at[z],
                r.a_send.at[by - 1],
                r.a_recv.at[by - 1],
                z_peers[by - 1],
            )
        )
    def send_student():
        for by in range(1, NZ):
            sent.start(
                remote(
                    r.s_out.at[turn(z, by, NZ)],
                    r.s_in.at[by - 1],
                    r.sz_send.at[by - 1],
                    r.sz_recv.at[by - 1],
                    z_peers[by - 1],
                )
            )

    r.heads[z] = r.attended[rows_of(z), :]
    wide_whole()
    for by in range(1, NZ):
        block = r.heads.at[turn(z, -by, NZ)]
        remote(block, block, r.a_send.at[by - 1], r.a_recv.at[by - 1], z_peers[by - 1]).wait_recv()
    chunk = width // 4
    joined = jnp.concatenate([r.heads[index] for index in range(NZ)], axis=1)
    depth = joined.shape[1]

    def half_rows(plane):
        return pl.ds(pl.multiple_of(plane * own, own), own)

    def swap(step):
        sems = r.o_send.at[step], r.o_recv.at[step]
        return remote(r.out_send.at[step], r.out_recv.at[step], *sems, partner)

    for step in range(width // chunk):
        at = slice(step * chunk, (step + 1) * chunk)
        r.partial[step] = jnp.dot(
            joined, r.wide[:, :, at].reshape(depth, chunk), preferred_element_type=F32
        )
        r.out_send[step] = r.partial[step, half_rows(1 - x_hi), :].astype(BF16)
        sent.start(swap(step))
    send_student()
    keep_tokens(r)
    for step in range(width // chunk):
        at = slice(step * chunk, (step + 1) * chunk)
        mine = r.partial[step, half_rows(x_hi), :] + r.my_tokens[:, at].astype(F32)
        swap(step).wait_recv()
        r.mixed[:, at] = (mine + r.out_recv[step].astype(F32)).astype(BF16)
    mixed = r.mixed[...]
    loaded("mlp_gain")
    r.blocks[row] = (rms(mixed.astype(F32)) * r.mlp_gain[...]).astype(BF16)

    waited = []

    def units(zs):
        if not waited:
            loaded("w_gate", "w_up")
            waited.append(True)
        value = jnp.concatenate(
            [r.blocks[pl.ds(zz * 2, 2)].reshape(pair, width) for zz in zs], axis=0
        )
        gate = jnp.dot(value, r.w_gate[...], preferred_element_type=F32)
        up = jnp.dot(value, r.w_up[...], preferred_element_type=F32)
        found = (gate * jax.nn.sigmoid(gate) * up).astype(BF16)
        for at, zz in enumerate(zs):
            r.hidden[zz] = found[at * pair : (at + 1) * pair]

    def predict():
        student_sum = r.s_out[z].astype(F32)
        for by in range(1, NZ):
            got = r.s_in.at[by - 1]
            sems = r.sz_send.at[by - 1], r.sz_recv.at[by - 1]
            remote(got, got, *sems, z_peers[by - 1]).wait_recv()
            student_sum = student_sum + r.s_in[by - 1].astype(F32)
        r.predicted[...] = r.student[my_rows, :].astype(F32) + student_sum

    def ready(distances):
        zs = []
        for by in distances:
            zs += [z] if by == 0 else [turn(z, by, NZ), turn(z, -by, NZ)]
        units(zs)
        if 2 in distances:
            predict()

    fresh = [3, 4]

    def make(zs):
        if fresh:
            fresh.pop()
            units(zs)
        value = jnp.concatenate([r.hidden[zz] for zz in zs], axis=0)

        @pl.loop(0, width // chunk)
        def _(step):
            at = pl.ds(pl.multiple_of(step * chunk, chunk), chunk)
            out = jnp.dot(value, r.w_down[:, at], preferred_element_type=F32).astype(BF16)
            for index, zz in enumerate(zs):
                for plane in range(2):
                    top = index * pair + plane * own
                    r.parts[zz * 2 + plane, :, at] = out[top : top + own]

    scratch = (r.sbuf, r.rbuf, r.xbuf, r.xlast, r.xgot, r.r_send, r.r_recv, r.rx_send, r.rx_recv)
    begin_sum, rest_of_sum = mix_scatter(r.parts, make, scratch)
    loaded("w_down")
    mix_gather(
        r.blocks,
        lambda zz, plane: zz * 2 + plane,
        own // 2,
        (r.g_send, r.g_recv, r.gx_send, r.gx_recv),
        ready=ready,
        tail=begin_sum,
    )
    top, bottom, more = rest_of_sum()
    loaded("projector")

    def last_rows(first, summed):
        at = slice(first, first + own // 2)
        teacher = (r.mixed[at, :].astype(F32) + summed).astype(BF16)
        r.teacher[at, :] = teacher
        target = jnp.dot(teacher, r.projector[...], preferred_element_type=F32)
        scaled = (r.predicted[at, :] - target) * total_rows ** (-0.5)
        r.gathered[row, at, :] = scaled.astype(BF16)

    last_rows(own // 2, bottom)
    last_rows(0, top())

    def place(by, plane):
        return r.gathered.at[turn(z, by, NZ) * 2 + plane]

    def across(by, plane):
        block = place(by, plane)
        at = by % NZ
        return remote(block, block, r.px_send.at[at], r.px_recv.at[at], partner)

    def along(by, device):
        block = place(-by if device is None else 0, x_hi)
        sems = r.p_send.at[by - 1], r.p_recv.at[by - 1]
        return remote(block, block, *sems, z_peers[by - 1])

    for by in (4, 3, 5, 2, 6, 1, 7):
        sent.start(along(by, True))
    sent.start(across(0, x_hi))
    for by in (1, 7, 2, 6, 3, 5, 4):
        along(by, None).wait_recv()
        sent.start(across(-by, x_hi))
    for by, peer in enumerate(t_peers):
        sent.start(
            remote(
                r.teacher.at[:, pl.ds(pl.multiple_of(peer * HD, HD), HD)],
                r.columns.at[row],
                r.t_send.at[by],
                r.t_recv.at[by],
                (dp, peer),
            )
        )
    r.columns[row] = r.teacher[:, pl.ds(pl.multiple_of(tensor * HD, HD), HD)]
    for by in (0, 1, 7, 2, 6, 3, 5, 4):
        across(-by, 1 - x_hi).wait_recv()

    scaled = r.gathered[...].reshape(rows, -1)
    grad_hidden = lax.dot_general(
        scaled, r.s_down[...], (((1,), (1,)), ((), ())), preferred_element_type=F32
    )
    both = jnp.concatenate(
        [(grad_hidden * r.by_gate[...]).astype(BF16), (grad_hidden * r.by_up[...]).astype(BF16)],
        axis=1,
    )
    both = jnp.dot(r.normed_t[...], both, preferred_element_type=F32).astype(BF16)
    down = jnp.dot(r.hidden_t[...], scaled, preferred_element_type=F32).astype(BF16)
    count = grad_hidden.shape[1]
    r.grads[:, :own] = both[:, :count].reshape(size, own, count)
    r.grads[:, own:pair] = both[:, count:].reshape(size, own, count)
    down = jnp.concatenate([down[:, at : at + HD] for at in range(0, down.shape[1], HD)], axis=0)
    r.grads[:, pair : 3 * own] = down.reshape(size, own, HD)
    squares = scaled.astype(F32)
    squares = jnp.sum((squares * squares).reshape(-1, 8, scaled.shape[1]), axis=0)
    squares = sum(squares[:, at : at + HD] for at in range(0, scaled.shape[1], HD))
    high = squares.astype(BF16)
    low = (squares - high.astype(F32)).astype(BF16)
    both = jnp.concatenate([high, low], axis=0)
    r.grads[:, 3 * own :] = jnp.broadcast_to(both[None], (size,) + both.shape)

    def origin(by):
        return turn(dp, -(by + 1), size)

    r.inbox[dp] = r.grads[dp]
    for by, peer in enumerate(d_peers):
        sems = r.send1.at[by], r.recv1.at[by]
        sent.start(remote(r.grads.at[peer], r.inbox.at[dp], *sems, (peer, tensor)))
    for by, peer in enumerate(d_peers):
        block = r.inbox.at[origin(by)]
        remote(block, block, r.send1.at[by], r.recv1.at[by], (peer, tensor)).wait_recv()
    total = r.inbox[0].astype(F32)
    for index in range(1, size):
        total = total + r.inbox[index].astype(F32)
    r.sums[dp] = total[: 3 * own].astype(BF16)
    r.error[...] = total[3 * own : 3 * own + 8] + total[3 * own + 8 :]
    for by, peer in enumerate(d_peers):
        block = r.sums.at[dp]
        sent.start(remote(block, block, r.send2.at[by], r.recv2.at[by], (peer, tensor)))
    for by, peer in enumerate(t_peers):
        source = turn(tensor, -(by + 1), size)
        block = r.columns.at[lax.rem(source, NZ) * 2 + source // NZ]
        remote(block, block, r.t_send.at[by], r.t_recv.at[by], (dp, peer)).wait_recv()
    for by, peer in enumerate(d_peers):
        block = r.sums.at[origin(by)]
        remote(block, block, r.send2.at[by], r.recv2.at[by], (peer, tensor)).wait_recv()
    finish_exchange()
    sent.finish()
    more.finish()


def finish_body(columns_ref, sums_ref, squares_ref, teacher_ref, gate_ref, up_ref, down_ref, error_ref):
    rows, width = teacher_ref.shape
    own = rows // (2 * NZ)
    teacher_ref[...] = columns_ref[...].reshape(rows, width)
    sums = sums_ref[...].astype(F32)
    gate_ref[...] = sums[:, :own].reshape(-1, width)
    up_ref[...] = sums[:, own : 2 * own].reshape(-1, width)
    down = sums[:, 2 * own :].reshape(-1, width)
    for index in range(down.shape[0] // width):
        lanes = slice(index * width, (index + 1) * width)
        down_ref[:, lanes] = down[lanes]
    total = jnp.sum(jnp.sum(squares_ref[...], axis=0, keepdims=True), axis=1, keepdims=True)
    error_ref[...] = total / down_ref.shape[1]


def finish(columns, sums, squares):
    own, units = columns.shape[1:]
    rows = 2 * NZ * own
    shapes = (
        ((rows, units), BF16),
        ((rows, units), F32),
        ((rows, units), F32),
        ((units, rows), F32),
        ((1, 1), F32),
    )
    return pl.pallas_call(
        finish_body,
        out_shape=tuple(jax.ShapeDtypeStruct(shape, kind) for shape, kind in shapes),
        in_specs=[VM] * 3,
        out_specs=(VM,) * 5,
        compiler_params=pltpu.CompilerParams(vmem_limit_bytes=LIMIT),
        name="finish",
    )(columns, sums, squares)


def frequencies(head_dim):
    indices = np.arange(head_dim // 2)
    found = np.exp(-np.log(500000.0) * 2.0 * indices / head_dim).astype(np.float32)
    return np.concatenate([found, found])[None]


def local(
    tokens,
    series_ids,
    offsets,
    norm_gain,
    mlp_gain,
    w_query,
    w_key,
    w_value,
    w_out,
    w_gate,
    w_up,
    w_down,
    projector,
    student_in,
    s_gate,
    s_up,
    s_down,
):
    rows = tokens.shape[0]
    size = 2 * NZ
    own = rows // size
    width = projector.shape[0]
    narrow = student_in.shape[1]
    units = s_gate.shape[1]
    ff = w_gate.shape[1]
    frequency = jnp.asarray(frequencies(HD))
    inputs = {
        "tokens": tokens,
        "series": series_ids.reshape(-1, HD),
        "norm_gain": norm_gain.reshape(-1, HD),
        "offsets": offsets.reshape(-1, HD),
        "frequency": frequency,
        "w_query": w_query,
        "w_key": w_key,
        "w_value": w_value,
        "w_out": w_out,
        "mlp_gain": mlp_gain[None],
        "w_gate": w_gate,
        "w_up": w_up,
        "w_down": w_down,
        "projector": projector,
        "student": student_in,
        "s_gate": s_gate,
        "s_up": s_up,
        "s_down": s_down,
    }
    outputs = {
        "columns": ((size, own, HD), BF16),
        "sums": ((size, 3 * own, units), BF16),
        "error": ((8, HD), F32),
    }
    one = pltpu.SemaphoreType.DMA
    half = own // 2
    scratch = {
        "tok": pltpu.VMEM((size, rows, HD), BF16),
        "cosine": pltpu.VMEM((rows, HD), F32),
        "sine": pltpu.VMEM((rows, HD), F32),
        "square": pltpu.VMEM((rows, HD), F32),
        "product": pltpu.VMEM((rows, 3 * HD), F32),
        "predicted": pltpu.VMEM((own, narrow), F32),
        "weights": pltpu.VMEM((width, 3 * HD), BF16),
        "query": pltpu.VMEM((rows, HD), BF16),
        "my_tokens": pltpu.VMEM((own, width), BF16),
        "part": pltpu.VMEM((2, NZ, own, narrow), BF16),
        "normed_t": pltpu.VMEM((narrow, rows), BF16),
        "hidden_t": pltpu.VMEM((units, rows), BF16),
        "by_gate": pltpu.VMEM((rows, units), F32),
        "by_up": pltpu.VMEM((rows, units), F32),
        "q_send": dma(2, 4, 3),
        "q_recv": dma(2, 4, 3),
        "qx_send": dma(9),
        "qx_recv": dma(9),
        "pairs": pltpu.VMEM((4 * NY, 2, rows, HD), BF16),
        "wide": pltpu.VMEM((NZ,) + w_out.shape, BF16),
        "start": pltpu.VMEM((rows, HD), jnp.int32),
        "peak": pltpu.VMEM((rows, HD), F32),
        "denom": pltpu.VMEM((rows, HD), F32),
        "accum": pltpu.VMEM((rows, HD), F32),
        "attended": pltpu.VMEM((rows, HD), BF16),
        "k_send": dma(9, 2),
        "k_recv": dma(9, 2),
        "c_send": dma(9),
        "c_recv": dma(9),
        "w_send": dma(2, 4, 2),
        "w_recv": dma(2, 4, 2),
        "wc_send": dma(7),
        "wc_recv": dma(7),
        "s_got": pltpu.VMEM((NZ, own, narrow), BF16),
        "s_out": pltpu.VMEM((NZ, own, narrow), BF16),
        "s_in": pltpu.VMEM((NZ - 1, own, narrow), BF16),
        "sx_send": one,
        "sx_recv": one,
        "sz_send": dma(7),
        "sz_recv": dma(7),
        "load_sem": dma(len(ORDER)),
        "heads": pltpu.VMEM((NZ, 2 * own, HD), BF16),
        "a_send": dma(7),
        "a_recv": dma(7),
        "out_send": pltpu.VMEM((4, own, width // 4), BF16),
        "out_recv": pltpu.VMEM((4, own, width // 4), BF16),
        "o_send": dma(4),
        "o_recv": dma(4),
        "partial": pltpu.VMEM((4, 2 * own, width // 4), F32),
        "mixed": pltpu.VMEM((own, width), BF16),
        "blocks": pltpu.VMEM((size, own, width), BF16),
        "hidden": pltpu.VMEM((NZ, 2 * own, ff), BF16),
        "parts": pltpu.VMEM((size, own, width), BF16),
        "g_send": dma(2, 4, 3),
        "g_recv": dma(2, 4, 3),
        "gx_send": dma(9),
        "gx_recv": dma(9),
    }
    names = ("sbuf", "rbuf", "xbuf", "xlast", "xgot", "r_send", "r_recv", "rx_send", "rx_recv")
    scratch.update(zip(names, scatter_scratch(half, width), strict=True))
    scratch.update(
        {
            "teacher": pltpu.VMEM((own, width), BF16),
            "gathered": pltpu.VMEM((size, own, narrow), BF16),
            "px_send": dma(8),
            "px_recv": dma(8),
            "p_send": dma(7),
            "p_recv": dma(7),
            "t_send": dma(size - 1),
            "t_recv": dma(size - 1),
            "grads": pltpu.VMEM((size, 3 * own + 16, units), BF16),
            "inbox": pltpu.VMEM((size, 3 * own + 16, units), BF16),
            "send1": dma(size - 1),
            "recv1": dma(size - 1),
            "send2": dma(size - 1),
            "recv2": dma(size - 1),
        }
    )
    elsewhere = ("tokens", "w_query", "w_key", "w_value", "w_out")
    for name in ORDER:
        if name not in elsewhere:
            scratch[name] = pltpu.VMEM(inputs[name].shape, inputs[name].dtype)
    names = [name + "_hbm" for name in inputs]
    columns, sums, squares = call(
        functools.partial(
            layer_body, (*names, *outputs, *scratch), rows * lax.axis_size("dp")
        ),
        "layer",
        1,
        tuple(inputs.values()),
        tuple(outputs.values()),
        list(scratch.values()),
        [pl.BlockSpec(memory_space=pl.ANY)] * len(inputs),
    )
    teacher_out, grad_gate, grad_up, grad_down, error = finish(columns, sums, squares)
    return (teacher_out, grad_gate, grad_up, grad_down, error.reshape(()))


def solution(mesh):
    in_specs = (
        P("dp", "tensor"),
        P(),
        P("dp"),
        P(),
        P(),
        P(None, "tensor"),
        P(None, "tensor"),
        P(None, "tensor"),
        P("tensor", None),
        P(None, "tensor"),
        P(None, "tensor"),
        P("tensor", None),
        P(),
        P("dp", None),
        P(None, "tensor"),
        P(None, "tensor"),
        P("tensor", None),
    )
    out_specs = (P("dp", "tensor"), P(None, "tensor"), P(None, "tensor"), P("tensor", None), P())
    return jax.shard_map(local, mesh=mesh, in_specs=in_specs, out_specs=out_specs, check_vma=False)
```

```python
import functools

import jax
import jax.numpy as jnp
import numpy as np
from jax import lax
from jax.experimental import pallas as pl
from jax.experimental.pallas import tpu as pltpu
from jax.sharding import PartitionSpec as P

HD = 128
NZ = 8
NY = 4
MESH = pl.DeviceIdType.MESH
VM = pl.BlockSpec(memory_space=pltpu.VMEM)
LIMIT = 56 * 1024 * 1024
F32 = jnp.float32
BF16 = jnp.bfloat16


def params(collective_id):
    return pltpu.CompilerParams(
        collective_id=collective_id, has_side_effects=True, vmem_limit_bytes=LIMIT
    )


def remote(src, dst, send_sem, recv_sem, device):
    return pltpu.make_async_remote_copy(
        src_ref=src,
        dst_ref=dst,
        send_sem=send_sem,
        recv_sem=recv_sem,
        device_id=device,
        device_id_type=MESH,
    )


def greet(devices, meanwhile=None):
    barrier = pltpu.get_barrier_semaphore()
    for device in devices:
        pl.semaphore_signal(barrier, inc=1, device_id=device, device_id_type=MESH)
    if meanwhile is not None:
        meanwhile()
    pl.semaphore_wait(barrier, len(devices))


def places():
    dp, tensor = lax.axis_index("dp"), lax.axis_index("tensor")
    x_hi, z = tensor // NZ, lax.rem(tensor, NZ)
    return dp, tensor, x_hi, z


def turn(z, by, size):
    return lax.rem(z + by + size, size)


def dma(*shape):
    return pltpu.SemaphoreType.DMA(shape)


def call(body, name, collective_id, inputs, outputs, scratch, specs=None):
    return pl.pallas_call(
        body,
        out_shape=tuple(jax.ShapeDtypeStruct(shape, kind) for shape, kind in outputs),
        in_specs=specs or [VM] * len(inputs),
        out_specs=tuple([VM] * len(outputs)),
        scratch_shapes=scratch,
        compiler_params=params(collective_id),
        name=name,
    )(*inputs)


class Sent:
    def __init__(self):
        self.copies = []

    def start(self, copy):
        copy.start()
        self.copies.append(copy)

    def finish(self):
        for copy in self.copies:
            copy.wait_send()


def on_ring(way, far, sub):
    return far < 4 or (way == 1) == (sub == 1)


def towards(way, by):
    return by if way == 0 else -by


def mix_gather(ref, at, half, sems, hook=lambda step: None, ready=None, tail=None):
    ring_send, ring_recv, x_send, x_recv = sems
    dp, tensor, x_hi, z = places()
    partner = (dp, (1 - x_hi) * NZ + z)
    nexts = tuple((dp, x_hi * NZ + turn(z, by, NZ)) for by in (1, -1))
    sent = Sent()

    def view(zz, sub):
        plane = x_hi if sub < 2 else 1 - x_hi
        return ref.at[at(zz, plane), pl.ds((sub % 2) * half, half)]

    def ring(way, far, sub, hops):
        block = view(turn(z, -towards(way, hops), NZ), sub)
        sems = ring_send.at[way, far - 1, sub], ring_recv.at[way, far - 1, sub]
        return remote(block, block, *sems, nexts[way])

    def cross(zz, sub, slot):
        block = view(zz, sub)
        return remote(block, block, x_send.at[slot], x_recv.at[slot], partner)

    def slot(way, far):
        return 1 + far + 3 * way if way == 0 else 4 + far

    def crossed(far):
        if far == 0:
            cross(z, 3, 1).wait_recv()
        for way in range(2):
            if 0 < far < 4 + way:
                cross(turn(z, -towards(way, far), NZ), 3, slot(way, far)).wait_recv()

    sent.start(cross(z, 0, 0))
    for sub in range(2):
        for way in range(2):
            sent.start(ring(way, 1, sub, 0))
    sent.start(cross(z, 1, 1))
    hook(0)
    cross(z, 2, 0).wait_recv()
    for way in range(2):
        sent.start(ring(way, 1, 2, 0))
    for far in range(2, 5):
        hook(far - 1)
        for sub in range(3):
            for way in range(2):
                ring(way, far - 1, sub, far - 1).wait_recv()
                if on_ring(way, far, sub):
                    sent.start(ring(way, far, sub, far - 1))
                if sub == 1:
                    origin = turn(z, -towards(way, far - 1), NZ)
                    sent.start(cross(origin, 1, slot(way, far - 1)))
        if far == 3:
            crossed(0)
            crossed(1)
            if ready:
                ready((0, 1))
        if far == 4:
            crossed(2)
            if ready:
                ready((2,))
    ring(1, 4, 1, 4).wait_recv()
    sent.start(cross(turn(z, 4, NZ), 1, slot(1, 4)))
    crossed(3)
    if tail:
        tail()
    for sub in (0, 2):
        ring(0, 4, sub, 4).wait_recv()
    crossed(4)
    sent.finish()


def scatter_scratch(half, width):
    return [
        pltpu.VMEM((2, 4, 3, half, width), BF16),
        pltpu.VMEM((2, 4, 3, half, width), BF16),
        pltpu.VMEM((8, half, width), BF16),
        pltpu.VMEM((half, width), BF16),
        pltpu.VMEM((half, width), BF16),
        dma(2, 4, 3),
        dma(2, 4, 3),
        dma(9),
        dma(9),
    ]


def mix_scatter(part, make, scratch):
    sbuf, rbuf, xbuf, xlast, xgot, ring_send, ring_recv, x_send, x_recv = scratch
    half = sbuf.shape[3]
    dp, tensor, x_hi, z = places()
    partner = (dp, (1 - x_hi) * NZ + z)
    nexts = tuple((dp, x_hi * NZ + turn(z, by, NZ)) for by in (1, -1))
    sent = Sent()

    def view(zz, sub):
        plane = x_hi if sub < 2 else 1 - x_hi
        return part.at[zz * 2 + plane, pl.ds((sub % 2) * half, half)]

    def slot(way, far):
        return 7 if far == 4 else 1 + 3 * way + far - 1

    def cross(zz, at):
        return remote(view(zz, 3), xbuf.at[at], x_send.at[at], x_recv.at[at], partner)

    def ring(way, far, sub, source):
        sems = ring_send.at[way, far - 1, sub], ring_recv.at[way, far - 1, sub]
        return remote(source, rbuf.at[way, far - 1, sub], *sems, nexts[way])

    def arrived(way, far, sub):
        ring(way, far, sub, rbuf.at[way, far - 1, sub]).wait_recv()
        return rbuf[way, far - 1, sub].astype(F32)

    def crossed(at):
        cross(z, at).wait_recv()
        return xbuf[at].astype(F32)

    def send(way, far, sub):
        source = view(turn(z, towards(way, far), NZ), sub)
        extra = []
        if far < 4 and on_ring(way, far + 1, sub):
            extra.append(arrived(way, far + 1, sub))
        if sub == 1:
            extra.append(crossed(slot(way, far)))
        if extra:
            total = source[...].astype(F32)
            for one in extra:
                total = total + one
            sbuf[way, far - 1, sub] = total.astype(BF16)
            source = sbuf.at[way, far - 1, sub]
        sent.start(ring(way, far, sub, source))

    def make_pair(far):
        pair = [turn(z, by, NZ) for by in (far, -far)]
        make(pair)
        for way in range(2):
            sent.start(cross(pair[way], slot(way, far)))

    def begin():
        make_pair(3)
        for sub in (0, 2):
            send(1, 3, sub)

    def rest():
        far4 = turn(z, 4, NZ)
        make([far4])
        sent.start(cross(far4, 7))
        for sub in (0, 2):
            send(0, 4, sub)
        make_pair(2)
        send(1, 4, 1)
        for sub in (1, 2, 0):
            send(0, 3, sub)
        send(1, 3, 1)
        make_pair(1)
        for sub in (2, 0, 1):
            for way in range(2):
                send(way, 2, sub)
        make([z])
        sent.start(cross(z, 0))
        for sub in (2, 0, 1):
            for way in range(2):
                send(way, 1, sub)
        return last_sums()

    def total(sub):
        return view(z, sub)[...].astype(F32) + arrived(0, 1, sub) + arrived(1, 1, sub)

    def last_sums():
        xlast[...] = total(2).astype(BF16)
        last = remote(xlast, xgot, x_send.at[8], x_recv.at[8], partner)
        sent.start(last)
        second = total(1) + crossed(0)
        first = total(0)

        def other():
            last.wait_recv()
            return first + xgot[...].astype(F32)

        return other, second, sent

    return begin, rest


def rms(values):
    return values * lax.rsqrt(jnp.mean(values * values, axis=-1, keepdims=True) + 1e-05)


def student(r, step):
    own = r.student.shape[0] // (2 * NZ)
    at = pl.ds(step * 128, 128)
    values = rms(r.student[at, :].astype(F32))
    r.normed_t[:, at] = values.T.astype(BF16)
    values = values.astype(BF16)
    gate = jnp.dot(values, r.s_gate[...], preferred_element_type=F32)
    up = jnp.dot(values, r.s_up[...], preferred_element_type=F32)
    sigmoid = jax.nn.sigmoid(gate)
    r.by_gate[at, :] = up * sigmoid * (1.0 + gate * (1.0 - sigmoid))
    r.by_up[at, :] = gate * sigmoid
    hidden = gate * sigmoid * up
    r.hidden_t[:, at] = hidden.T.astype(BF16)
    out = jnp.dot(hidden.astype(BF16), r.s_down[...], preferred_element_type=F32)
    for index in range(128 // own):
        block = out[index * own : (index + 1) * own].astype(BF16)
        r.part[index % 2, step * (64 // own) + index // 2] = block


def project(r, before, after, weights_there):
    dp, tensor, x_hi, z = places()
    rows = r.tok.shape[1]
    own = rows // (2 * NZ)

    def hook(step):
        if step == 0:
            weights_there()
            student(r, 3)

    tile = 256
    started = []

    def add(distances):
        places_now = []
        for by in distances:
            for zz in [z] if by == 0 else [turn(z, 4, NZ)] if by == 4 else [turn(z, by, NZ), turn(z, -by, NZ)]:
                places_now += [zz, NZ + zz]
        weights = jnp.concatenate(
            [r.weights[pl.ds(pl.multiple_of(at * HD, HD), HD), :] for at in places_now], axis=0
        )
        for step in range(rows // tile):
            at = pl.ds(step * tile, tile)
            square = None if not started else r.square[at, :]
            values = []
            for index in places_now:
                value = r.tok[index, at, :].astype(F32)
                square = value * value if square is None else square + value * value
                values.append((value * r.norm_gain[pl.ds(index, 1), :]).astype(BF16))
            r.square[at, :] = square
            out = jnp.dot(jnp.concatenate(values, axis=1), weights, preferred_element_type=F32)
            r.product[at, :] = out if not started else r.product[at, :] + out
        started.append(True)

    def tail():
        before()
        add((3,))

    mix_gather(
        r.tok,
        lambda zz, plane: plane * NZ + zz,
        rows // 2,
        (r.q_send, r.q_recv, r.qx_send, r.qx_recv),
        hook,
        ready=add,
        tail=tail,
    )
    after()
    add((4,))
    for step in range(rows // tile):
        at = pl.ds(step * tile, tile)
        mean = jnp.sum(r.square[at, :], axis=1, keepdims=True) / (2 * NZ * HD)
        out = r.product[at, :] * lax.rsqrt(mean + 1e-05)
        cosine, sine = r.cosine[at, :], r.sine[at, :]

        def rotary(values):
            return (values * cosine + pltpu.roll(values, HD // 2, 1) * sine).astype(BF16)

        r.pairs[dp, 0, at, :] = rotary(out[:, HD : 2 * HD])
        r.pairs[dp, 1, at, :] = out[:, 2 * HD :].astype(BF16)
        r.query[at, :] = rotary(out[:, :HD])


def keep_tokens(r):
    _, _, x_hi, z = places()
    own = r.my_tokens.shape[0]
    my_rows = pl.multiple_of((z * 2 + x_hi) * own, own)
    for index in range(2 * NZ):
        r.my_tokens[:, index * HD : (index + 1) * HD] = r.tok[index, pl.ds(my_rows, own)]


def find_starts(r):
    dp = lax.axis_index("dp")
    rows = r.start.shape[0]
    position = (dp * rows + lax.broadcasted_iota(jnp.int32, r.start.shape, 0)).astype(F32)
    found = jnp.zeros(r.start.shape, F32)
    for number in range(1, 8):
        before = jnp.where(r.series[...] < number, 1.0, 0.0)
        begin = jnp.sum(jnp.sum(before, axis=0, keepdims=True), axis=1, keepdims=True)
        found = jnp.where(begin <= position, jnp.maximum(found, begin), found)
    r.start[...] = found.astype(jnp.int32)


def prepare(r, loaded):
    loaded("series")
    find_starts(r)
    loaded("offsets", "frequency")
    for step in range(r.offsets.shape[0]):
        at = pl.ds(step * HD, HD)
        offset = jnp.broadcast_to(r.offsets[step : step + 1, :].astype(F32), (HD, HD)).T
        angle = offset * r.frequency[...]
        lane = lax.broadcasted_iota(jnp.int32, (HD, HD), 1)
        r.cosine[at, :] = jnp.cos(angle)
        sine = jnp.sin(angle)
        r.sine[at, :] = jnp.where(lane < HD // 2, -sine, sine)
    loaded("student", "s_gate", "s_up", "s_down")
    for step in range(3):
        student(r, step)


R1, R2, R3, X0, X1, H1, H2, H3, OWN = range(9)


class Refs:
    def __init__(self, names, refs):
        for name, ref in zip(names, refs, strict=True):
            setattr(self, name, ref)


def attend(r, mine, j, diagonal, tile=256):
    rows, span = r.query.shape[0], r.pairs.shape[2]
    factor = HD ** (-0.5) * 1.4426950408889634
    key, value = r.pairs[j, 0], r.pairs[j, 1]
    for index in range(rows // tile):
        at = slice(index * tile, (index + 1) * tile)
        scores = lax.dot_general(
            r.query[at, :], key, (((1,), (1,)), ((), ())), preferred_element_type=F32
        )
        column = lax.broadcasted_iota(jnp.int32, (tile, span), 1)
        allowed = column >= r.start[at, :1] - j * span
        if diagonal:
            row = index * tile + lax.broadcasted_iota(jnp.int32, (tile, span), 0)
            allowed = allowed & (column <= row)
        scores = jnp.where(allowed, scores, -1e30)
        top = jnp.max(scores, axis=1, keepdims=True)
        if not diagonal:
            old = r.peak[at, :1]
            top = jnp.maximum(old, top)
        weights = jnp.exp2((scores - top) * factor)
        denom = jnp.sum(weights, axis=1, keepdims=True)
        accum = jnp.dot(weights.astype(BF16), value, preferred_element_type=F32)
        if not diagonal:
            scale = jnp.exp2((old - top) * factor)
            denom = denom + r.denom[at, :1] * scale
            accum = accum + r.accum[at, :] * scale
        r.peak[at, :] = jnp.broadcast_to(top, (tile, HD))
        r.denom[at, :] = jnp.broadcast_to(denom, (tile, HD))
        r.accum[at, :] = accum


def exchange(r, sent):
    dp, tensor, x_hi, z = places()
    x_lo, y, core = dp // (2 * NY), lax.rem(dp // 2, NY), lax.rem(dp, 2)

    def index(xx, yy, cc):
        return xx * 2 * NY + yy * 2 + cc

    k_partner = (index(1 - x_lo, y, core), tensor)
    sibling = (index(x_lo, y, 1 - core), tensor)
    up, down = ((index(x_lo, turn(y, by, NY), core), tensor) for by in (1, -1))
    z_peers = [(dp, x_hi * NZ + turn(z, by, NZ)) for by in range(1, NZ)]
    z_nexts = (z_peers[0], z_peers[-1])
    s_partner = (dp, (1 - x_hi) * NZ + z)
    deep = r.wide.shape[1] // 4
    first, second = x_lo == 0, x_lo == 1

    def chip(by):
        return turn(y, by, NY)

    arrives = {
        R1: (y >= 1, x_lo, chip(-1)),
        R2: (y >= 2, x_lo, chip(-2)),
        R3: (y == 3, x_lo, chip(1)),
        X0: (second, 0, y),
        X1: (second & (y >= 1), 0, chip(-1)),
        H1: (second & (y <= 2), 0, chip(1)),
        H2: (second & (y <= 1), 0, chip(2)),
        H3: (second & (y == 0), 0, chip(-1)),
        OWN: (None, x_lo, y),
    }

    def k_copy(event, part, xx, yy, device):
        block = r.pairs.at[index(xx, yy, core), part]
        return remote(block, block, r.k_send.at[event, part], r.k_recv.at[event, part], device)

    later = []

    def when(condition, copy):
        @pl.when(condition)
        def _():
            copy.start()

        later.append((condition, copy))

    def k_wait(event, part):
        condition, xx, yy = arrives[event]

        @pl.when(condition)
        def _():
            k_copy(event, part, xx, yy, up).wait_recv()

    def c_copy(event, cc):
        _, xx, yy = arrives[event]
        block = r.pairs.at[index(xx, yy, cc)]
        return remote(block, block, r.c_send.at[event], r.c_recv.at[event], sibling)

    def share(event):
        condition = arrives[event][0]
        if condition is None:
            sent.start(c_copy(event, core))
        else:
            when(condition, c_copy(event, core))

    def shared(*events):
        for event in events:
            condition = arrives[event][0]
            if condition is None:
                c_copy(event, 1 - core).wait_recv()
            else:

                @pl.when(condition)
                def _(event=event):
                    c_copy(event, 1 - core).wait_recv()

    def work(*events):
        found = []
        for event in events:
            condition, xx, yy = arrives[event]
            for cc in (core, 1 - core):
                if event == OWN and cc is core:
                    continue
                j = index(xx, yy, cc)
                needed = (j < dp) & (j >= dp - 10)
                found.append((j, needed if condition is None else needed & condition))

        @pl.loop(0, len(found))
        def _(step):
            j, needed = found[0]
            needed = needed.astype(jnp.int32)
            for number, (jj, wanted) in enumerate(found[1:], 1):
                j = jnp.where(step == number, jj, j)
                needed = jnp.where(step == number, wanted.astype(jnp.int32), needed)

            @pl.when(needed == 1)
            def _():
                attend(r, dp, j, False)

    def w_copy(way, far, sub, hops):
        top = pl.multiple_of(core * 2 * deep + sub * deep, deep)
        block = r.wide.at[turn(z, -towards(way, hops), NZ), pl.ds(top, deep)]
        sems = r.w_send.at[way, far - 1, sub], r.w_recv.at[way, far - 1, sub]
        return remote(block, block, *sems, z_nexts[way])

    def w_share(by, slot, cc):
        top = pl.multiple_of(cc * 2 * deep, 2 * deep)
        block = r.wide.at[turn(z, by, NZ), pl.ds(top, 2 * deep)]
        return remote(block, block, r.wc_send.at[slot], r.wc_recv.at[slot], sibling)

    def w_forward(far, sub):
        for way in range(2):
            if far < 4 or sub == way:
                w_copy(way, far, sub, far).wait_recv()
            if far < 3 or (far == 3 and sub == way):
                sent.start(w_copy(way, far + 1, sub, far))

    def w_spread(far):
        for way in range(2):
            sent.start(w_share(towards(way, -far), 2 * (far - 1) + way, core))

    s_cross = remote(r.part.at[1 - x_hi], r.s_got, r.sx_send, r.sx_recv, s_partner)

    def begin_student():
        sent.start(s_cross)

    def begin_wide():
        for sub in range(2):
            for way in range(2):
                sent.start(w_copy(way, 1, sub, 0))

    def arrive():
        for part in range(2):
            when(y <= 2, k_copy(R1, part, x_lo, y, up))
            when(y == 0, k_copy(R3, part, x_lo, y, down))
            when(first, k_copy(X0, part, 0, y, k_partner))
        share(OWN)
        w_forward(1, 0)
        w_forward(1, 1)
        w_spread(1)
        attend(r, dp, dp, True)
        for part in range(2):
            k_wait(R1, part)
            when((y >= 1) & (y <= 2), k_copy(R2, part, x_lo, chip(-1), up))
            when(first & (y >= 1), k_copy(X1, part, 0, chip(-1), k_partner))
            k_wait(X0, part)
            when(second & (y >= 1), k_copy(H1, part, 0, y, down))
            when(second & (y == 3), k_copy(H3, part, 0, y, up))
            w_forward(2, part)
        share(R1)
        share(X0)
        w_spread(2)
        k_wait(R3, 0)
        k_wait(R3, 1)
        share(R3)
        s_cross.wait_recv()
        r.s_out[...] = (r.part[x_hi].astype(F32) + r.s_got[...].astype(F32)).astype(BF16)
        shared(OWN, R1)
        work(OWN, R1)
        for part in range(2):
            k_wait(H1, part)
            when(second & (y >= 1) & (y <= 2), k_copy(H2, part, 0, chip(1), down))
        share(H1)
        w_forward(3, 0)
        shared(X0)
        work(X0)
        w_forward(3, 1)
        w_spread(3)
        for event in (X1, R2, H3):
            k_wait(event, 0)
            k_wait(event, 1)
            share(event)
        shared(R3, H1)
        work(R3, H1)
        w_forward(4, 0)
        w_forward(4, 1)
        sent.start(w_share(4, 6, core))
        k_wait(H2, 0)
        k_wait(H2, 1)
        share(H2)
        shared(X1, R2, H3)
        work(X1, R2, H3)
        shared(H2)
        work(H2)
        r.attended[...] = (r.accum[...] / r.denom[...]).astype(BF16)

    def finish():
        for condition, copy in later:

            @pl.when(condition)
            def _(copy=copy):
                copy.wait_send()

    def wide_whole():
        for slot, by in enumerate([-1, 1, -2, 2, -3, 3, 4]):
            w_share(by, slot, 1 - core).wait_recv()

    return begin_student, begin_wide, arrive, wide_whole, finish


ORDER = (
    "tokens",
    "series",
    "offsets",
    "frequency",
    "student",
    "s_gate",
    "s_up",
    "s_down",
    "w_query",
    "w_key",
    "w_value",
    "norm_gain",
    "w_out",
    "mlp_gain",
    "w_gate",
    "w_up",
    "w_down",
    "projector",
)


def layer_body(names, total_rows, *refs):
    r = Refs(names, refs)
    dp, tensor, x_hi, z = places()
    size = 2 * NZ
    rows, width = r.tok.shape[1], r.w_gate.shape[0]
    own = rows // size
    pair = 2 * own
    row = z * 2 + x_hi
    my_rows = pl.ds(pl.multiple_of(row * own, own), own)
    partner = (dp, (1 - x_hi) * NZ + z)
    z_peers = [(dp, x_hi * NZ + turn(z, by, NZ)) for by in range(1, NZ)]
    t_peers = [turn(tensor, by, size) for by in range(1, size)]
    d_peers = [turn(dp, by, size) for by in range(1, size)]
    loads = {}
    near = {
        "tokens": r.tok.at[tensor],
        "w_query": r.weights.at[:, pl.ds(0, HD)],
        "w_key": r.weights.at[:, pl.ds(HD, HD)],
        "w_value": r.weights.at[:, pl.ds(2 * HD, HD)],
        "w_out": r.wide.at[z],
    }
    for index, name in enumerate(ORDER):
        target = near[name] if name in near else getattr(r, name)
        loads[name] = pltpu.make_async_copy(
            getattr(r, name + "_hbm"), target, r.load_sem.at[index]
        )
        loads[name].start()

    def loaded(*names):
        for name in names:
            loads.pop(name).wait()

    greet(
        [(dp, peer) for peer in t_peers] + [(peer, tensor) for peer in d_peers],
        lambda: prepare(r, loaded),
    )
    sent = Sent()
    begin_student, begin_wide, arrive, wide_whole, finish_exchange = exchange(r, sent)
    loaded("tokens")

    def after():
        loaded("w_out")
        begin_wide()

    project(r, begin_student, after, lambda: loaded("w_query", "w_key", "w_value", "norm_gain"))
    arrive()

    def rows_of(zz):
        return pl.ds(pl.multiple_of(zz * pair, pair), pair)

    for by in range(1, NZ):
        sent.start(
            remote(
                r.attended.at[rows_of(turn(z, by, NZ))],
                r.heads.at[z],
                r.a_send.at[by - 1],
                r.a_recv.at[by - 1],
                z_peers[by - 1],
            )
        )
    def send_student():
        for by in range(1, NZ):
            sent.start(
                remote(
                    r.s_out.at[turn(z, by, NZ)],
                    r.s_in.at[by - 1],
                    r.sz_send.at[by - 1],
                    r.sz_recv.at[by - 1],
                    z_peers[by - 1],
                )
            )

    r.heads[z] = r.attended[rows_of(z), :]
    wide_whole()
    for by in range(1, NZ):
        block = r.heads.at[turn(z, -by, NZ)]
        remote(block, block, r.a_send.at[by - 1], r.a_recv.at[by - 1], z_peers[by - 1]).wait_recv()
    chunk = width // 4
    joined = jnp.concatenate([r.heads[index] for index in range(NZ)], axis=1)
    depth = joined.shape[1]

    def half_rows(plane):
        return pl.ds(pl.multiple_of(plane * own, own), own)

    def swap(step):
        sems = r.o_send.at[step], r.o_recv.at[step]
        return remote(r.out_send.at[step], r.out_recv.at[step], *sems, partner)

    for step in range(width // chunk):
        at = slice(step * chunk, (step + 1) * chunk)
        r.partial[step] = jnp.dot(
            joined, r.wide[:, :, at].reshape(depth, chunk), preferred_element_type=F32
        )
        r.out_send[step] = r.partial[step, half_rows(1 - x_hi), :].astype(BF16)
        sent.start(swap(step))
        if step == 0:
            send_student()
    keep_tokens(r)
    for step in range(width // chunk):
        at = slice(step * chunk, (step + 1) * chunk)
        mine = r.partial[step, half_rows(x_hi), :] + r.my_tokens[:, at].astype(F32)
        swap(step).wait_recv()
        r.mixed[:, at] = (mine + r.out_recv[step].astype(F32)).astype(BF16)
    mixed = r.mixed[...]
    loaded("mlp_gain")
    r.blocks[row] = (rms(mixed.astype(F32)) * r.mlp_gain[...]).astype(BF16)

    waited = []

    def units(zs):
        if not waited:
            loaded("w_gate", "w_up")
            waited.append(True)
        value = jnp.concatenate(
            [r.blocks[pl.ds(zz * 2, 2)].reshape(pair, width) for zz in zs], axis=0
        )
        gate = jnp.dot(value, r.w_gate[...], preferred_element_type=F32)
        up = jnp.dot(value, r.w_up[...], preferred_element_type=F32)
        found = (gate * jax.nn.sigmoid(gate) * up).astype(BF16)
        for at, zz in enumerate(zs):
            r.hidden[zz] = found[at * pair : (at + 1) * pair]

    def predict():
        student_sum = r.s_out[z].astype(F32)
        for by in range(1, NZ):
            got = r.s_in.at[by - 1]
            sems = r.sz_send.at[by - 1], r.sz_recv.at[by - 1]
            remote(got, got, *sems, z_peers[by - 1]).wait_recv()
            student_sum = student_sum + r.s_in[by - 1].astype(F32)
        r.predicted[...] = r.student[my_rows, :].astype(F32) + student_sum

    def ready(distances):
        zs = []
        for by in distances:
            zs += [z] if by == 0 else [turn(z, by, NZ), turn(z, -by, NZ)]
        units(zs)
        if 2 in distances:
            predict()

    fresh = [3, 4]

    def make(zs):
        if fresh:
            fresh.pop()
            units(zs)
        value = jnp.concatenate([r.hidden[zz] for zz in zs], axis=0)

        @pl.loop(0, width // chunk)
        def _(step):
            at = pl.ds(pl.multiple_of(step * chunk, chunk), chunk)
            out = jnp.dot(value, r.w_down[:, at], preferred_element_type=F32).astype(BF16)
            for index, zz in enumerate(zs):
                for plane in range(2):
                    top = index * pair + plane * own
                    r.parts[zz * 2 + plane, :, at] = out[top : top + own]

    scratch = (r.sbuf, r.rbuf, r.xbuf, r.xlast, r.xgot, r.r_send, r.r_recv, r.rx_send, r.rx_recv)
    begin_sum, rest_of_sum = mix_scatter(r.parts, make, scratch)
    loaded("w_down")
    mix_gather(
        r.blocks,
        lambda zz, plane: zz * 2 + plane,
        own // 2,
        (r.g_send, r.g_recv, r.gx_send, r.gx_recv),
        ready=ready,
        tail=begin_sum,
    )
    top, bottom, more = rest_of_sum()
    loaded("projector")

    def last_rows(first, summed):
        at = slice(first, first + own // 2)
        teacher = (r.mixed[at, :].astype(F32) + summed).astype(BF16)
        r.teacher[at, :] = teacher
        target = jnp.dot(teacher, r.projector[...], preferred_element_type=F32)
        scaled = (r.predicted[at, :] - target) * total_rows ** (-0.5)
        r.gathered[row, at, :] = scaled.astype(BF16)

    last_rows(own // 2, bottom)
    last_rows(0, top())

    def place(by, plane):
        return r.gathered.at[turn(z, by, NZ) * 2 + plane]

    def across(by, plane):
        block = place(by, plane)
        at = by % NZ
        return remote(block, block, r.px_send.at[at], r.px_recv.at[at], partner)

    def along(by, device):
        block = place(-by if device is None else 0, x_hi)
        sems = r.p_send.at[by - 1], r.p_recv.at[by - 1]
        return remote(block, block, *sems, z_peers[by - 1])

    for by in (4, 3, 5, 2, 6, 1, 7):
        sent.start(along(by, True))
    sent.start(across(0, x_hi))
    for by in (1, 7, 2, 6, 3, 5, 4):
        along(by, None).wait_recv()
        sent.start(across(-by, x_hi))
    for by, peer in enumerate(t_peers):
        sent.start(
            remote(
                r.teacher.at[:, pl.ds(pl.multiple_of(peer * HD, HD), HD)],
                r.columns.at[row],
                r.t_send.at[by],
                r.t_recv.at[by],
                (dp, peer),
            )
        )
    r.columns[row] = r.teacher[:, pl.ds(pl.multiple_of(tensor * HD, HD), HD)]
    for by in (0, 1, 7, 2, 6, 3, 5, 4):
        across(-by, 1 - x_hi).wait_recv()

    scaled = r.gathered[...].reshape(rows, -1)
    grad_hidden = lax.dot_general(
        scaled, r.s_down[...], (((1,), (1,)), ((), ())), preferred_element_type=F32
    )
    both = jnp.concatenate(
        [(grad_hidden * r.by_gate[...]).astype(BF16), (grad_hidden * r.by_up[...]).astype(BF16)],
        axis=1,
    )
    both = jnp.dot(r.normed_t[...], both, preferred_element_type=F32).astype(BF16)
    down = jnp.dot(r.hidden_t[...], scaled, preferred_element_type=F32).astype(BF16)
    count = grad_hidden.shape[1]
    r.grads[:, :own] = both[:, :count].reshape(size, own, count)
    r.grads[:, own:pair] = both[:, count:].reshape(size, own, count)
    down = jnp.concatenate([down[:, at : at + HD] for at in range(0, down.shape[1], HD)], axis=0)
    r.grads[:, pair : 3 * own] = down.reshape(size, own, HD)
    squares = scaled.astype(F32)
    squares = jnp.sum((squares * squares).reshape(-1, 8, scaled.shape[1]), axis=0)
    squares = sum(squares[:, at : at + HD] for at in range(0, scaled.shape[1], HD))
    high = squares.astype(BF16)
    low = (squares - high.astype(F32)).astype(BF16)
    both = jnp.concatenate([high, low], axis=0)
    r.grads[:, 3 * own :] = jnp.broadcast_to(both[None], (size,) + both.shape)

    def origin(by):
        return turn(dp, -(by + 1), size)

    r.inbox[dp] = r.grads[dp]
    for by, peer in enumerate(d_peers):
        sems = r.send1.at[by], r.recv1.at[by]
        sent.start(remote(r.grads.at[peer], r.inbox.at[dp], *sems, (peer, tensor)))
    for by, peer in enumerate(d_peers):
        block = r.inbox.at[origin(by)]
        remote(block, block, r.send1.at[by], r.recv1.at[by], (peer, tensor)).wait_recv()
    total = r.inbox[0].astype(F32)
    for index in range(1, size):
        total = total + r.inbox[index].astype(F32)
    r.sums[dp] = total[: 3 * own].astype(BF16)
    r.error[...] = total[3 * own : 3 * own + 8] + total[3 * own + 8 :]
    for by, peer in enumerate(d_peers):
        block = r.sums.at[dp]
        sent.start(remote(block, block, r.send2.at[by], r.recv2.at[by], (peer, tensor)))
    for by, peer in enumerate(t_peers):
        source = turn(tensor, -(by + 1), size)
        block = r.columns.at[lax.rem(source, NZ) * 2 + source // NZ]
        remote(block, block, r.t_send.at[by], r.t_recv.at[by], (dp, peer)).wait_recv()
    for by, peer in enumerate(d_peers):
        block = r.sums.at[origin(by)]
        remote(block, block, r.send2.at[by], r.recv2.at[by], (peer, tensor)).wait_recv()
    finish_exchange()
    sent.finish()
    more.finish()


def finish_body(columns_ref, sums_ref, squares_ref, teacher_ref, gate_ref, up_ref, down_ref, error_ref):
    rows, width = teacher_ref.shape
    own = rows // (2 * NZ)
    teacher_ref[...] = columns_ref[...].reshape(rows, width)
    sums = sums_ref[...].astype(F32)
    gate_ref[...] = sums[:, :own].reshape(-1, width)
    up_ref[...] = sums[:, own : 2 * own].reshape(-1, width)
    down = sums[:, 2 * own :].reshape(-1, width)
    for index in range(down.shape[0] // width):
        lanes = slice(index * width, (index + 1) * width)
        down_ref[:, lanes] = down[lanes]
    total = jnp.sum(jnp.sum(squares_ref[...], axis=0, keepdims=True), axis=1, keepdims=True)
    error_ref[...] = total / down_ref.shape[1]


def finish(columns, sums, squares):
    own, units = columns.shape[1:]
    rows = 2 * NZ * own
    shapes = (
        ((rows, units), BF16),
        ((rows, units), F32),
        ((rows, units), F32),
        ((units, rows), F32),
        ((1, 1), F32),
    )
    return pl.pallas_call(
        finish_body,
        out_shape=tuple(jax.ShapeDtypeStruct(shape, kind) for shape, kind in shapes),
        in_specs=[VM] * 3,
        out_specs=(VM,) * 5,
        compiler_params=pltpu.CompilerParams(vmem_limit_bytes=LIMIT),
        name="finish",
    )(columns, sums, squares)


def frequencies(head_dim):
    indices = np.arange(head_dim // 2)
    found = np.exp(-np.log(500000.0) * 2.0 * indices / head_dim).astype(np.float32)
    return np.concatenate([found, found])[None]


def local(
    tokens,
    series_ids,
    offsets,
    norm_gain,
    mlp_gain,
    w_query,
    w_key,
    w_value,
    w_out,
    w_gate,
    w_up,
    w_down,
    projector,
    student_in,
    s_gate,
    s_up,
    s_down,
):
    rows = tokens.shape[0]
    size = 2 * NZ
    own = rows // size
    width = projector.shape[0]
    narrow = student_in.shape[1]
    units = s_gate.shape[1]
    ff = w_gate.shape[1]
    frequency = jnp.asarray(frequencies(HD))
    inputs = {
        "tokens": tokens,
        "series": series_ids.reshape(-1, HD),
        "norm_gain": norm_gain.reshape(-1, HD),
        "offsets": offsets.reshape(-1, HD),
        "frequency": frequency,
        "w_query": w_query,
        "w_key": w_key,
        "w_value": w_value,
        "w_out": w_out,
        "mlp_gain": mlp_gain[None],
        "w_gate": w_gate,
        "w_up": w_up,
        "w_down": w_down,
        "projector": projector,
        "student": student_in,
        "s_gate": s_gate,
        "s_up": s_up,
        "s_down": s_down,
    }
    outputs = {
        "columns": ((size, own, HD), BF16),
        "sums": ((size, 3 * own, units), BF16),
        "error": ((8, HD), F32),
    }
    one = pltpu.SemaphoreType.DMA
    half = own // 2
    scratch = {
        "tok": pltpu.VMEM((size, rows, HD), BF16),
        "cosine": pltpu.VMEM((rows, HD), F32),
        "sine": pltpu.VMEM((rows, HD), F32),
        "square": pltpu.VMEM((rows, HD), F32),
        "product": pltpu.VMEM((rows, 3 * HD), F32),
        "predicted": pltpu.VMEM((own, narrow), F32),
        "weights": pltpu.VMEM((width, 3 * HD), BF16),
        "query": pltpu.VMEM((rows, HD), BF16),
        "my_tokens": pltpu.VMEM((own, width), BF16),
        "part": pltpu.VMEM((2, NZ, own, narrow), BF16),
        "normed_t": pltpu.VMEM((narrow, rows), BF16),
        "hidden_t": pltpu.VMEM((units, rows), BF16),
        "by_gate": pltpu.VMEM((rows, units), F32),
        "by_up": pltpu.VMEM((rows, units), F32),
        "q_send": dma(2, 4, 3),
        "q_recv": dma(2, 4, 3),
        "qx_send": dma(9),
        "qx_recv": dma(9),
        "pairs": pltpu.VMEM((4 * NY, 2, rows, HD), BF16),
        "wide": pltpu.VMEM((NZ,) + w_out.shape, BF16),
        "start": pltpu.VMEM((rows, HD), jnp.int32),
        "peak": pltpu.VMEM((rows, HD), F32),
        "denom": pltpu.VMEM((rows, HD), F32),
        "accum": pltpu.VMEM((rows, HD), F32),
        "attended": pltpu.VMEM((rows, HD), BF16),
        "k_send": dma(9, 2),
        "k_recv": dma(9, 2),
        "c_send": dma(9),
        "c_recv": dma(9),
        "w_send": dma(2, 4, 2),
        "w_recv": dma(2, 4, 2),
        "wc_send": dma(7),
        "wc_recv": dma(7),
        "s_got": pltpu.VMEM((NZ, own, narrow), BF16),
        "s_out": pltpu.VMEM((NZ, own, narrow), BF16),
        "s_in": pltpu.VMEM((NZ - 1, own, narrow), BF16),
        "sx_send": one,
        "sx_recv": one,
        "sz_send": dma(7),
        "sz_recv": dma(7),
        "load_sem": dma(len(ORDER)),
        "heads": pltpu.VMEM((NZ, 2 * own, HD), BF16),
        "a_send": dma(7),
        "a_recv": dma(7),
        "out_send": pltpu.VMEM((4, own, width // 4), BF16),
        "out_recv": pltpu.VMEM((4, own, width // 4), BF16),
        "o_send": dma(4),
        "o_recv": dma(4),
        "partial": pltpu.VMEM((4, 2 * own, width // 4), F32),
        "mixed": pltpu.VMEM((own, width), BF16),
        "blocks": pltpu.VMEM((size, own, width), BF16),
        "hidden": pltpu.VMEM((NZ, 2 * own, ff), BF16),
        "parts": pltpu.VMEM((size, own, width), BF16),
        "g_send": dma(2, 4, 3),
        "g_recv": dma(2, 4, 3),
        "gx_send": dma(9),
        "gx_recv": dma(9),
    }
    names = ("sbuf", "rbuf", "xbuf", "xlast", "xgot", "r_send", "r_recv", "rx_send", "rx_recv")
    scratch.update(zip(names, scatter_scratch(half, width), strict=True))
    scratch.update(
        {
            "teacher": pltpu.VMEM((own, width), BF16),
            "gathered": pltpu.VMEM((size, own, narrow), BF16),
            "px_send": dma(8),
            "px_recv": dma(8),
            "p_send": dma(7),
            "p_recv": dma(7),
            "t_send": dma(size - 1),
            "t_recv": dma(size - 1),
            "grads": pltpu.VMEM((size, 3 * own + 16, units), BF16),
            "inbox": pltpu.VMEM((size, 3 * own + 16, units), BF16),
            "send1": dma(size - 1),
            "recv1": dma(size - 1),
            "send2": dma(size - 1),
            "recv2": dma(size - 1),
        }
    )
    elsewhere = ("tokens", "w_query", "w_key", "w_value", "w_out")
    for name in ORDER:
        if name not in elsewhere:
            scratch[name] = pltpu.VMEM(inputs[name].shape, inputs[name].dtype)
    names = [name + "_hbm" for name in inputs]
    columns, sums, squares = call(
        functools.partial(
            layer_body, (*names, *outputs, *scratch), rows * lax.axis_size("dp")
        ),
        "layer",
        1,
        tuple(inputs.values()),
        tuple(outputs.values()),
        list(scratch.values()),
        [pl.BlockSpec(memory_space=pl.ANY)] * len(inputs),
    )
    teacher_out, grad_gate, grad_up, grad_down, error = finish(columns, sums, squares)
    return (teacher_out, grad_gate, grad_up, grad_down, error.reshape(()))


def solution(mesh):
    in_specs = (
        P("dp", "tensor"),
        P(),
        P("dp"),
        P(),
        P(),
        P(None, "tensor"),
        P(None, "tensor"),
        P(None, "tensor"),
        P("tensor", None),
        P(None, "tensor"),
        P(None, "tensor"),
        P("tensor", None),
        P(),
        P("dp", None),
        P(None, "tensor"),
        P(None, "tensor"),
        P("tensor", None),
    )
    out_specs = (P("dp", "tensor"), P(None, "tensor"), P(None, "tensor"), P("tensor", None), P())
    return jax.shard_map(local, mesh=mesh, in_specs=in_specs, out_specs=out_specs, check_vma=False)
```

```python
import functools

import jax
import jax.numpy as jnp
import numpy as np
from jax import lax
from jax.experimental import pallas as pl
from jax.experimental.pallas import tpu as pltpu
from jax.sharding import PartitionSpec as P

HD = 128
NZ = 8
NY = 4
MESH = pl.DeviceIdType.MESH
VM = pl.BlockSpec(memory_space=pltpu.VMEM)
LIMIT = 56 * 1024 * 1024
F32 = jnp.float32
BF16 = jnp.bfloat16


def params(collective_id):
    return pltpu.CompilerParams(
        collective_id=collective_id, has_side_effects=True, vmem_limit_bytes=LIMIT
    )


def remote(src, dst, send_sem, recv_sem, device):
    return pltpu.make_async_remote_copy(
        src_ref=src,
        dst_ref=dst,
        send_sem=send_sem,
        recv_sem=recv_sem,
        device_id=device,
        device_id_type=MESH,
    )


def greet(devices, meanwhile=None):
    barrier = pltpu.get_barrier_semaphore()
    for device in devices:
        pl.semaphore_signal(barrier, inc=1, device_id=device, device_id_type=MESH)
    if meanwhile is not None:
        meanwhile()
    pl.semaphore_wait(barrier, len(devices))


def places():
    dp, tensor = lax.axis_index("dp"), lax.axis_index("tensor")
    x_hi, z = tensor // NZ, lax.rem(tensor, NZ)
    return dp, tensor, x_hi, z


def turn(z, by, size):
    return lax.rem(z + by + size, size)


def dma(*shape):
    return pltpu.SemaphoreType.DMA(shape)


def call(body, name, collective_id, inputs, outputs, scratch, specs=None):
    return pl.pallas_call(
        body,
        out_shape=tuple(jax.ShapeDtypeStruct(shape, kind) for shape, kind in outputs),
        in_specs=specs or [VM] * len(inputs),
        out_specs=tuple([VM] * len(outputs)),
        scratch_shapes=scratch,
        compiler_params=params(collective_id),
        name=name,
    )(*inputs)


class Sent:
    def __init__(self):
        self.copies = []

    def start(self, copy):
        copy.start()
        self.copies.append(copy)

    def finish(self):
        for copy in self.copies:
            copy.wait_send()


def on_ring(way, far, sub):
    return far < 4 or (way == 1) == (sub == 1)


def towards(way, by):
    return by if way == 0 else -by


def mix_gather(ref, at, half, sems, hook=lambda step: None, ready=None, tail=None):
    ring_send, ring_recv, x_send, x_recv = sems
    dp, tensor, x_hi, z = places()
    partner = (dp, (1 - x_hi) * NZ + z)
    nexts = tuple((dp, x_hi * NZ + turn(z, by, NZ)) for by in (1, -1))
    sent = Sent()

    def view(zz, sub):
        plane = x_hi if sub < 2 else 1 - x_hi
        return ref.at[at(zz, plane), pl.ds((sub % 2) * half, half)]

    def ring(way, far, sub, hops):
        block = view(turn(z, -towards(way, hops), NZ), sub)
        sems = ring_send.at[way, far - 1, sub], ring_recv.at[way, far - 1, sub]
        return remote(block, block, *sems, nexts[way])

    def cross(zz, sub, slot):
        block = view(zz, sub)
        return remote(block, block, x_send.at[slot], x_recv.at[slot], partner)

    def slot(way, far):
        return 1 + far + 3 * way if way == 0 else 4 + far

    def crossed(far):
        if far == 0:
            cross(z, 3, 1).wait_recv()
        for way in range(2):
            if 0 < far < 4 + way:
                cross(turn(z, -towards(way, far), NZ), 3, slot(way, far)).wait_recv()

    sent.start(cross(z, 0, 0))
    for sub in range(2):
        for way in range(2):
            sent.start(ring(way, 1, sub, 0))
    sent.start(cross(z, 1, 1))
    hook(0)
    cross(z, 2, 0).wait_recv()
    for way in range(2):
        sent.start(ring(way, 1, 2, 0))
    for far in range(2, 5):
        hook(far - 1)
        for sub in range(3):
            for way in range(2):
                ring(way, far - 1, sub, far - 1).wait_recv()
                if on_ring(way, far, sub):
                    sent.start(ring(way, far, sub, far - 1))
                if sub == 1:
                    origin = turn(z, -towards(way, far - 1), NZ)
                    sent.start(cross(origin, 1, slot(way, far - 1)))
        if far == 3:
            crossed(0)
            crossed(1)
            if ready:
                ready((0, 1))
        if far == 4:
            crossed(2)
            if ready:
                ready((2,))
    ring(1, 4, 1, 4).wait_recv()
    sent.start(cross(turn(z, 4, NZ), 1, slot(1, 4)))
    crossed(3)
    if tail:
        tail()
    for sub in (0, 2):
        ring(0, 4, sub, 4).wait_recv()
    crossed(4)
    sent.finish()


def scatter_scratch(half, width):
    return [
        pltpu.VMEM((2, 4, 3, half, width), BF16),
        pltpu.VMEM((2, 4, 3, half, width), BF16),
        pltpu.VMEM((8, half, width), BF16),
        pltpu.VMEM((half, width), BF16),
        pltpu.VMEM((half, width), BF16),
        dma(2, 4, 3),
        dma(2, 4, 3),
        dma(9),
        dma(9),
    ]


def mix_scatter(part, make, scratch):
    sbuf, rbuf, xbuf, xlast, xgot, ring_send, ring_recv, x_send, x_recv = scratch
    half = sbuf.shape[3]
    dp, tensor, x_hi, z = places()
    partner = (dp, (1 - x_hi) * NZ + z)
    nexts = tuple((dp, x_hi * NZ + turn(z, by, NZ)) for by in (1, -1))
    sent = Sent()

    def view(zz, sub):
        plane = x_hi if sub < 2 else 1 - x_hi
        return part.at[zz * 2 + plane, pl.ds((sub % 2) * half, half)]

    def slot(way, far):
        return 7 if far == 4 else 1 + 3 * way + far - 1

    def cross(zz, at):
        return remote(view(zz, 3), xbuf.at[at], x_send.at[at], x_recv.at[at], partner)

    def ring(way, far, sub, source):
        sems = ring_send.at[way, far - 1, sub], ring_recv.at[way, far - 1, sub]
        return remote(source, rbuf.at[way, far - 1, sub], *sems, nexts[way])

    def arrived(way, far, sub):
        ring(way, far, sub, rbuf.at[way, far - 1, sub]).wait_recv()
        return rbuf[way, far - 1, sub].astype(F32)

    def crossed(at):
        cross(z, at).wait_recv()
        return xbuf[at].astype(F32)

    def send(way, far, sub):
        source = view(turn(z, towards(way, far), NZ), sub)
        extra = []
        if far < 4 and on_ring(way, far + 1, sub):
            extra.append(arrived(way, far + 1, sub))
        if sub == 1:
            extra.append(crossed(slot(way, far)))
        if extra:
            total = source[...].astype(F32)
            for one in extra:
                total = total + one
            sbuf[way, far - 1, sub] = total.astype(BF16)
            source = sbuf.at[way, far - 1, sub]
        sent.start(ring(way, far, sub, source))

    def make_pair(far):
        pair = [turn(z, by, NZ) for by in (far, -far)]
        make(pair)
        for way in range(2):
            sent.start(cross(pair[way], slot(way, far)))

    def begin():
        make_pair(3)
        for sub in (0, 2):
            send(1, 3, sub)

    def rest():
        far4 = turn(z, 4, NZ)
        make([far4])
        sent.start(cross(far4, 7))
        for sub in (0, 2):
            send(0, 4, sub)
        make_pair(2)
        send(1, 4, 1)
        for sub in (1, 2, 0):
            send(0, 3, sub)
        send(1, 3, 1)
        make_pair(1)
        for sub in (2, 0, 1):
            for way in range(2):
                send(way, 2, sub)
        make([z])
        sent.start(cross(z, 0))
        for sub in (2, 0, 1):
            for way in range(2):
                send(way, 1, sub)
        return last_sums()

    def total(sub):
        return view(z, sub)[...].astype(F32) + arrived(0, 1, sub) + arrived(1, 1, sub)

    def last_sums():
        xlast[...] = total(2).astype(BF16)
        last = remote(xlast, xgot, x_send.at[8], x_recv.at[8], partner)
        sent.start(last)
        second = total(1) + crossed(0)
        first = total(0)

        def other():
            last.wait_recv()
            return first + xgot[...].astype(F32)

        return other, second, sent

    return begin, rest


def rms(values):
    return values * lax.rsqrt(jnp.mean(values * values, axis=-1, keepdims=True) + 1e-05)


def student(r, step):
    own = r.student.shape[0] // (2 * NZ)
    at = pl.ds(step * 128, 128)
    values = rms(r.student[at, :].astype(F32))
    r.normed_t[:, at] = values.T.astype(BF16)
    values = values.astype(BF16)
    gate = jnp.dot(values, r.s_gate[...], preferred_element_type=F32)
    up = jnp.dot(values, r.s_up[...], preferred_element_type=F32)
    sigmoid = jax.nn.sigmoid(gate)
    r.by_gate[at, :] = up * sigmoid * (1.0 + gate * (1.0 - sigmoid))
    r.by_up[at, :] = gate * sigmoid
    hidden = gate * sigmoid * up
    r.hidden_t[:, at] = hidden.T.astype(BF16)
    out = jnp.dot(hidden.astype(BF16), r.s_down[...], preferred_element_type=F32)
    for index in range(128 // own):
        block = out[index * own : (index + 1) * own].astype(BF16)
        r.part[index % 2, step * (64 // own) + index // 2] = block


def project(r, before, after, weights_there):
    dp, tensor, x_hi, z = places()
    rows = r.tok.shape[1]
    own = rows // (2 * NZ)

    def hook(step):
        if step == 0:
            weights_there()
            student(r, 3)

    tile = 256
    started = []

    def add(distances):
        places_now = []
        for by in distances:
            for zz in [z] if by == 0 else [turn(z, 4, NZ)] if by == 4 else [turn(z, by, NZ), turn(z, -by, NZ)]:
                places_now += [zz, NZ + zz]
        weights = jnp.concatenate(
            [r.weights[pl.ds(pl.multiple_of(at * HD, HD), HD), :] for at in places_now], axis=0
        )
        for step in range(rows // tile):
            at = pl.ds(step * tile, tile)
            square = None if not started else r.square[at, :]
            values = []
            for index in places_now:
                value = r.tok[index, at, :].astype(F32)
                square = value * value if square is None else square + value * value
                values.append((value * r.norm_gain[pl.ds(index, 1), :]).astype(BF16))
            r.square[at, :] = square
            out = jnp.dot(jnp.concatenate(values, axis=1), weights, preferred_element_type=F32)
            r.product[at, :] = out if not started else r.product[at, :] + out
        started.append(True)

    def tail():
        before()
        add((3,))

    mix_gather(
        r.tok,
        lambda zz, plane: plane * NZ + zz,
        rows // 2,
        (r.q_send, r.q_recv, r.qx_send, r.qx_recv),
        hook,
        ready=add,
        tail=tail,
    )
    after()
    add((4,))
    for step in range(rows // tile):
        at = pl.ds(step * tile, tile)
        mean = jnp.sum(r.square[at, :], axis=1, keepdims=True) / (2 * NZ * HD)
        out = r.product[at, :] * lax.rsqrt(mean + 1e-05)
        cosine, sine = r.cosine[at, :], r.sine[at, :]

        def rotary(values):
            return (values * cosine + pltpu.roll(values, HD // 2, 1) * sine).astype(BF16)

        r.pairs[dp, 0, at, :] = rotary(out[:, HD : 2 * HD])
        r.pairs[dp, 1, at, :] = out[:, 2 * HD :].astype(BF16)
        r.query[at, :] = rotary(out[:, :HD])


def keep_tokens(r):
    _, _, x_hi, z = places()
    own = r.my_tokens.shape[0]
    my_rows = pl.multiple_of((z * 2 + x_hi) * own, own)
    for index in range(2 * NZ):
        r.my_tokens[:, index * HD : (index + 1) * HD] = r.tok[index, pl.ds(my_rows, own)]


def find_starts(r):
    dp = lax.axis_index("dp")
    rows = r.start.shape[0]
    position = (dp * rows + lax.broadcasted_iota(jnp.int32, r.start.shape, 0)).astype(F32)
    found = jnp.zeros(r.start.shape, F32)
    for number in range(1, 8):
        before = jnp.where(r.series[...] < number, 1.0, 0.0)
        begin = jnp.sum(jnp.sum(before, axis=0, keepdims=True), axis=1, keepdims=True)
        found = jnp.where(begin <= position, jnp.maximum(found, begin), found)
    r.start[...] = found.astype(jnp.int32)


def prepare(r, loaded):
    loaded("series")
    find_starts(r)
    loaded("offsets", "frequency")
    for step in range(r.offsets.shape[0]):
        at = pl.ds(step * HD, HD)
        offset = jnp.broadcast_to(r.offsets[step : step + 1, :].astype(F32), (HD, HD)).T
        angle = offset * r.frequency[...]
        lane = lax.broadcasted_iota(jnp.int32, (HD, HD), 1)
        r.cosine[at, :] = jnp.cos(angle)
        sine = jnp.sin(angle)
        r.sine[at, :] = jnp.where(lane < HD // 2, -sine, sine)
    loaded("student", "s_gate", "s_up", "s_down")
    for step in range(3):
        student(r, step)


R1, R2, R3, X0, X1, H1, H2, H3, OWN = range(9)


class Refs:
    def __init__(self, names, refs):
        for name, ref in zip(names, refs, strict=True):
            setattr(self, name, ref)


def attend(r, mine, j, diagonal, tile=256):
    rows, span = r.query.shape[0], r.pairs.shape[2]
    factor = HD ** (-0.5) * 1.4426950408889634
    key, value = r.pairs[j, 0], r.pairs[j, 1]
    for index in range(rows // tile):
        at = slice(index * tile, (index + 1) * tile)
        scores = lax.dot_general(
            r.query[at, :], key, (((1,), (1,)), ((), ())), preferred_element_type=F32
        )
        column = lax.broadcasted_iota(jnp.int32, (tile, span), 1)
        allowed = column >= r.start[at, :1] - j * span
        if diagonal:
            row = index * tile + lax.broadcasted_iota(jnp.int32, (tile, span), 0)
            allowed = allowed & (column <= row)
        scores = jnp.where(allowed, scores, -1e30)
        top = jnp.max(scores, axis=1, keepdims=True)
        if not diagonal:
            old = r.peak[at, :1]
            top = jnp.maximum(old, top)
        weights = jnp.exp2((scores - top) * factor)
        denom = jnp.sum(weights, axis=1, keepdims=True)
        accum = jnp.dot(weights.astype(BF16), value, preferred_element_type=F32)
        if not diagonal:
            scale = jnp.exp2((old - top) * factor)
            denom = denom + r.denom[at, :1] * scale
            accum = accum + r.accum[at, :] * scale
        r.peak[at, :] = jnp.broadcast_to(top, (tile, HD))
        r.denom[at, :] = jnp.broadcast_to(denom, (tile, HD))
        r.accum[at, :] = accum


def exchange(r, sent):
    dp, tensor, x_hi, z = places()
    x_lo, y, core = dp // (2 * NY), lax.rem(dp // 2, NY), lax.rem(dp, 2)

    def index(xx, yy, cc):
        return xx * 2 * NY + yy * 2 + cc

    k_partner = (index(1 - x_lo, y, core), tensor)
    sibling = (index(x_lo, y, 1 - core), tensor)
    up, down = ((index(x_lo, turn(y, by, NY), core), tensor) for by in (1, -1))
    z_peers = [(dp, x_hi * NZ + turn(z, by, NZ)) for by in range(1, NZ)]
    z_nexts = (z_peers[0], z_peers[-1])
    s_partner = (dp, (1 - x_hi) * NZ + z)
    deep = r.wide.shape[1] // 4
    first, second = x_lo == 0, x_lo == 1
    half = r.pairs.shape[2] // 2

    def chip(by):
        return turn(y, by, NY)

    arrives = {
        R1: (y >= 1, x_lo, chip(-1)),
        R2: (y >= 2, x_lo, chip(-2)),
        R3: (y == 3, x_lo, chip(1)),
        X0: (second, 0, y),
        X1: (second & (y >= 1), 0, chip(-1)),
        H1: (second & (y <= 2), 0, chip(1)),
        H2: (second & (y <= 1), 0, chip(2)),
        H3: (second & (y == 0), 0, chip(-1)),
        OWN: (None, x_lo, y),
    }

    def k_copy(event, part, xx, yy, device):
        top = (part % 2) * half
        block = r.pairs.at[index(xx, yy, core), part // 2, pl.ds(top, half)]
        return remote(block, block, r.k_send.at[event, part], r.k_recv.at[event, part], device)

    later = []

    def when(condition, copy):
        @pl.when(condition)
        def _():
            copy.start()

        later.append((condition, copy))

    def k_wait(event, part):
        condition, xx, yy = arrives[event]

        @pl.when(condition)
        def _():
            k_copy(event, part, xx, yy, up).wait_recv()

    def c_copy(event, cc):
        _, xx, yy = arrives[event]
        block = r.pairs.at[index(xx, yy, cc)]
        return remote(block, block, r.c_send.at[event], r.c_recv.at[event], sibling)

    def share(event):
        condition = arrives[event][0]
        if condition is None:
            sent.start(c_copy(event, core))
        else:
            when(condition, c_copy(event, core))

    def shared(*events):
        for event in events:
            condition = arrives[event][0]
            if condition is None:
                c_copy(event, 1 - core).wait_recv()
            else:

                @pl.when(condition)
                def _(event=event):
                    c_copy(event, 1 - core).wait_recv()

    def work(*events):
        found = []
        for event in events:
            condition, xx, yy = arrives[event]
            for cc in (core, 1 - core):
                if event == OWN and cc is core:
                    continue
                j = index(xx, yy, cc)
                needed = (j < dp) & (j >= dp - 10)
                found.append((j, needed if condition is None else needed & condition))

        @pl.loop(0, len(found))
        def _(step):
            j, needed = found[0]
            needed = needed.astype(jnp.int32)
            for number, (jj, wanted) in enumerate(found[1:], 1):
                j = jnp.where(step == number, jj, j)
                needed = jnp.where(step == number, wanted.astype(jnp.int32), needed)

            @pl.when(needed == 1)
            def _():
                attend(r, dp, j, False)

    def w_copy(way, far, sub, hops):
        top = pl.multiple_of(core * 2 * deep + sub * deep, deep)
        block = r.wide.at[turn(z, -towards(way, hops), NZ), pl.ds(top, deep)]
        sems = r.w_send.at[way, far - 1, sub], r.w_recv.at[way, far - 1, sub]
        return remote(block, block, *sems, z_nexts[way])

    def w_share(by, slot, cc):
        top = pl.multiple_of(cc * 2 * deep, 2 * deep)
        block = r.wide.at[turn(z, by, NZ), pl.ds(top, 2 * deep)]
        return remote(block, block, r.wc_send.at[slot], r.wc_recv.at[slot], sibling)

    def w_forward(far, sub):
        for way in range(2):
            if far < 4 or sub == way:
                w_copy(way, far, sub, far).wait_recv()
            if far < 3 or (far == 3 and sub == way):
                sent.start(w_copy(way, far + 1, sub, far))

    def w_spread(far):
        for way in range(2):
            sent.start(w_share(towards(way, -far), 2 * (far - 1) + way, core))

    s_cross = remote(r.part.at[1 - x_hi], r.s_got, r.sx_send, r.sx_recv, s_partner)

    def begin_student():
        sent.start(s_cross)

    def begin_wide():
        for sub in range(2):
            for way in range(2):
                sent.start(w_copy(way, 1, sub, 0))

    def arrive():
        for part in range(4):
            when(y <= 2, k_copy(R1, part, x_lo, y, up))
            when(y == 0, k_copy(R3, part, x_lo, y, down))
            when(first, k_copy(X0, part, 0, y, k_partner))
        share(OWN)
        w_forward(1, 0)
        w_forward(1, 1)
        w_spread(1)
        attend(r, dp, dp, True)
        for part in range(4):
            k_wait(R1, part)
            when((y >= 1) & (y <= 2), k_copy(R2, part, x_lo, chip(-1), up))
            when(first & (y >= 1), k_copy(X1, part, 0, chip(-1), k_partner))
            k_wait(X0, part)
            when(second & (y >= 1), k_copy(H1, part, 0, y, down))
            when(second & (y == 3), k_copy(H3, part, 0, y, up))
            if part % 2:
                w_forward(2, part // 2)
        share(R1)
        share(X0)
        w_spread(2)
        for part in range(4):
            k_wait(R3, part)
        share(R3)
        s_cross.wait_recv()
        r.s_out[...] = (r.part[x_hi].astype(F32) + r.s_got[...].astype(F32)).astype(BF16)
        shared(OWN, R1)
        work(OWN, R1)
        for part in range(4):
            k_wait(H1, part)
            when(second & (y >= 1) & (y <= 2), k_copy(H2, part, 0, chip(1), down))
        share(H1)
        w_forward(3, 0)
        shared(X0)
        work(X0)
        w_forward(3, 1)
        w_spread(3)
        for event in (X1, R2, H3):
            for part in range(4):
                k_wait(event, part)
            share(event)
        shared(R3, H1)
        work(R3, H1)
        w_forward(4, 0)
        w_forward(4, 1)
        sent.start(w_share(4, 6, core))
        for part in range(4):
            k_wait(H2, part)
        share(H2)
        shared(X1, R2, H3)
        work(X1, R2, H3)
        shared(H2)
        work(H2)
        r.attended[...] = (r.accum[...] / r.denom[...]).astype(BF16)

    def finish():
        for condition, copy in later:

            @pl.when(condition)
            def _(copy=copy):
                copy.wait_send()

    def wide_whole():
        for slot, by in enumerate([-1, 1, -2, 2, -3, 3, 4]):
            w_share(by, slot, 1 - core).wait_recv()

    return begin_student, begin_wide, arrive, wide_whole, finish


ORDER = (
    "tokens",
    "series",
    "offsets",
    "frequency",
    "student",
    "s_gate",
    "s_up",
    "s_down",
    "w_query",
    "w_key",
    "w_value",
    "norm_gain",
    "w_out",
    "mlp_gain",
    "w_gate",
    "w_up",
    "w_down",
    "projector",
)


def layer_body(names, total_rows, *refs):
    r = Refs(names, refs)
    dp, tensor, x_hi, z = places()
    size = 2 * NZ
    rows, width = r.tok.shape[1], r.w_gate.shape[0]
    own = rows // size
    pair = 2 * own
    row = z * 2 + x_hi
    my_rows = pl.ds(pl.multiple_of(row * own, own), own)
    partner = (dp, (1 - x_hi) * NZ + z)
    z_peers = [(dp, x_hi * NZ + turn(z, by, NZ)) for by in range(1, NZ)]
    t_peers = [turn(tensor, by, size) for by in range(1, size)]
    d_peers = [turn(dp, by, size) for by in range(1, size)]
    loads = {}
    near = {
        "tokens": r.tok.at[tensor],
        "w_query": r.weights.at[:, pl.ds(0, HD)],
        "w_key": r.weights.at[:, pl.ds(HD, HD)],
        "w_value": r.weights.at[:, pl.ds(2 * HD, HD)],
        "w_out": r.wide.at[z],
    }
    for index, name in enumerate(ORDER):
        target = near[name] if name in near else getattr(r, name)
        loads[name] = pltpu.make_async_copy(
            getattr(r, name + "_hbm"), target, r.load_sem.at[index]
        )
        loads[name].start()

    def loaded(*names):
        for name in names:
            loads.pop(name).wait()

    greet(
        [(dp, peer) for peer in t_peers] + [(peer, tensor) for peer in d_peers],
        lambda: prepare(r, loaded),
    )
    sent = Sent()
    begin_student, begin_wide, arrive, wide_whole, finish_exchange = exchange(r, sent)
    loaded("tokens")

    def after():
        loaded("w_out")
        begin_wide()

    project(r, begin_student, after, lambda: loaded("w_query", "w_key", "w_value", "norm_gain"))
    arrive()

    def rows_of(zz):
        return pl.ds(pl.multiple_of(zz * pair, pair), pair)

    for by in range(1, NZ):
        sent.start(
            remote(
                r.attended.at[rows_of(turn(z, by, NZ))],
                r.heads.at[z],
                r.a_send.at[by - 1],
                r.a_recv.at[by - 1],
                z_peers[by - 1],
            )
        )
    def send_student():
        for by in range(1, NZ):
            sent.start(
                remote(
                    r.s_out.at[turn(z, by, NZ)],
                    r.s_in.at[by - 1],
                    r.sz_send.at[by - 1],
                    r.sz_recv.at[by - 1],
                    z_peers[by - 1],
                )
            )

    r.heads[z] = r.attended[rows_of(z), :]
    wide_whole()
    for by in range(1, NZ):
        block = r.heads.at[turn(z, -by, NZ)]
        remote(block, block, r.a_send.at[by - 1], r.a_recv.at[by - 1], z_peers[by - 1]).wait_recv()
    chunk = width // 4
    joined = jnp.concatenate([r.heads[index] for index in range(NZ)], axis=1)
    depth = joined.shape[1]

    def half_rows(plane):
        return pl.ds(pl.multiple_of(plane * own, own), own)

    def swap(step):
        sems = r.o_send.at[step], r.o_recv.at[step]
        return remote(r.out_send.at[step], r.out_recv.at[step], *sems, partner)

    for step in range(width // chunk):
        at = slice(step * chunk, (step + 1) * chunk)
        r.partial[step] = jnp.dot(
            joined, r.wide[:, :, at].reshape(depth, chunk), preferred_element_type=F32
        )
        r.out_send[step] = r.partial[step, half_rows(1 - x_hi), :].astype(BF16)
        sent.start(swap(step))
        if step == 0:
            send_student()
    keep_tokens(r)
    for step in range(width // chunk):
        at = slice(step * chunk, (step + 1) * chunk)
        mine = r.partial[step, half_rows(x_hi), :] + r.my_tokens[:, at].astype(F32)
        swap(step).wait_recv()
        r.mixed[:, at] = (mine + r.out_recv[step].astype(F32)).astype(BF16)
    mixed = r.mixed[...]
    loaded("mlp_gain")
    r.blocks[row] = (rms(mixed.astype(F32)) * r.mlp_gain[...]).astype(BF16)

    waited = []

    def units(zs):
        if not waited:
            loaded("w_gate", "w_up")
            waited.append(True)
        value = jnp.concatenate(
            [r.blocks[pl.ds(zz * 2, 2)].reshape(pair, width) for zz in zs], axis=0
        )
        gate = jnp.dot(value, r.w_gate[...], preferred_element_type=F32)
        up = jnp.dot(value, r.w_up[...], preferred_element_type=F32)
        found = (gate * jax.nn.sigmoid(gate) * up).astype(BF16)
        for at, zz in enumerate(zs):
            r.hidden[zz] = found[at * pair : (at + 1) * pair]

    def predict():
        student_sum = r.s_out[z].astype(F32)
        for by in range(1, NZ):
            got = r.s_in.at[by - 1]
            sems = r.sz_send.at[by - 1], r.sz_recv.at[by - 1]
            remote(got, got, *sems, z_peers[by - 1]).wait_recv()
            student_sum = student_sum + r.s_in[by - 1].astype(F32)
        r.predicted[...] = r.student[my_rows, :].astype(F32) + student_sum

    def ready(distances):
        zs = []
        for by in distances:
            zs += [z] if by == 0 else [turn(z, by, NZ), turn(z, -by, NZ)]
        units(zs)
        if 2 in distances:
            predict()

    fresh = [3, 4]

    def make(zs):
        if fresh:
            fresh.pop()
            units(zs)
        value = jnp.concatenate([r.hidden[zz] for zz in zs], axis=0)

        @pl.loop(0, width // chunk)
        def _(step):
            at = pl.ds(pl.multiple_of(step * chunk, chunk), chunk)
            out = jnp.dot(value, r.w_down[:, at], preferred_element_type=F32).astype(BF16)
            for index, zz in enumerate(zs):
                for plane in range(2):
                    top = index * pair + plane * own
                    r.parts[zz * 2 + plane, :, at] = out[top : top + own]

    scratch = (r.sbuf, r.rbuf, r.xbuf, r.xlast, r.xgot, r.r_send, r.r_recv, r.rx_send, r.rx_recv)
    begin_sum, rest_of_sum = mix_scatter(r.parts, make, scratch)
    loaded("w_down")
    mix_gather(
        r.blocks,
        lambda zz, plane: zz * 2 + plane,
        own // 2,
        (r.g_send, r.g_recv, r.gx_send, r.gx_recv),
        ready=ready,
        tail=begin_sum,
    )
    top, bottom, more = rest_of_sum()
    loaded("projector")

    def last_rows(first, summed):
        at = slice(first, first + own // 2)
        teacher = (r.mixed[at, :].astype(F32) + summed).astype(BF16)
        r.teacher[at, :] = teacher
        target = jnp.dot(teacher, r.projector[...], preferred_element_type=F32)
        scaled = (r.predicted[at, :] - target) * total_rows ** (-0.5)
        r.gathered[row, at, :] = scaled.astype(BF16)

    last_rows(own // 2, bottom)
    last_rows(0, top())

    def place(by, plane):
        return r.gathered.at[turn(z, by, NZ) * 2 + plane]

    def across(by, plane):
        block = place(by, plane)
        at = by % NZ
        return remote(block, block, r.px_send.at[at], r.px_recv.at[at], partner)

    def along(by, device):
        block = place(-by if device is None else 0, x_hi)
        sems = r.p_send.at[by - 1], r.p_recv.at[by - 1]
        return remote(block, block, *sems, z_peers[by - 1])

    for by in (4, 3, 5, 2, 6, 1, 7):
        sent.start(along(by, True))
    sent.start(across(0, x_hi))
    for by in (1, 7, 2, 6, 3, 5, 4):
        along(by, None).wait_recv()
        sent.start(across(-by, x_hi))
    for by, peer in enumerate(t_peers):
        sent.start(
            remote(
                r.teacher.at[:, pl.ds(pl.multiple_of(peer * HD, HD), HD)],
                r.columns.at[row],
                r.t_send.at[by],
                r.t_recv.at[by],
                (dp, peer),
            )
        )
    r.columns[row] = r.teacher[:, pl.ds(pl.multiple_of(tensor * HD, HD), HD)]
    for by in (0, 1, 7, 2, 6, 3, 5, 4):
        across(-by, 1 - x_hi).wait_recv()

    scaled = r.gathered[...].reshape(rows, -1)
    grad_hidden = lax.dot_general(
        scaled, r.s_down[...], (((1,), (1,)), ((), ())), preferred_element_type=F32
    )
    both = jnp.concatenate(
        [(grad_hidden * r.by_gate[...]).astype(BF16), (grad_hidden * r.by_up[...]).astype(BF16)],
        axis=1,
    )
    both = jnp.dot(r.normed_t[...], both, preferred_element_type=F32).astype(BF16)
    down = jnp.dot(r.hidden_t[...], scaled, preferred_element_type=F32).astype(BF16)
    count = grad_hidden.shape[1]
    r.grads[:, :own] = both[:, :count].reshape(size, own, count)
    r.grads[:, own:pair] = both[:, count:].reshape(size, own, count)
    down = jnp.concatenate([down[:, at : at + HD] for at in range(0, down.shape[1], HD)], axis=0)
    r.grads[:, pair : 3 * own] = down.reshape(size, own, HD)
    squares = scaled.astype(F32)
    squares = jnp.sum((squares * squares).reshape(-1, 8, scaled.shape[1]), axis=0)
    squares = sum(squares[:, at : at + HD] for at in range(0, scaled.shape[1], HD))
    high = squares.astype(BF16)
    low = (squares - high.astype(F32)).astype(BF16)
    both = jnp.concatenate([high, low], axis=0)
    r.grads[:, 3 * own :] = jnp.broadcast_to(both[None], (size,) + both.shape)

    def origin(by):
        return turn(dp, -(by + 1), size)

    r.inbox[dp] = r.grads[dp]
    for by, peer in enumerate(d_peers):
        sems = r.send1.at[by], r.recv1.at[by]
        sent.start(remote(r.grads.at[peer], r.inbox.at[dp], *sems, (peer, tensor)))
    for by, peer in enumerate(d_peers):
        block = r.inbox.at[origin(by)]
        remote(block, block, r.send1.at[by], r.recv1.at[by], (peer, tensor)).wait_recv()
    total = r.inbox[0].astype(F32)
    for index in range(1, size):
        total = total + r.inbox[index].astype(F32)
    r.sums[dp] = total[: 3 * own].astype(BF16)
    r.error[...] = total[3 * own : 3 * own + 8] + total[3 * own + 8 :]
    for by, peer in enumerate(d_peers):
        block = r.sums.at[dp]
        sent.start(remote(block, block, r.send2.at[by], r.recv2.at[by], (peer, tensor)))
    for by, peer in enumerate(t_peers):
        source = turn(tensor, -(by + 1), size)
        block = r.columns.at[lax.rem(source, NZ) * 2 + source // NZ]
        remote(block, block, r.t_send.at[by], r.t_recv.at[by], (dp, peer)).wait_recv()
    for by, peer in enumerate(d_peers):
        block = r.sums.at[origin(by)]
        remote(block, block, r.send2.at[by], r.recv2.at[by], (peer, tensor)).wait_recv()
    finish_exchange()
    sent.finish()
    more.finish()


def finish_body(columns_ref, sums_ref, squares_ref, teacher_ref, gate_ref, up_ref, down_ref, error_ref):
    rows, width = teacher_ref.shape
    own = rows // (2 * NZ)
    teacher_ref[...] = columns_ref[...].reshape(rows, width)
    sums = sums_ref[...].astype(F32)
    gate_ref[...] = sums[:, :own].reshape(-1, width)
    up_ref[...] = sums[:, own : 2 * own].reshape(-1, width)
    down = sums[:, 2 * own :].reshape(-1, width)
    for index in range(down.shape[0] // width):
        lanes = slice(index * width, (index + 1) * width)
        down_ref[:, lanes] = down[lanes]
    total = jnp.sum(jnp.sum(squares_ref[...], axis=0, keepdims=True), axis=1, keepdims=True)
    error_ref[...] = total / down_ref.shape[1]


def finish(columns, sums, squares):
    own, units = columns.shape[1:]
    rows = 2 * NZ * own
    shapes = (
        ((rows, units), BF16),
        ((rows, units), F32),
        ((rows, units), F32),
        ((units, rows), F32),
        ((1, 1), F32),
    )
    return pl.pallas_call(
        finish_body,
        out_shape=tuple(jax.ShapeDtypeStruct(shape, kind) for shape, kind in shapes),
        in_specs=[VM] * 3,
        out_specs=(VM,) * 5,
        compiler_params=pltpu.CompilerParams(vmem_limit_bytes=LIMIT),
        name="finish",
    )(columns, sums, squares)


def frequencies(head_dim):
    indices = np.arange(head_dim // 2)
    found = np.exp(-np.log(500000.0) * 2.0 * indices / head_dim).astype(np.float32)
    return np.concatenate([found, found])[None]


def local(
    tokens,
    series_ids,
    offsets,
    norm_gain,
    mlp_gain,
    w_query,
    w_key,
    w_value,
    w_out,
    w_gate,
    w_up,
    w_down,
    projector,
    student_in,
    s_gate,
    s_up,
    s_down,
):
    rows = tokens.shape[0]
    size = 2 * NZ
    own = rows // size
    width = projector.shape[0]
    narrow = student_in.shape[1]
    units = s_gate.shape[1]
    ff = w_gate.shape[1]
    frequency = jnp.asarray(frequencies(HD))
    inputs = {
        "tokens": tokens,
        "series": series_ids.reshape(-1, HD),
        "norm_gain": norm_gain.reshape(-1, HD),
        "offsets": offsets.reshape(-1, HD),
        "frequency": frequency,
        "w_query": w_query,
        "w_key": w_key,
        "w_value": w_value,
        "w_out": w_out,
        "mlp_gain": mlp_gain[None],
        "w_gate": w_gate,
        "w_up": w_up,
        "w_down": w_down,
        "projector": projector,
        "student": student_in,
        "s_gate": s_gate,
        "s_up": s_up,
        "s_down": s_down,
    }
    outputs = {
        "columns": ((size, own, HD), BF16),
        "sums": ((size, 3 * own, units), BF16),
        "error": ((8, HD), F32),
    }
    one = pltpu.SemaphoreType.DMA
    half = own // 2
    scratch = {
        "tok": pltpu.VMEM((size, rows, HD), BF16),
        "cosine": pltpu.VMEM((rows, HD), F32),
        "sine": pltpu.VMEM((rows, HD), F32),
        "square": pltpu.VMEM((rows, HD), F32),
        "product": pltpu.VMEM((rows, 3 * HD), F32),
        "predicted": pltpu.VMEM((own, narrow), F32),
        "weights": pltpu.VMEM((width, 3 * HD), BF16),
        "query": pltpu.VMEM((rows, HD), BF16),
        "my_tokens": pltpu.VMEM((own, width), BF16),
        "part": pltpu.VMEM((2, NZ, own, narrow), BF16),
        "normed_t": pltpu.VMEM((narrow, rows), BF16),
        "hidden_t": pltpu.VMEM((units, rows), BF16),
        "by_gate": pltpu.VMEM((rows, units), F32),
        "by_up": pltpu.VMEM((rows, units), F32),
        "q_send": dma(2, 4, 3),
        "q_recv": dma(2, 4, 3),
        "qx_send": dma(9),
        "qx_recv": dma(9),
        "pairs": pltpu.VMEM((4 * NY, 2, rows, HD), BF16),
        "wide": pltpu.VMEM((NZ,) + w_out.shape, BF16),
        "start": pltpu.VMEM((rows, HD), jnp.int32),
        "peak": pltpu.VMEM((rows, HD), F32),
        "denom": pltpu.VMEM((rows, HD), F32),
        "accum": pltpu.VMEM((rows, HD), F32),
        "attended": pltpu.VMEM((rows, HD), BF16),
        "k_send": dma(9, 4),
        "k_recv": dma(9, 4),
        "c_send": dma(9),
        "c_recv": dma(9),
        "w_send": dma(2, 4, 2),
        "w_recv": dma(2, 4, 2),
        "wc_send": dma(7),
        "wc_recv": dma(7),
        "s_got": pltpu.VMEM((NZ, own, narrow), BF16),
        "s_out": pltpu.VMEM((NZ, own, narrow), BF16),
        "s_in": pltpu.VMEM((NZ - 1, own, narrow), BF16),
        "sx_send": one,
        "sx_recv": one,
        "sz_send": dma(7),
        "sz_recv": dma(7),
        "load_sem": dma(len(ORDER)),
        "heads": pltpu.VMEM((NZ, 2 * own, HD), BF16),
        "a_send": dma(7),
        "a_recv": dma(7),
        "out_send": pltpu.VMEM((4, own, width // 4), BF16),
        "out_recv": pltpu.VMEM((4, own, width // 4), BF16),
        "o_send": dma(4),
        "o_recv": dma(4),
        "partial": pltpu.VMEM((4, 2 * own, width // 4), F32),
        "mixed": pltpu.VMEM((own, width), BF16),
        "blocks": pltpu.VMEM((size, own, width), BF16),
        "hidden": pltpu.VMEM((NZ, 2 * own, ff), BF16),
        "parts": pltpu.VMEM((size, own, width), BF16),
        "g_send": dma(2, 4, 3),
        "g_recv": dma(2, 4, 3),
        "gx_send": dma(9),
        "gx_recv": dma(9),
    }
    names = ("sbuf", "rbuf", "xbuf", "xlast", "xgot", "r_send", "r_recv", "rx_send", "rx_recv")
    scratch.update(zip(names, scatter_scratch(half, width), strict=True))
    scratch.update(
        {
            "teacher": pltpu.VMEM((own, width), BF16),
            "gathered": pltpu.VMEM((size, own, narrow), BF16),
            "px_send": dma(8),
            "px_recv": dma(8),
            "p_send": dma(7),
            "p_recv": dma(7),
            "t_send": dma(size - 1),
            "t_recv": dma(size - 1),
            "grads": pltpu.VMEM((size, 3 * own + 16, units), BF16),
            "inbox": pltpu.VMEM((size, 3 * own + 16, units), BF16),
            "send1": dma(size - 1),
            "recv1": dma(size - 1),
            "send2": dma(size - 1),
            "recv2": dma(size - 1),
        }
    )
    elsewhere = ("tokens", "w_query", "w_key", "w_value", "w_out")
    for name in ORDER:
        if name not in elsewhere:
            scratch[name] = pltpu.VMEM(inputs[name].shape, inputs[name].dtype)
    names = [name + "_hbm" for name in inputs]
    columns, sums, squares = call(
        functools.partial(
            layer_body, (*names, *outputs, *scratch), rows * lax.axis_size("dp")
        ),
        "layer",
        1,
        tuple(inputs.values()),
        tuple(outputs.values()),
        list(scratch.values()),
        [pl.BlockSpec(memory_space=pl.ANY)] * len(inputs),
    )
    teacher_out, grad_gate, grad_up, grad_down, error = finish(columns, sums, squares)
    return (teacher_out, grad_gate, grad_up, grad_down, error.reshape(()))


def solution(mesh):
    in_specs = (
        P("dp", "tensor"),
        P(),
        P("dp"),
        P(),
        P(),
        P(None, "tensor"),
        P(None, "tensor"),
        P(None, "tensor"),
        P("tensor", None),
        P(None, "tensor"),
        P(None, "tensor"),
        P("tensor", None),
        P(),
        P("dp", None),
        P(None, "tensor"),
        P(None, "tensor"),
        P("tensor", None),
    )
    out_specs = (P("dp", "tensor"), P(None, "tensor"), P(None, "tensor"), P("tensor", None), P())
    return jax.shard_map(local, mesh=mesh, in_specs=in_specs, out_specs=out_specs, check_vma=False)
```
